32 devices in a mesh: seq: 8 (over y, x, core), chan: 4 (over z).
Axes of the slice: x: 2, y: 2, z: 4, core: 2. Of those that a mesh axis runs over, the one named last changes fastest.
Arguments:
- tokens: bfloat16 [8192, 4096], P('seq', 'chan'), may hold values from -6 to 6
- in_weight: bfloat16 [3, 4096, 2048], P(None, None, 'chan'), may hold values from -0.09375 to 0.09375
- conv_weight: float32 [3, 3, 2048], P(None, None, 'chan'), may hold values from -3 to 3
- spectrum: float32 [2, 2048, 16, 1024], P(None, 'chan', 'seq'), may hold values from -6 to 6
- skip: float32 [2048], P('chan'), may hold values from -4 to 4
- out_weight: bfloat16 [2048, 4096], P('chan'), may hold values from -0.125 to 0.125
Outputs:
- mixed: bfloat16 [8192, 4096], P('seq', 'chan')
The draws below stay inside these ranges and needn't reach their ends.
All inputs are finite; a program needn't handle non-finite values.
Results may differ from the reference program's by a relative error of at most 0.03.
Values may be sent and summed in bfloat16 or wider, within the bound.
No kernel may reach another device: no remote copies, remote signals or barrier semaphores. Data moves between devices by JAX's collectives and lax.ppermute only.
A program may use at most 256 MiB of HBM per device.

```python
import jax
import jax.numpy as jnp
from jax import lax

D = 4096
C = 2048
TAPS = 3
TOK_DEV = 1024
TOKENS = 8192
KB = 16
NFFT = 16384
N_CHAN = 4


def levels(rng, extent, cuts, low, largest):
    level, own = 1.0, jax.random.fold_in(rng, 6)
    for dim, shards_of in cuts:
        heights = jnp.exp(jax.random.uniform(jax.random.fold_in(own, dim), (shards_of,), jnp.float32, low / len(cuts), largest / len(cuts)))
        level = level * jnp.repeat(heights, extent[dim] // shards_of).reshape([-1 if axis == dim else 1 for axis in range(len(extent))])
    return level


def gaussian(rng, dims, scale, most, cuts=(), dtype=jnp.bfloat16):
    drawn = jax.random.normal(rng, dims, jnp.float32) * scale
    if len(cuts) > 0:
        drawn = levels(rng, dims, cuts, -0.22, 0.18) * drawn
    return jnp.clip(drawn, min=-most, max=most).astype(dtype)


def setup_inputs(seed: int = 0) -> dict:
    streams_of = jax.random.split(jax.random.key(seed), 7)
    tokens = gaussian(streams_of[0], (TOKENS, D), 1.0, 6.0, ((0, 8), (1, 4)))
    in_weight = gaussian(streams_of[1], (3, D, C), D ** -0.5, 0.09375, ((2, 4),))
    conv_weight = gaussian(streams_of[2], (TAPS, 3, C), 0.6, 3.0, ((2, 4),), jnp.float32)
    spectrum = gaussian(streams_of[3], (2, C, KB, TOK_DEV), 1.0, 6.0, ((1, 4), (2, 8)), jnp.float32)
    skip = gaussian(streams_of[4], (C,), 1.0, 4.0, ((0, 4),), jnp.float32)
    out_weight = gaussian(streams_of[5], (C, D), C ** -0.5, 0.125, ((0, 4),))
    return dict(tokens=tokens, in_weight=in_weight, conv_weight=conv_weight, spectrum=spectrum, skip=skip, out_weight=out_weight)


def reference(tokens, in_weight, conv_weight, spectrum, skip, out_weight):
    projected = jnp.einsum("td,pdc->pct", tokens.astype(jnp.float32), in_weight.astype(jnp.float32)).astype(jnp.bfloat16)
    seq_length = projected.shape[2]
    margin = TAPS - 1
    padded = jnp.pad(projected.astype(jnp.float32), ((0, 0), (0, 0), (margin, 0)))
    filtered = conv_weight[0][:, :, None] * padded[:, :, margin:margin + seq_length]
    for tap_index in range(1, TAPS):
        filtered = filtered + conv_weight[tap_index][:, :, None] * padded[:, :, margin - tap_index:margin - tap_index + seq_length]
    query_rows = filtered[0]
    signal = (filtered[1] * filtered[2]).astype(jnp.bfloat16)
    response = lax.complex(spectrum[0], spectrum[1]).transpose(0, 2, 1).reshape(C, NFFT)
    width_block = min(C, 256)
    signal_blocks = signal.astype(jnp.float32).reshape(C // width_block, width_block, seq_length)
    response_blocks = response.reshape(C // width_block, width_block, NFFT)

    def convolve(paired):
        values, filter_block = paired
        extended = jnp.pad(values, ((0, 0), (0, NFFT - seq_length)))
        frequencies = jnp.fft.fft(extended, axis=1)
        return jnp.real(jnp.fft.ifft(frequencies * filter_block, axis=1))[:, :seq_length]

    longconv = lax.map(convolve, (signal_blocks, response_blocks)).reshape(C, seq_length)
    gated = (query_rows * (longconv + skip[:, None] * signal.astype(jnp.float32))).astype(jnp.bfloat16)
    group_rows = C // N_CHAN
    gated_groups = gated.reshape(N_CHAN, group_rows, seq_length)
    weight_groups = out_weight.reshape(N_CHAN, group_rows, D)

    def add_group(running, paired):
        gated_part, weight_part = paired
        partial_out = jnp.dot(gated_part.T, weight_part, preferred_element_type=jnp.float32).astype(jnp.bfloat16)
        partial_out = lax.optimization_barrier(partial_out)
        return running + partial_out.astype(jnp.float32), None

    total, unused = lax.scan(add_group, jnp.zeros((seq_length, D), jnp.float32), (gated_groups, weight_groups))
    return total.astype(jnp.bfloat16)
```

```python
import math

import jax
import jax.numpy as jnp
import numpy as np
from jax import lax
from jax.experimental import pallas as pl
from jax.experimental.pallas import tpu as pltpu
from jax.sharding import PartitionSpec as P

TAPS = 3
LANES = 128
CHAN_BLOCK = 8


def from_behind(value, axis, by):
    size = lax.axis_size(axis)
    pairs = [(i, i + by) for i in range(size) if 0 <= i + by < size]
    return lax.ppermute(value, axis, pairs)


def gather_by_doubling(value, axis):
    size = lax.axis_size(axis)
    index = lax.axis_index(axis)
    held = value[None]
    bit = 1
    while bit < size:
        other = lax.ppermute(held, axis, [(i, i ^ bit) for i in range(size)])
        upper = (index // bit) % 2 == 1
        first = jnp.where(upper, other, held)
        second = jnp.where(upper, held, other)
        held = jnp.concatenate([first, second], axis=0)
        bit *= 2
    return held


def transform_tables(seq_count, tok_rows):
    runs = tok_rows // LANES
    wide = 2 * seq_count * runs
    fft_len = wide * LANES
    k1 = np.arange(seq_count + 1)[:, None]
    k2a = np.arange(runs)[None, :]
    ka = (k1 + 2 * seq_count * k2a).reshape(-1)
    a = np.arange(seq_count * runs)
    b = np.arange(LANES)
    outer = 2.0 * np.pi * ((ka[:, None] * a[None, :]) % wide) / wide
    first = np.concatenate([np.cos(outer), -np.sin(outer)], axis=0)
    last = first.T / fft_len
    turn = 2.0 * np.pi * ((ka[:, None] * b[None, :]) % fft_len) / fft_len
    inner = 2.0 * np.pi * ((b[:, None] * b[None, :]) % LANES) / LANES
    cos, sin = np.cos(inner), np.sin(inner)
    forward = np.block([[cos, -sin], [sin, cos]])
    backward = np.block([[cos, sin], [-sin, cos]])
    half = lambda table: jnp.asarray(table, jnp.bfloat16)
    full = lambda table: jnp.asarray(table, jnp.float32)
    return half(first), half(last), full(np.cos(turn)), full(np.sin(turn)), half(forward), half(backward)


def conv_kernel(signal_ref, resp_ref, first_ref, last_ref, cos_ref, sin_ref, fwd_ref, bwd_ref, out_ref, held):
    seq_count, block, tok_rows = signal_ref.shape
    runs = tok_rows // LANES
    span = seq_count * runs
    rows = cos_ref.shape[0]
    for s in range(seq_count):
        for r in range(runs):
            piece = signal_ref[s, :, r * LANES : (r + 1) * LANES].astype(jnp.float32)
            held[pl.ds(s * runs + r, block, stride=span), :] = piece
    cos, sin = cos_ref[...], sin_ref[...]
    for c in range(block):
        x = held[c * span : (c + 1) * span, :].astype(jnp.bfloat16)
        y = jnp.dot(first_ref[...], x, preferred_element_type=jnp.float32)
        re, im = y[:rows], y[rows:]
        z = jnp.concatenate([re * cos + im * sin, im * cos - re * sin], axis=1)
        f = jnp.dot(z.astype(jnp.bfloat16), fwd_ref[...], preferred_element_type=jnp.float32)
        re, im = f[:, :LANES], f[:, LANES:]
        hr = resp_ref[0, c].astype(jnp.float32)
        hi = resp_ref[1, c].astype(jnp.float32)
        p = jnp.concatenate([re * hr - im * hi, re * hi + im * hr], axis=1)
        q = jnp.dot(p.astype(jnp.bfloat16), bwd_ref[...], preferred_element_type=jnp.float32)
        re, im = q[:, :LANES], q[:, LANES:]
        w = jnp.concatenate([re * cos - im * sin, im * cos + re * sin], axis=0)
        held[c * span : (c + 1) * span, :] = jnp.dot(
            last_ref[...], w.astype(jnp.bfloat16), preferred_element_type=jnp.float32
        )
    for s in range(seq_count):
        for r in range(runs):
            piece = held[pl.ds(s * runs + r, block, stride=span), :]
            out_ref[s, :, r * LANES : (r + 1) * LANES] = piece.astype(out_ref.dtype)


def long_conv(values, response):
    seq_count, chans, tok_rows = values.shape
    rows = response.shape[2]
    block = min(CHAN_BLOCK, chans)
    tables = transform_tables(seq_count, tok_rows)
    fixed = [pl.BlockSpec(t.shape, lambda i: (0, 0)) for t in tables]
    span = seq_count * tok_rows // LANES
    flops = chans * 2 * (2 * 2 * rows * span * LANES + 2 * rows * 4 * LANES * LANES)
    return pl.pallas_call(
        conv_kernel,
        grid=(chans // block,),
        in_specs=[
            pl.BlockSpec((seq_count, block, tok_rows), lambda i: (0, i, 0)),
            pl.BlockSpec((2, block, rows, LANES), lambda i: (0, i, 0, 0)),
            *fixed,
        ],
        out_specs=pl.BlockSpec((seq_count, block, tok_rows), lambda i: (0, i, 0)),
        out_shape=jax.ShapeDtypeStruct((seq_count, chans, tok_rows), jnp.bfloat16),
        scratch_shapes=[pltpu.VMEM((block * span, LANES), jnp.float32)],
        compiler_params=pltpu.CompilerParams(vmem_limit_bytes=48 * 1024 * 1024),
        cost_estimate=pl.CostEstimate(flops=flops, bytes_accessed=8 * 2**20, transcendentals=0),
    )(values, response, *tables)


def folded_response(spectrum, seq_count):
    parts, chans, own, tok_rows = spectrum.shape
    runs = tok_rows // LANES
    each = chans // seq_count
    sent = spectrum.astype(jnp.bfloat16).reshape(parts, seq_count, each, own, LANES, runs)
    sent = sent.transpose(1, 0, 2, 3, 5, 4)
    got = lax.all_to_all(sent, "seq", split_axis=0, concat_axis=0, tiled=True)
    got = got.transpose(1, 2, 0, 3, 4, 5).reshape(parts, each, own * seq_count, runs, LANES)
    kept = got[:, :, : seq_count + 1].astype(jnp.float32)
    mirror = got[:, :, seq_count + 1 :][:, :, ::-1, ::-1, ::-1].astype(jnp.float32)
    mirror = jnp.stack([mirror[0], -mirror[1]])
    mirror = jnp.pad(mirror, ((0, 0), (0, 0), (1, 1), (0, 0), (0, 0)))
    return (kept + mirror).astype(jnp.bfloat16).reshape(parts, each, (seq_count + 1) * runs, LANES)


def feature_slice(out_weight, seq_count):
    group = out_weight.shape[0]
    each = group // seq_count
    own = lax.dynamic_slice_in_dim(out_weight, lax.axis_index("seq") * each, each, axis=0)
    own = lax.all_to_all(own, "chan", split_axis=1, concat_axis=0, tiled=True)
    chan_count = lax.axis_size("chan")
    whole = gather_by_doubling(own.reshape(chan_count, each, own.shape[1]), "seq")
    return whole.transpose(1, 0, 2, 3).reshape(chan_count * group, own.shape[1])


def shards(tokens, in_weight, conv_weight, spectrum, skip, out_weight):
    tok_rows = tokens.shape[0]
    seq_count = lax.axis_size("seq")
    gathered = lax.all_gather(tokens, "chan", axis=1, tiled=True)
    response = folded_response(spectrum, seq_count)
    weight_slice = feature_slice(out_weight, seq_count)
    projected = jnp.einsum(
        "td,pdc->pct", gathered, in_weight, preferred_element_type=jnp.float32
    ).astype(jnp.bfloat16)
    margin = TAPS - 1
    earlier = from_behind(projected[:, :, tok_rows - margin :], "seq", 1)
    extended = jnp.concatenate([earlier, projected], axis=2).astype(jnp.float32)
    filtered = conv_weight[0][:, :, None] * extended[:, :, margin : margin + tok_rows]
    for tap_index in range(1, TAPS):
        filtered = (
            filtered
            + conv_weight[tap_index][:, :, None]
            * extended[:, :, margin - tap_index : margin - tap_index + tok_rows]
        )
    query_rows = filtered[0]
    signal = (filtered[1] * filtered[2]).astype(jnp.bfloat16)
    chans = signal.shape[0]
    values = signal.reshape(seq_count, chans // seq_count, tok_rows)
    values = lax.all_to_all(values, "seq", split_axis=0, concat_axis=0, tiled=True)
    longconv = lax.all_to_all(
        long_conv(values, response), "seq", split_axis=0, concat_axis=0, tiled=True
    ).reshape(chans, tok_rows).astype(jnp.float32)
    gated = (query_rows * (longconv + skip[:, None] * signal.astype(jnp.float32))).astype(
        jnp.bfloat16
    )
    gated = lax.all_gather(gated, "chan", axis=0, tiled=True)
    return lax.dot_general(
        gated, weight_slice, (((0,), (0,)), ((), ())), preferred_element_type=jnp.float32
    ).astype(jnp.bfloat16)


def solution(mesh):
    placed = (
        P("seq", "chan"),
        P(None, None, "chan"),
        P(None, None, "chan"),
        P(None, "chan", "seq", None),
        P("chan"),
        P("chan", None),
    )
    return jax.shard_map(
        shards, mesh=mesh, in_specs=placed, out_specs=P("seq", "chan"), check_vma=False
    )
```

```python
import jax
import jax.numpy as jnp
import numpy as np
from jax import lax
from jax.experimental import pallas as pl
from jax.experimental.pallas import tpu as pltpu
from jax.sharding import PartitionSpec as P

TAPS = 3
LANES = 128
HALO = 16
CHAN_BLOCK = 16
CHUNK_QUARTERS = (1, 1, 2)
VMEM_BYTES = 48 * 1024 * 1024


def from_behind(value, axis, by):
    size = lax.axis_size(axis)
    pairs = [(i, i + by) for i in range(size) if 0 <= i + by < size]
    return lax.ppermute(value, axis, pairs)


def gather_by_doubling(value, axis):
    size = lax.axis_size(axis)
    index = lax.axis_index(axis)
    held = value[None]
    bit = size // 2
    while bit >= 1:
        other = lax.ppermute(held, axis, [(i, i ^ bit) for i in range(size)])
        upper = (index // bit) % 2 == 1
        first = jnp.where(upper, other, held)
        second = jnp.where(upper, held, other)
        held = jnp.stack([first, second], axis=1).reshape((2 * held.shape[0],) + held.shape[1:])
        bit //= 2
    return held


def chunk_ranges(chans, seq_count):
    quarter = chans // sum(CHUNK_QUARTERS)
    if quarter % LANES or (quarter // seq_count) % CHAN_BLOCK:
        return [(0, chans)]
    ends = np.cumsum(CHUNK_QUARTERS) * quarter
    return [(int(end) - size * quarter, int(end)) for end, size in zip(ends, CHUNK_QUARTERS)]


def project_kernel(extras, tok_ref, w_ref, taps_ref, *rest):
    signal_ref, signal_t_ref, query_t_ref, acc = rest[extras:]
    step = pl.program_id(1)
    rows = signal_t_ref.shape[0]
    for p in range(3):
        part = jnp.dot(tok_ref[0], w_ref[p], preferred_element_type=jnp.float32)
        acc[p] = part + jnp.where(step == 0, 0.0, acc[p])

    @pl.when(step == pl.num_programs(1) - 1)
    def _():
        for p in range(3):
            acc[p] = acc[p].astype(jnp.bfloat16).astype(jnp.float32)
        tile = min(LANES, rows)
        for r in range(0, rows, tile):
            streams = []
            for p in range(3):
                total = taps_ref[0, p][None, :] * acc[p, pl.ds(HALO + r, tile), :]
                for j in range(1, TAPS):
                    total = total + taps_ref[j, p][None, :] * acc[p, pl.ds(HALO + r - j, tile), :]
                streams.append(total)
            signal = streams[1] * streams[2]
            query_t_ref[r : r + tile, :] = streams[0].astype(query_t_ref.dtype)
            signal_t_ref[r : r + tile, :] = signal.astype(signal_t_ref.dtype)
            signal_ref[:, r : r + tile] = signal.T.astype(signal_ref.dtype)


def project(gathered, in_weight, conv_weight, *after):
    parts, held_rows, depth = gathered.shape
    rows = held_rows - HALO
    chans = in_weight.shape[2]
    tile = 2 * LANES if chans % (2 * LANES) == 0 else chans
    flat = jax.ShapeDtypeStruct((rows, chans), jnp.bfloat16)
    return pl.pallas_call(
        lambda *refs: project_kernel(len(after), *refs),
        grid=(chans // tile, parts),
        in_specs=[
            pl.BlockSpec((1, held_rows, depth), lambda i, z: (z, 0, 0)),
            pl.BlockSpec((3, depth, tile), lambda i, z: (0, z, i)),
            pl.BlockSpec((TAPS, 3, tile), lambda i, z: (0, 0, i)),
            *[pl.BlockSpec(memory_space=pl.ANY) for _ in after],
        ],
        out_specs=[
            pl.BlockSpec((tile, rows), lambda i, z: (i, 0)),
            pl.BlockSpec((rows, tile), lambda i, z: (0, i)),
            pl.BlockSpec((rows, tile), lambda i, z: (0, i)),
        ],
        out_shape=[jax.ShapeDtypeStruct((chans, rows), jnp.bfloat16), flat, flat],
        scratch_shapes=[pltpu.VMEM((3, held_rows, tile), jnp.float32)],
        compiler_params=pltpu.CompilerParams(vmem_limit_bytes=VMEM_BYTES),
        cost_estimate=pl.CostEstimate(
            flops=2 * 3 * held_rows * depth * parts * chans,
            bytes_accessed=2 * depth * parts * (3 * chans + 2 * held_rows),
            transcendentals=0,
        ),
    )(gathered, in_weight, conv_weight, *after)


def transform_tables(seq_count, tok_rows):
    runs = tok_rows // LANES
    wide = 2 * seq_count * runs
    fft_len = wide * LANES
    k1 = np.arange(seq_count + 1)[:, None]
    k2a = np.arange(runs)[None, :]
    ka = (k1 + 2 * seq_count * k2a).reshape(-1)
    a = np.arange(seq_count * runs)
    b = np.arange(LANES)
    outer = 2.0 * np.pi * ((ka[:, None] * a[None, :]) % wide) / wide
    first = np.concatenate([np.cos(outer), -np.sin(outer)], axis=0)
    last = first.T / fft_len
    turn = 2.0 * np.pi * ((ka[:, None] * b[None, :]) % fft_len) / fft_len
    inner = 2.0 * np.pi * ((b[:, None] * b[None, :]) % LANES) / LANES
    cos, sin = np.cos(inner), np.sin(inner)
    forward = np.block([[cos, -sin], [sin, cos]])
    backward = np.block([[cos, sin], [-sin, cos]])
    half = lambda table: jnp.asarray(table, jnp.bfloat16)
    full = lambda table: jnp.asarray(table, jnp.float32)
    return half(first), half(last), full(np.cos(turn)), full(np.sin(turn)), half(forward), half(backward)


def conv_kernel(signal_ref, resp_ref, first_ref, last_ref, cos_ref, sin_ref, fwd_ref, bwd_ref, out_ref, held, low, high):
    seq_count, block, tok_rows = signal_ref.shape
    runs = tok_rows // LANES
    span = seq_count * runs
    rows = cos_ref.shape[0]
    pair = 2 * rows
    for s in range(seq_count):
        for r in range(runs):
            piece = signal_ref[s, :, r * LANES : (r + 1) * LANES].astype(jnp.float32)
            held[pl.ds(s * runs + r, block, stride=span), :] = piece
    cos, sin = cos_ref[...], sin_ref[...]
    for c in range(0, block, 2):
        x = jnp.concatenate([held[c * span : (c + 1) * span, :], held[(c + 1) * span : (c + 2) * span, :]], axis=1)
        y = jnp.dot(first_ref[...], x.astype(jnp.bfloat16), preferred_element_type=jnp.float32)
        turned = []
        for half in (slice(0, LANES), slice(LANES, 2 * LANES)):
            re, im = y[:rows, half], y[rows:, half]
            turned.append(jnp.concatenate([re * cos + im * sin, im * cos - re * sin], axis=1))
        low[c * rows : c * rows + pair, :] = jnp.concatenate(turned, axis=0).astype(jnp.bfloat16)
    high[...] = jnp.dot(low[...], fwd_ref[...], preferred_element_type=jnp.float32)
    for c in range(0, block, 2):
        done = []
        for d in (c, c + 1):
            re = high[d * rows : (d + 1) * rows, :LANES]
            im = high[d * rows : (d + 1) * rows, LANES:]
            hr = resp_ref[0, d].astype(jnp.float32)
            hi = resp_ref[1, d].astype(jnp.float32)
            done.append(jnp.concatenate([re * hr - im * hi, re * hi + im * hr], axis=1))
        low[c * rows : c * rows + pair, :] = jnp.concatenate(done, axis=0).astype(jnp.bfloat16)
    high[...] = jnp.dot(low[...], bwd_ref[...], preferred_element_type=jnp.float32)
    for c in range(0, block, 2):
        turned = []
        for d in (c, c + 1):
            re = high[d * rows : (d + 1) * rows, :LANES]
            im = high[d * rows : (d + 1) * rows, LANES:]
            turned.append(jnp.concatenate([re * cos - im * sin, im * cos + re * sin], axis=0))
        w = jnp.concatenate(turned, axis=1).astype(jnp.bfloat16)
        y = jnp.dot(last_ref[...], w, preferred_element_type=jnp.float32)
        held[c * span : (c + 1) * span, :] = y[:, :LANES]
        held[(c + 1) * span : (c + 2) * span, :] = y[:, LANES:]
    for s in range(seq_count):
        for r in range(runs):
            piece = held[pl.ds(s * runs + r, block, stride=span), :]
            out_ref[s, :, r * LANES : (r + 1) * LANES] = piece.astype(out_ref.dtype)


def long_conv(values, response, start=0):
    seq_count, chans, tok_rows = values.shape
    rows = response.shape[2]
    block = min(CHAN_BLOCK, chans)
    tables = transform_tables(seq_count, tok_rows)
    fixed = [pl.BlockSpec(t.shape, lambda i: (0, 0)) for t in tables]
    span = seq_count * tok_rows // LANES
    flops = chans * 2 * (2 * 2 * rows * span * LANES + 2 * rows * 4 * LANES * LANES)
    moved = 2 * (2 * values.size + 2 * chans * rows * LANES)
    return pl.pallas_call(
        conv_kernel,
        grid=(chans // block,),
        in_specs=[
            pl.BlockSpec((seq_count, block, tok_rows), lambda i: (0, i, 0)),
            pl.BlockSpec((2, block, rows, LANES), lambda i: (0, start // block + i, 0, 0)),
            *fixed,
        ],
        out_specs=pl.BlockSpec((seq_count, block, tok_rows), lambda i: (0, i, 0)),
        out_shape=jax.ShapeDtypeStruct((seq_count, chans, tok_rows), jnp.bfloat16),
        scratch_shapes=[
            pltpu.VMEM((block * span, LANES), jnp.float32),
            pltpu.VMEM((block * rows, 2 * LANES), jnp.bfloat16),
            pltpu.VMEM((block * rows, 2 * LANES), jnp.float32),
        ],
        compiler_params=pltpu.CompilerParams(vmem_limit_bytes=VMEM_BYTES),
        cost_estimate=pl.CostEstimate(flops=flops, bytes_accessed=moved, transcendentals=0),
    )(values, response, *tables)


def gate_kernel(conv_ref, skip_ref, *refs):
    out_ref = refs[-1]
    conv = conv_ref[...].astype(jnp.float32).T
    skip = skip_ref[...]
    at = 0
    for signal_ref, query_ref in zip(refs[0:-1:2], refs[1:-1:2]):
        rows = signal_ref.shape[0]
        inner = conv[at : at + rows] + skip * signal_ref[...].astype(jnp.float32)
        out_ref[at : at + rows, :] = (query_ref[...].astype(jnp.float32) * inner).astype(out_ref.dtype)
        at += rows


def gate(longconv, skip, start, pieces):
    chans, tok_rows = longconv.shape
    first = start // LANES
    given, specs = [], []
    for piece in pieces:
        for array in piece:
            given.append(array)
            specs.append(pl.BlockSpec((array.shape[0], LANES), lambda i: (0, first + i)))
    return pl.pallas_call(
        gate_kernel,
        grid=(chans // LANES,),
        in_specs=[
            pl.BlockSpec((LANES, tok_rows), lambda i: (i, 0)),
            pl.BlockSpec((1, LANES), lambda i: (0, first + i)),
            *specs,
        ],
        out_specs=pl.BlockSpec((tok_rows, LANES), lambda i: (0, i)),
        out_shape=jax.ShapeDtypeStruct((tok_rows, chans), jnp.bfloat16),
        compiler_params=pltpu.CompilerParams(vmem_limit_bytes=VMEM_BYTES),
        cost_estimate=pl.CostEstimate(flops=4 * chans * tok_rows, bytes_accessed=8 * chans * tok_rows, transcendentals=0),
    )(longconv, skip[None, :], *given)


def folded_response(spectrum, seq_count, ranges):
    parts, chans, own, tok_rows = spectrum.shape
    runs = tok_rows // LANES
    each = chans // seq_count
    sent = spectrum.astype(jnp.bfloat16)
    sent = jnp.concatenate(
        [sent[:, lo:hi].reshape(parts, seq_count, (hi - lo) // seq_count, own, LANES, runs) for lo, hi in ranges],
        axis=2,
    )
    sent = sent.transpose(1, 0, 2, 3, 5, 4)
    got = lax.all_to_all(sent, "seq", split_axis=0, concat_axis=0, tiled=True)
    got = got.transpose(1, 2, 0, 3, 4, 5).reshape(parts, each, own * seq_count, runs, LANES)
    kept = got[:, :, : seq_count + 1].astype(jnp.float32)
    mirror = got[:, :, seq_count + 1 :][:, :, ::-1, ::-1, ::-1].astype(jnp.float32)
    mirror = jnp.stack([mirror[0], -mirror[1]])
    mirror = jnp.pad(mirror, ((0, 0), (0, 0), (1, 1), (0, 0), (0, 0)))
    return (kept + mirror).astype(jnp.bfloat16).reshape(parts, each, (seq_count + 1) * runs, LANES)


def feature_slice(out_weight, seq_count):
    group = out_weight.shape[0]
    each = group // seq_count
    own = lax.dynamic_slice_in_dim(out_weight, lax.axis_index("seq") * each, each, axis=0)
    own = lax.all_to_all(own, "chan", split_axis=1, concat_axis=0, tiled=True)
    chan_count = lax.axis_size("chan")
    whole = gather_by_doubling(own.reshape(chan_count, each, own.shape[1]), "seq")
    return whole.transpose(1, 0, 2, 3).reshape(chan_count, group, own.shape[1])


def shards(tokens, in_weight, conv_weight, spectrum, skip, out_weight):
    tok_rows = tokens.shape[0]
    seq_count = lax.axis_size("seq")
    chans = in_weight.shape[2]
    ranges = chunk_ranges(chans, seq_count)
    cut = tok_rows // 4
    later = lax.all_gather(tokens[cut - HALO :], "chan")
    halo = from_behind(tokens[tok_rows - HALO :], "seq", 1)
    earlier = lax.all_gather(jnp.concatenate([halo, tokens[:cut]], axis=0), "chan")
    response = folded_response(spectrum, seq_count, ranges)
    weight_slice = feature_slice(out_weight, seq_count)
    signal_b, signal_bt, query_bt = project(later, in_weight, conv_weight)
    signal_a, signal_at, query_at = project(earlier, in_weight, conv_weight, response, weight_slice)
    signal = jnp.concatenate([signal_a, signal_b], axis=1)
    pieces = ((signal_at, query_at), (signal_bt, query_bt))
    total = None
    for lo, hi in ranges:
        values = signal[lo:hi].reshape(seq_count, (hi - lo) // seq_count, tok_rows)
        values = lax.all_to_all(values, "seq", split_axis=0, concat_axis=0, tiled=True)
        longconv = lax.all_to_all(
            long_conv(values, response, lo // seq_count), "seq", split_axis=0, concat_axis=0, tiled=True
        ).reshape(hi - lo, tok_rows)
        gated = lax.all_gather(gate(longconv, skip, lo, pieces), "chan", axis=1, tiled=True)
        weight = weight_slice[:, lo:hi].reshape(gated.shape[1], weight_slice.shape[2])
        term = jnp.dot(gated, weight, preferred_element_type=jnp.float32)
        total = term if total is None else total + term
    return total.astype(jnp.bfloat16)


def solution(mesh):
    placed = (
        P("seq", "chan"),
        P(None, None, "chan"),
        P(None, None, "chan"),
        P(None, "chan", "seq", None),
        P("chan"),
        P("chan", None),
    )
    return jax.shard_map(
        shards, mesh=mesh, in_specs=placed, out_specs=P("seq", "chan"), check_vma=False
    )
```

```python
import jax
import jax.numpy as jnp
import numpy as np
from jax import lax
from jax.experimental import pallas as pl
from jax.experimental.pallas import tpu as pltpu
from jax.sharding import PartitionSpec as P

TAPS = 3
LANES = 128
HALO = 16
CHAN_BLOCK = 16
CHUNKS = 2
VMEM_BYTES = 48 * 1024 * 1024


def from_behind(value, axis, by):
    size = lax.axis_size(axis)
    pairs = [(i, i + by) for i in range(size) if 0 <= i + by < size]
    return lax.ppermute(value, axis, pairs)


def gather_by_doubling(value, axis):
    size = lax.axis_size(axis)
    index = lax.axis_index(axis)
    held = value[None]
    bit = size // 2
    while bit >= 1:
        other = lax.ppermute(held, axis, [(i, i ^ bit) for i in range(size)])
        upper = (index // bit) % 2 == 1
        first = jnp.where(upper, other, held)
        second = jnp.where(upper, held, other)
        held = jnp.stack([first, second], axis=1).reshape((2 * held.shape[0],) + held.shape[1:])
        bit //= 2
    return held


def chunk_count(chans, seq_count):
    size = chans // CHUNKS
    return 1 if size % LANES or (size // seq_count) % CHAN_BLOCK else CHUNKS


def project_kernel(extras, tok_ref, w_ref, taps_ref, halo_ref, *rest):
    signal_ref, signal_t_ref, query_t_ref, tok, held, keys, sems = rest[extras:]
    rows = tok.shape[0]
    tile = rows // sems.shape[0]
    stream = pl.program_id(1)
    first = jnp.logical_and(pl.program_id(0) == 0, stream == 0)
    pieces = [pl.ds(r, tile) for r in range(0, rows, tile)]
    copies = [pltpu.make_async_copy(tok_ref.at[p], tok.at[p], sems.at[i]) for i, p in enumerate(pieces)]

    @pl.when(first)
    def _():
        for copy in copies:
            copy.start()

    held[0:HALO, :] = halo_ref[0].astype(jnp.float32)
    for r, copy in zip(range(0, rows, tile), copies):
        pl.when(first)(copy.wait)
        part = jnp.dot(tok[r : r + tile, :], w_ref[0], preferred_element_type=jnp.float32)
        held[HALO + r : HALO + r + tile, :] = part.astype(jnp.bfloat16).astype(jnp.float32)

    def filtered(r, size):
        total = taps_ref[0, 0] * held[pl.ds(HALO + r, size), :]
        for j in range(1, TAPS):
            total = total + taps_ref[0, j] * held[pl.ds(HALO + r - j, size), :]
        return total

    @pl.when(stream == 0)
    def _():
        for r in range(0, rows, LANES):
            query_t_ref[r : r + LANES, :] = filtered(r, LANES).astype(query_t_ref.dtype)

    @pl.when(stream == 1)
    def _():
        for r in range(0, rows, LANES):
            keys[r : r + LANES, :] = filtered(r, LANES)

    @pl.when(stream == 2)
    def _():
        for r in range(0, rows, LANES):
            signal = keys[r : r + LANES, :] * filtered(r, LANES)
            signal_t_ref[r : r + LANES, :] = signal.astype(signal_t_ref.dtype)
            signal_ref[:, r : r + LANES] = signal.T.astype(signal_ref.dtype)


def project(gathered, in_weight, conv_weight, halo, *after):
    rows, depth = gathered.shape
    chans = in_weight.shape[2]
    tile = 2 * LANES if chans % (2 * LANES) == 0 else chans
    pieces = 4
    flat = jax.ShapeDtypeStruct((rows, chans), jnp.bfloat16)
    taps = conv_weight.transpose(1, 0, 2)[:, :, None, :]
    return pl.pallas_call(
        lambda *refs: project_kernel(len(after), *refs),
        grid=(chans // tile, 3),
        in_specs=[
            pl.BlockSpec(memory_space=pl.ANY),
            pl.BlockSpec((1, depth, tile), lambda i, p: (p, 0, i)),
            pl.BlockSpec((1, TAPS, 1, tile), lambda i, p: (p, 0, 0, i)),
            pl.BlockSpec((1, HALO, tile), lambda i, p: (p, 0, i)),
            *[pl.BlockSpec(memory_space=pl.ANY) for _ in after],
        ],
        out_specs=[
            pl.BlockSpec((tile, rows), lambda i, p: (i, 0)),
            pl.BlockSpec((rows, tile), lambda i, p: (0, i)),
            pl.BlockSpec((rows, tile), lambda i, p: (0, i)),
        ],
        out_shape=[jax.ShapeDtypeStruct((chans, rows), jnp.bfloat16), flat, flat],
        scratch_shapes=[
            pltpu.VMEM((rows, depth), jnp.bfloat16),
            pltpu.VMEM((HALO + rows, tile), jnp.float32),
            pltpu.VMEM((rows, tile), jnp.float32),
            pltpu.SemaphoreType.DMA((pieces,)),
        ],
        compiler_params=pltpu.CompilerParams(vmem_limit_bytes=VMEM_BYTES),
        cost_estimate=pl.CostEstimate(
            flops=2 * 3 * rows * depth * chans,
            bytes_accessed=2 * depth * (3 * chans + rows),
            transcendentals=0,
        ),
    )(gathered, in_weight, taps, halo, *after)


def transform_tables(seq_count, tok_rows):
    runs = tok_rows // LANES
    wide = 2 * seq_count * runs
    fft_len = wide * LANES
    k1 = np.arange(seq_count + 1)[:, None]
    k2a = np.arange(runs)[None, :]
    ka = (k1 + 2 * seq_count * k2a).reshape(-1)
    a = np.arange(seq_count * runs)
    b = np.arange(LANES)
    outer = 2.0 * np.pi * ((ka[:, None] * a[None, :]) % wide) / wide
    first = np.concatenate([np.cos(outer), -np.sin(outer)], axis=0)
    last = first.T / fft_len
    turn = 2.0 * np.pi * ((ka[:, None] * b[None, :]) % fft_len) / fft_len
    inner = 2.0 * np.pi * ((b[:, None] * b[None, :]) % LANES) / LANES
    cos, sin = np.cos(inner), np.sin(inner)
    forward = np.block([[cos, -sin], [sin, cos]])
    backward = np.block([[cos, sin], [-sin, cos]])
    half = lambda table: jnp.asarray(table, jnp.bfloat16)
    full = lambda table: jnp.asarray(table, jnp.float32)
    return half(first), half(last), full(np.cos(turn)), full(np.sin(turn)), half(forward), half(backward)


def conv_kernel(signal_ref, resp_ref, first_ref, last_ref, cos_ref, sin_ref, fwd_ref, bwd_ref, out_ref, held, low, high):
    seq_count, block, tok_rows = signal_ref.shape
    runs = tok_rows // LANES
    span = seq_count * runs
    rows = cos_ref.shape[0]
    pair = 2 * rows
    for s in range(seq_count):
        for r in range(runs):
            piece = signal_ref[s, :, r * LANES : (r + 1) * LANES].astype(jnp.float32)
            held[pl.ds(s * runs + r, block, stride=span), :] = piece
    cos, sin = cos_ref[...], sin_ref[...]
    for c in range(0, block, 2):
        x = jnp.concatenate([held[c * span : (c + 1) * span, :], held[(c + 1) * span : (c + 2) * span, :]], axis=1)
        y = jnp.dot(first_ref[...], x.astype(jnp.bfloat16), preferred_element_type=jnp.float32)
        turned = []
        for half in (slice(0, LANES), slice(LANES, 2 * LANES)):
            re, im = y[:rows, half], y[rows:, half]
            turned.append(jnp.concatenate([re * cos + im * sin, im * cos - re * sin], axis=1))
        low[c * rows : c * rows + pair, :] = jnp.concatenate(turned, axis=0).astype(jnp.bfloat16)
    high[...] = jnp.dot(low[...], fwd_ref[...], preferred_element_type=jnp.float32)
    for c in range(0, block, 2):
        done = []
        for d in (c, c + 1):
            re = high[d * rows : (d + 1) * rows, :LANES]
            im = high[d * rows : (d + 1) * rows, LANES:]
            hr = resp_ref[0, d].astype(jnp.float32)
            hi = resp_ref[1, d].astype(jnp.float32)
            done.append(jnp.concatenate([re * hr - im * hi, re * hi + im * hr], axis=1))
        low[c * rows : c * rows + pair, :] = jnp.concatenate(done, axis=0).astype(jnp.bfloat16)
    high[...] = jnp.dot(low[...], bwd_ref[...], preferred_element_type=jnp.float32)
    for c in range(0, block, 2):
        turned = []
        for d in (c, c + 1):
            re = high[d * rows : (d + 1) * rows, :LANES]
            im = high[d * rows : (d + 1) * rows, LANES:]
            turned.append(jnp.concatenate([re * cos - im * sin, im * cos + re * sin], axis=0))
        w = jnp.concatenate(turned, axis=1).astype(jnp.bfloat16)
        y = jnp.dot(last_ref[...], w, preferred_element_type=jnp.float32)
        held[c * span : (c + 1) * span, :] = y[:, :LANES]
        held[(c + 1) * span : (c + 2) * span, :] = y[:, LANES:]
    for s in range(seq_count):
        for r in range(runs):
            piece = held[pl.ds(s * runs + r, block, stride=span), :]
            out_ref[s, :, r * LANES : (r + 1) * LANES] = piece.astype(out_ref.dtype)


def long_conv(values, response, start=0):
    seq_count, chans, tok_rows = values.shape
    rows = response.shape[2]
    block = min(CHAN_BLOCK, chans)
    tables = transform_tables(seq_count, tok_rows)
    fixed = [pl.BlockSpec(t.shape, lambda i: (0, 0)) for t in tables]
    span = seq_count * tok_rows // LANES
    flops = chans * 2 * (2 * 2 * rows * span * LANES + 2 * rows * 4 * LANES * LANES)
    moved = 2 * (2 * values.size + 2 * chans * rows * LANES)
    return pl.pallas_call(
        conv_kernel,
        grid=(chans // block,),
        in_specs=[
            pl.BlockSpec((seq_count, block, tok_rows), lambda i: (0, i, 0)),
            pl.BlockSpec((2, block, rows, LANES), lambda i: (0, start // block + i, 0, 0)),
            *fixed,
        ],
        out_specs=pl.BlockSpec((seq_count, block, tok_rows), lambda i: (0, i, 0)),
        out_shape=jax.ShapeDtypeStruct((seq_count, chans, tok_rows), jnp.bfloat16),
        scratch_shapes=[
            pltpu.VMEM((block * span, LANES), jnp.float32),
            pltpu.VMEM((block * rows, 2 * LANES), jnp.bfloat16),
            pltpu.VMEM((block * rows, 2 * LANES), jnp.float32),
        ],
        compiler_params=pltpu.CompilerParams(vmem_limit_bytes=VMEM_BYTES),
        cost_estimate=pl.CostEstimate(flops=flops, bytes_accessed=moved, transcendentals=0),
    )(values, response, *tables)


def gate_kernel(conv_ref, skip_ref, *refs):
    out_ref = refs[-1]
    conv = conv_ref[...].astype(jnp.float32).T
    skip = skip_ref[...]
    at = 0
    for signal_ref, query_ref in zip(refs[0:-1:2], refs[1:-1:2]):
        rows = signal_ref.shape[0]
        inner = conv[at : at + rows] + skip * signal_ref[...].astype(jnp.float32)
        out_ref[at : at + rows, :] = (query_ref[...].astype(jnp.float32) * inner).astype(out_ref.dtype)
        at += rows


def gate(longconv, skip, start, pieces):
    chans, tok_rows = longconv.shape
    first = start // LANES
    given, specs = [], []
    for piece in pieces:
        for array in piece:
            given.append(array)
            specs.append(pl.BlockSpec((array.shape[0], LANES), lambda i: (0, first + i)))
    return pl.pallas_call(
        gate_kernel,
        grid=(chans // LANES,),
        in_specs=[
            pl.BlockSpec((LANES, tok_rows), lambda i: (i, 0)),
            pl.BlockSpec((1, LANES), lambda i: (0, first + i)),
            *specs,
        ],
        out_specs=pl.BlockSpec((tok_rows, LANES), lambda i: (0, i)),
        out_shape=jax.ShapeDtypeStruct((tok_rows, chans), jnp.bfloat16),
        compiler_params=pltpu.CompilerParams(vmem_limit_bytes=VMEM_BYTES),
        cost_estimate=pl.CostEstimate(flops=4 * chans * tok_rows, bytes_accessed=8 * chans * tok_rows, transcendentals=0),
    )(longconv, skip[None, :], *given)


def reorder_kernel(spec_ref, order_ref, out_ref):
    each = out_ref.shape[3]
    x = spec_ref[0].astype(jnp.bfloat16)
    y = jnp.dot(x, order_ref[...], preferred_element_type=jnp.float32).astype(jnp.bfloat16)
    for d in range(out_ref.shape[0]):
        out_ref[d, 0, 0] = y[d * each : (d + 1) * each]


def fold_kernel(got_ref, out_ref, came, held):
    seq_count, pairs, tok_rows = got_ref.shape[0], got_ref.shape[3], got_ref.shape[4]
    chans = pairs // 2
    runs = tok_rows // LANES
    rows = (seq_count + 1) * runs
    for part in range(2):
        sign = 1.0 if part == 0 else -1.0
        for s in range(seq_count):
            for r in range(runs):
                at = (s * runs + r) * pairs
                lanes = slice(r * LANES, (r + 1) * LANES)
                came[at : at + pairs, :] = got_ref[s, part, 0, :, lanes].astype(jnp.float32)
        for k1 in range(seq_count + 1):
            other = 2 * seq_count - k1
            for r in range(runs):
                value = came[pl.ds((k1 // 2 * runs + r) * pairs + k1 % 2, chans, stride=2), :]
                if k1 == seq_count:
                    value = sign * value
                elif k1 > 0:
                    value = value + sign * came[pl.ds((other // 2 * runs + r) * pairs + other % 2, chans, stride=2), :]
                held[pl.ds(k1 * runs + r, chans, stride=rows), :] = value
        out_ref[part] = held[...].reshape(chans, rows, LANES).astype(out_ref.dtype)


def folded_response(spectrum, seq_count, chunks):
    parts, chans, own, tok_rows = spectrum.shape
    runs = tok_rows // LANES
    size = chans // chunks
    each = size // seq_count
    col = lax.broadcasted_iota(jnp.int32, (tok_rows, tok_rows), 1)
    row = lax.broadcasted_iota(jnp.int32, (tok_rows, tok_rows), 0)
    wanted = col // LANES + runs * (col % LANES)
    wanted = jnp.where(lax.axis_index("seq") >= seq_count // 2, tok_rows - 1 - wanted, wanted)
    order = (row == wanted).astype(jnp.bfloat16)
    shape = (seq_count, parts, chunks, own * each, tok_rows)
    sent = pl.pallas_call(
        reorder_kernel,
        grid=(parts, chunks),
        in_specs=[
            pl.BlockSpec((1, own * size, tok_rows), lambda p, j: (p, j, 0)),
            pl.BlockSpec((tok_rows, tok_rows), lambda p, j: (0, 0)),
        ],
        out_specs=pl.BlockSpec((seq_count, 1, 1, own * each, tok_rows), lambda p, j: (0, p, j, 0, 0)),
        out_shape=jax.ShapeDtypeStruct(shape, jnp.bfloat16),
        compiler_params=pltpu.CompilerParams(vmem_limit_bytes=VMEM_BYTES),
        cost_estimate=pl.CostEstimate(
            flops=2 * spectrum.size * tok_rows, bytes_accessed=6 * spectrum.size, transcendentals=0
        ),
    )(spectrum.reshape(parts, chans * own, tok_rows), order)
    got = lax.all_to_all(sent, "seq", split_axis=0, concat_axis=0, tiled=True)
    block = min(CHAN_BLOCK, each)
    rows = (seq_count + 1) * runs
    return pl.pallas_call(
        fold_kernel,
        grid=(chunks, each // block),
        in_specs=[pl.BlockSpec((seq_count, parts, 1, own * block, tok_rows), lambda j, i: (0, 0, j, i, 0))],
        out_specs=pl.BlockSpec((parts, block, rows, LANES), lambda j, i: (0, j * (each // block) + i, 0, 0)),
        out_shape=jax.ShapeDtypeStruct((parts, chans // seq_count, rows, LANES), jnp.bfloat16),
        scratch_shapes=[
            pltpu.VMEM((seq_count * runs * own * block, LANES), jnp.float32),
            pltpu.VMEM((block * rows, LANES), jnp.float32),
        ],
        compiler_params=pltpu.CompilerParams(vmem_limit_bytes=VMEM_BYTES),
        cost_estimate=pl.CostEstimate(flops=spectrum.size, bytes_accessed=3 * spectrum.size, transcendentals=0),
    )(got)


def feature_slice(out_weight, seq_count):
    group = out_weight.shape[0]
    each = group // seq_count
    own = lax.dynamic_slice_in_dim(out_weight, lax.axis_index("seq") * each, each, axis=0)
    own = lax.all_to_all(own, "chan", split_axis=1, concat_axis=0, tiled=True)
    chan_count = lax.axis_size("chan")
    whole = gather_by_doubling(own.reshape(chan_count, each, own.shape[1]), "seq")
    return whole.transpose(1, 0, 2, 3).reshape(chan_count, group, own.shape[1])


def shards(tokens, in_weight, conv_weight, spectrum, skip, out_weight):
    tok_rows, depth = tokens.shape
    seq_count = lax.axis_size("seq")
    chan_count = lax.axis_size("chan")
    chans = in_weight.shape[2]
    chunks = chunk_count(chans, seq_count)
    size = chans // chunks
    gathered = lax.all_gather(tokens, "chan", axis=1, tiled=True)
    halo = gather_by_doubling(from_behind(tokens[tok_rows - HALO :], "seq", 1), "chan")
    halo = jnp.einsum(
        "ztd,pzdc->ptc",
        halo,
        in_weight.reshape(3, chan_count, depth, chans),
        preferred_element_type=jnp.float32,
    ).astype(jnp.bfloat16)
    response = folded_response(spectrum, seq_count, chunks)
    weight_slice = feature_slice(out_weight, seq_count)
    signal, signal_t, query_t = project(gathered, in_weight, conv_weight, halo, response, weight_slice)
    total = None
    for lo in range(0, chans, size):
        values = signal[lo : lo + size].reshape(seq_count, size // seq_count, tok_rows)
        values = lax.all_to_all(values, "seq", split_axis=0, concat_axis=0, tiled=True)
        longconv = lax.all_to_all(
            long_conv(values, response, lo // seq_count), "seq", split_axis=0, concat_axis=0, tiled=True
        ).reshape(size, tok_rows)
        gated = lax.all_gather(
            gate(longconv, skip, lo, ((signal_t, query_t),)), "chan", axis=1, tiled=True
        )
        weight = weight_slice[:, lo : lo + size].reshape(gated.shape[1], weight_slice.shape[2])
        term = jnp.dot(gated, weight, preferred_element_type=jnp.float32)
        total = term if total is None else total + term
    return total.astype(jnp.bfloat16)


def solution(mesh):
    placed = (
        P("seq", "chan"),
        P(None, None, "chan"),
        P(None, None, "chan"),
        P(None, "chan", "seq", None),
        P("chan"),
        P("chan", None),
    )
    return jax.shard_map(
        shards, mesh=mesh, in_specs=placed, out_specs=P("seq", "chan"), check_vma=False
    )
```

```python
import jax
import jax.numpy as jnp
import numpy as np
from jax import lax
from jax.experimental import pallas as pl
from jax.experimental.pallas import tpu as pltpu
from jax.sharding import PartitionSpec as P

TAPS = 3
LANES = 128
HALO = 16
CHAN_BLOCK = 16
CHUNKS = 2
VMEM_BYTES = 48 * 1024 * 1024


def from_behind(value, axis, by):
    size = lax.axis_size(axis)
    pairs = [(i, i + by) for i in range(size) if 0 <= i + by < size]
    return lax.ppermute(value, axis, pairs)


def shifted(value, axis, by):
    size = lax.axis_size(axis)
    return lax.ppermute(value, axis, [(i, (i + by) % size) for i in range(size)])


def slots_of(value, axis):
    return [value] + [shifted(value, axis, by) for by in range(1, lax.axis_size(axis))]


def gather_by_doubling(value, axis):
    size = lax.axis_size(axis)
    index = lax.axis_index(axis)
    held = value[None]
    bit = size // 2
    while bit >= 1:
        other = lax.ppermute(held, axis, [(i, i ^ bit) for i in range(size)])
        upper = (index // bit) % 2 == 1
        first = jnp.where(upper, other, held)
        second = jnp.where(upper, held, other)
        held = jnp.stack([first, second], axis=1).reshape((2 * held.shape[0],) + held.shape[1:])
        bit //= 2
    return held


def chunk_count(chans, seq_count):
    size = chans // CHUNKS
    return 1 if size % LANES or (size // seq_count) % CHAN_BLOCK else CHUNKS


def project_kernel(slots, extras, me_ref, *refs):
    tok_refs = refs[:slots]
    w_ref, taps_ref, halo_ref = refs[slots : slots + 3]
    signal_ref, signal_t_ref, query_t_ref, tail_ref, acc = refs[slots + 3 + extras :]
    step = pl.program_id(1)
    rows = signal_t_ref.shape[0]
    for z, tok_ref in enumerate(tok_refs):

        @pl.when(step == z)
        def _():
            for p in range(3):
                part = jnp.dot(tok_ref[...], w_ref[p], preferred_element_type=jnp.float32)
                acc[p, HALO:, :] = part if z == 0 else part + acc[p, HALO:, :]

    @pl.when(step == slots - 1)
    def _():
        for p in range(3):
            acc[p, :HALO, :] = halo_ref[p].astype(jnp.float32)
            acc[p, HALO:, :] = acc[p, HALO:, :].astype(jnp.bfloat16).astype(jnp.float32)
            tail_ref[p] = acc[p, rows:, :].astype(tail_ref.dtype)
        for r in range(0, rows, LANES):
            streams = []
            for p in range(3):
                total = taps_ref[0, p][None, :] * acc[p, pl.ds(HALO + r, LANES), :]
                for j in range(1, TAPS):
                    total = total + taps_ref[j, p][None, :] * acc[p, pl.ds(HALO + r - j, LANES), :]
                streams.append(total)
            signal = streams[1] * streams[2]
            query_t_ref[r : r + LANES, :] = streams[0].astype(query_t_ref.dtype)
            signal_t_ref[r : r + LANES, :] = signal.astype(signal_t_ref.dtype)
            signal_ref[:, r : r + LANES] = signal.T.astype(signal_ref.dtype)


def project(slots, in_weight, conv_weight, halo, *after):
    rows, depth = slots[0].shape
    count = len(slots)
    chans = in_weight.shape[2]
    tile = 2 * LANES if chans % (2 * LANES) == 0 else chans
    flat = jax.ShapeDtypeStruct((rows, chans), jnp.bfloat16)
    me = lax.axis_index("chan").astype(jnp.int32).reshape(1)
    return pl.pallas_call(
        lambda *refs: project_kernel(count, len(after), *refs),
        grid_spec=pltpu.PrefetchScalarGridSpec(
            num_scalar_prefetch=1,
            grid=(chans // tile, count),
            in_specs=[
                *[pl.BlockSpec((rows, depth), lambda i, z, me: (0, 0)) for _ in slots],
                pl.BlockSpec((3, depth, tile), lambda i, z, me: (0, lax.rem(me[0] - z + count, count), i)),
                pl.BlockSpec((TAPS, 3, tile), lambda i, z, me: (0, 0, i)),
                pl.BlockSpec((3, HALO, tile), lambda i, z, me: (0, 0, i)),
                *[pl.BlockSpec(memory_space=pl.ANY) for _ in after],
            ],
            out_specs=[
                pl.BlockSpec((tile, rows), lambda i, z, me: (i, 0)),
                pl.BlockSpec((rows, tile), lambda i, z, me: (0, i)),
                pl.BlockSpec((rows, tile), lambda i, z, me: (0, i)),
                pl.BlockSpec((3, HALO, tile), lambda i, z, me: (0, 0, i)),
            ],
            scratch_shapes=[pltpu.VMEM((3, HALO + rows, tile), jnp.float32)],
        ),
        out_shape=[
            jax.ShapeDtypeStruct((chans, rows), jnp.bfloat16),
            flat,
            flat,
            jax.ShapeDtypeStruct((3, HALO, chans), jnp.bfloat16),
        ],
        compiler_params=pltpu.CompilerParams(vmem_limit_bytes=VMEM_BYTES),
        cost_estimate=pl.CostEstimate(
            flops=2 * 3 * rows * depth * count * chans,
            bytes_accessed=2 * depth * count * (3 * chans + rows),
            transcendentals=0,
        ),
    )(me, *slots, in_weight, conv_weight, halo, *after)


def transform_tables(seq_count, tok_rows):
    runs = tok_rows // LANES
    wide = 2 * seq_count * runs
    fft_len = wide * LANES
    k1 = np.arange(seq_count + 1)[:, None]
    k2a = np.arange(runs)[None, :]
    ka = (k1 + 2 * seq_count * k2a).reshape(-1)
    a = np.arange(seq_count * runs)
    b = np.arange(LANES)
    outer = 2.0 * np.pi * ((ka[:, None] * a[None, :]) % wide) / wide
    first = np.concatenate([np.cos(outer), -np.sin(outer)], axis=0)
    last = first.T / fft_len
    turn = 2.0 * np.pi * ((ka[:, None] * b[None, :]) % fft_len) / fft_len
    inner = 2.0 * np.pi * ((b[:, None] * b[None, :]) % LANES) / LANES
    cos, sin = np.cos(inner), np.sin(inner)
    forward = np.block([[cos, -sin], [sin, cos]])
    backward = np.block([[cos, sin], [-sin, cos]])
    half = lambda table: jnp.asarray(table, jnp.bfloat16)
    full = lambda table: jnp.asarray(table, jnp.float32)
    return half(first), half(last), full(np.cos(turn)), full(np.sin(turn)), half(forward), half(backward)


def conv_kernel(signal_ref, resp_ref, first_ref, last_ref, cos_ref, sin_ref, fwd_ref, bwd_ref, out_ref, held, low, high):
    seq_count, block, tok_rows = signal_ref.shape
    runs = tok_rows // LANES
    span = seq_count * runs
    rows = cos_ref.shape[0]
    pair = 2 * rows
    for s in range(seq_count):
        for r in range(runs):
            piece = signal_ref[s, :, r * LANES : (r + 1) * LANES].astype(jnp.float32)
            held[pl.ds(s * runs + r, block, stride=span), :] = piece
    cos, sin = cos_ref[...], sin_ref[...]
    for c in range(0, block, 2):
        x = jnp.concatenate([held[c * span : (c + 1) * span, :], held[(c + 1) * span : (c + 2) * span, :]], axis=1)
        y = jnp.dot(first_ref[...], x.astype(jnp.bfloat16), preferred_element_type=jnp.float32)
        turned = []
        for half in (slice(0, LANES), slice(LANES, 2 * LANES)):
            re, im = y[:rows, half], y[rows:, half]
            turned.append(jnp.concatenate([re * cos + im * sin, im * cos - re * sin], axis=1))
        low[c * rows : c * rows + pair, :] = jnp.concatenate(turned, axis=0).astype(jnp.bfloat16)
    high[...] = jnp.dot(low[...], fwd_ref[...], preferred_element_type=jnp.float32)
    for c in range(0, block, 2):
        done = []
        for d in (c, c + 1):
            re = high[d * rows : (d + 1) * rows, :LANES]
            im = high[d * rows : (d + 1) * rows, LANES:]
            hr = resp_ref[0, d].astype(jnp.float32)
            hi = resp_ref[1, d].astype(jnp.float32)
            done.append(jnp.concatenate([re * hr - im * hi, re * hi + im * hr], axis=1))
        low[c * rows : c * rows + pair, :] = jnp.concatenate(done, axis=0).astype(jnp.bfloat16)
    high[...] = jnp.dot(low[...], bwd_ref[...], preferred_element_type=jnp.float32)
    for c in range(0, block, 2):
        turned = []
        for d in (c, c + 1):
            re = high[d * rows : (d + 1) * rows, :LANES]
            im = high[d * rows : (d + 1) * rows, LANES:]
            turned.append(jnp.concatenate([re * cos - im * sin, im * cos + re * sin], axis=0))
        w = jnp.concatenate(turned, axis=1).astype(jnp.bfloat16)
        y = jnp.dot(last_ref[...], w, preferred_element_type=jnp.float32)
        held[c * span : (c + 1) * span, :] = y[:, :LANES]
        held[(c + 1) * span : (c + 2) * span, :] = y[:, LANES:]
    for s in range(seq_count):
        for r in range(runs):
            piece = held[pl.ds(s * runs + r, block, stride=span), :]
            out_ref[s, :, r * LANES : (r + 1) * LANES] = piece.astype(out_ref.dtype)


def long_conv(values, response, start=0):
    seq_count, chans, tok_rows = values.shape
    rows = response.shape[2]
    block = min(CHAN_BLOCK, chans)
    tables = transform_tables(seq_count, tok_rows)
    fixed = [pl.BlockSpec(t.shape, lambda i: (0, 0)) for t in tables]
    span = seq_count * tok_rows // LANES
    flops = chans * 2 * (2 * 2 * rows * span * LANES + 2 * rows * 4 * LANES * LANES)
    moved = 2 * (2 * values.size + 2 * chans * rows * LANES)
    return pl.pallas_call(
        conv_kernel,
        grid=(chans // block,),
        in_specs=[
            pl.BlockSpec((seq_count, block, tok_rows), lambda i: (0, i, 0)),
            pl.BlockSpec((2, block, rows, LANES), lambda i: (0, start // block + i, 0, 0)),
            *fixed,
        ],
        out_specs=pl.BlockSpec((seq_count, block, tok_rows), lambda i: (0, i, 0)),
        out_shape=jax.ShapeDtypeStruct((seq_count, chans, tok_rows), jnp.bfloat16),
        scratch_shapes=[
            pltpu.VMEM((block * span, LANES), jnp.float32),
            pltpu.VMEM((block * rows, 2 * LANES), jnp.bfloat16),
            pltpu.VMEM((block * rows, 2 * LANES), jnp.float32),
        ],
        compiler_params=pltpu.CompilerParams(vmem_limit_bytes=VMEM_BYTES),
        cost_estimate=pl.CostEstimate(flops=flops, bytes_accessed=moved, transcendentals=0),
    )(values, response, *tables)


def gate_kernel(conv_ref, skip_ref, *refs):
    out_ref = refs[-1]
    conv = conv_ref[...].astype(jnp.float32).T
    skip = skip_ref[...]
    at = 0
    for signal_ref, query_ref in zip(refs[0:-1:2], refs[1:-1:2]):
        rows = signal_ref.shape[0]
        inner = conv[at : at + rows] + skip * signal_ref[...].astype(jnp.float32)
        out_ref[at : at + rows, :] = (query_ref[...].astype(jnp.float32) * inner).astype(out_ref.dtype)
        at += rows


def gate(longconv, skip, start, pieces):
    chans, tok_rows = longconv.shape
    first = start // LANES
    given, specs = [], []
    for piece in pieces:
        for array in piece:
            given.append(array)
            specs.append(pl.BlockSpec((array.shape[0], LANES), lambda i: (0, first + i)))
    return pl.pallas_call(
        gate_kernel,
        grid=(chans // LANES,),
        in_specs=[
            pl.BlockSpec((LANES, tok_rows), lambda i: (i, 0)),
            pl.BlockSpec((1, LANES), lambda i: (0, first + i)),
            *specs,
        ],
        out_specs=pl.BlockSpec((tok_rows, LANES), lambda i: (0, i)),
        out_shape=jax.ShapeDtypeStruct((tok_rows, chans), jnp.bfloat16),
        compiler_params=pltpu.CompilerParams(vmem_limit_bytes=VMEM_BYTES),
        cost_estimate=pl.CostEstimate(flops=4 * chans * tok_rows, bytes_accessed=8 * chans * tok_rows, transcendentals=0),
    )(longconv, skip[None, :], *given)


def reorder_kernel(spec_ref, order_ref, out_ref):
    each = out_ref.shape[3]
    x = spec_ref[0].astype(jnp.bfloat16)
    y = jnp.dot(x, order_ref[...], preferred_element_type=jnp.float32).astype(jnp.bfloat16)
    for d in range(out_ref.shape[0]):
        out_ref[d, 0, 0] = y[d * each : (d + 1) * each]


def fold_kernel(got_ref, out_ref, came, held):
    seq_count, pairs, tok_rows = got_ref.shape[0], got_ref.shape[3], got_ref.shape[4]
    chans = pairs // 2
    runs = tok_rows // LANES
    rows = (seq_count + 1) * runs
    for part in range(2):
        sign = 1.0 if part == 0 else -1.0
        for s in range(seq_count):
            for r in range(runs):
                at = (s * runs + r) * pairs
                lanes = slice(r * LANES, (r + 1) * LANES)
                came[at : at + pairs, :] = got_ref[s, part, 0, :, lanes].astype(jnp.float32)
        for k1 in range(seq_count + 1):
            other = 2 * seq_count - k1
            for r in range(runs):
                value = came[pl.ds((k1 // 2 * runs + r) * pairs + k1 % 2, chans, stride=2), :]
                if k1 == seq_count:
                    value = sign * value
                elif k1 > 0:
                    value = value + sign * came[pl.ds((other // 2 * runs + r) * pairs + other % 2, chans, stride=2), :]
                held[pl.ds(k1 * runs + r, chans, stride=rows), :] = value
        out_ref[part] = held[...].reshape(chans, rows, LANES).astype(out_ref.dtype)


def folded_response(spectrum, seq_count, chunks):
    parts, chans, own, tok_rows = spectrum.shape
    runs = tok_rows // LANES
    size = chans // chunks
    each = size // seq_count
    col = lax.broadcasted_iota(jnp.int32, (tok_rows, tok_rows), 1)
    row = lax.broadcasted_iota(jnp.int32, (tok_rows, tok_rows), 0)
    wanted = col // LANES + runs * (col % LANES)
    wanted = jnp.where(lax.axis_index("seq") >= seq_count // 2, tok_rows - 1 - wanted, wanted)
    order = (row == wanted).astype(jnp.bfloat16)
    shape = (seq_count, parts, chunks, own * each, tok_rows)
    sent = pl.pallas_call(
        reorder_kernel,
        grid=(parts, chunks),
        in_specs=[
            pl.BlockSpec((1, own * size, tok_rows), lambda p, j: (p, j, 0)),
            pl.BlockSpec((tok_rows, tok_rows), lambda p, j: (0, 0)),
        ],
        out_specs=pl.BlockSpec((seq_count, 1, 1, own * each, tok_rows), lambda p, j: (0, p, j, 0, 0)),
        out_shape=jax.ShapeDtypeStruct(shape, jnp.bfloat16),
        compiler_params=pltpu.CompilerParams(vmem_limit_bytes=VMEM_BYTES),
        cost_estimate=pl.CostEstimate(
            flops=2 * spectrum.size * tok_rows, bytes_accessed=6 * spectrum.size, transcendentals=0
        ),
    )(spectrum.reshape(parts, chans * own, tok_rows), order)
    got = lax.all_to_all(sent, "seq", split_axis=0, concat_axis=0, tiled=True)
    block = min(CHAN_BLOCK, each)
    rows = (seq_count + 1) * runs
    return pl.pallas_call(
        fold_kernel,
        grid=(chunks, each // block),
        in_specs=[pl.BlockSpec((seq_count, parts, 1, own * block, tok_rows), lambda j, i: (0, 0, j, i, 0))],
        out_specs=pl.BlockSpec((parts, block, rows, LANES), lambda j, i: (0, j * (each // block) + i, 0, 0)),
        out_shape=jax.ShapeDtypeStruct((parts, chans // seq_count, rows, LANES), jnp.bfloat16),
        scratch_shapes=[
            pltpu.VMEM((seq_count * runs * own * block, LANES), jnp.float32),
            pltpu.VMEM((block * rows, LANES), jnp.float32),
        ],
        compiler_params=pltpu.CompilerParams(vmem_limit_bytes=VMEM_BYTES),
        cost_estimate=pl.CostEstimate(flops=spectrum.size, bytes_accessed=3 * spectrum.size, transcendentals=0),
    )(got)


def feature_rows(out_weight, seq_count):
    each = out_weight.shape[0] // seq_count
    own = lax.dynamic_slice_in_dim(out_weight, lax.axis_index("seq") * each, each, axis=0)
    count = lax.axis_size("chan")
    me = lax.axis_index("chan")
    wide = out_weight.shape[1] // count
    pieces = []
    for by in range(count):
        piece = lax.dynamic_slice_in_dim(own, lax.rem(me + by, count) * wide, wide, axis=1)
        pieces.append(shifted(piece, "chan", by) if by else piece)
    return jnp.stack(pieces)


def combine_kernel(slots, *refs):
    total_ref = refs[slots + 1] if len(refs) == slots + 3 else None
    w_ref, out_ref = refs[slots], refs[-1]
    total = None if total_ref is None else total_ref[...]
    for z in range(slots):
        weight = w_ref[:, z].reshape(refs[z].shape[1], out_ref.shape[1])
        term = jnp.dot(refs[z][...], weight, preferred_element_type=jnp.float32)
        total = term if total is None else total + term
    out_ref[...] = total.astype(out_ref.dtype)


def combine(slots, weight, start, total, dtype):
    tok_rows, size = slots[0].shape
    _, count, each, features = weight.shape
    per = size // each
    first = start // size
    tile = min(2 * LANES, features)
    block = pl.BlockSpec((tok_rows, tile), lambda i: (0, i))
    given = [] if total is None else [total]
    return pl.pallas_call(
        lambda *refs: combine_kernel(count, *refs),
        grid=(features // tile,),
        in_specs=[
            *[pl.BlockSpec((tok_rows, size), lambda i: (0, 0)) for _ in slots],
            pl.BlockSpec((per, count, each, tile), lambda i: (first, 0, 0, i)),
            *[block for _ in given],
        ],
        out_specs=block,
        out_shape=jax.ShapeDtypeStruct((tok_rows, features), dtype),
        compiler_params=pltpu.CompilerParams(vmem_limit_bytes=VMEM_BYTES),
        cost_estimate=pl.CostEstimate(
            flops=2 * tok_rows * size * count * features,
            bytes_accessed=2 * count * size * (tok_rows + features) + 6 * tok_rows * features,
            transcendentals=0,
        ),
    )(*slots, weight, *given)


def shards(tokens, in_weight, conv_weight, spectrum, skip, out_weight):
    tok_rows, depth = tokens.shape
    seq_count = lax.axis_size("seq")
    chan_count = lax.axis_size("chan")
    chans = in_weight.shape[2]
    chunks = chunk_count(chans, seq_count)
    size = chans // chunks
    cut = tok_rows * 3 // 4
    early = slots_of(tokens[:cut], "chan")
    halo = gather_by_doubling(from_behind(tokens[tok_rows - HALO :], "seq", 1), "chan")
    late, *early[1:] = lax.optimization_barrier((tokens[cut:], *early[1:]))
    late = slots_of(late, "chan")
    halo = jnp.einsum(
        "ztd,pzdc->ptc",
        halo,
        in_weight.reshape(3, chan_count, depth, chans),
        preferred_element_type=jnp.float32,
    ).astype(jnp.bfloat16)
    response = folded_response(spectrum, seq_count, chunks)
    signal_a, *piece_a, tail = project(early, in_weight, conv_weight, halo)
    signal_b, *piece_b, _ = project(late, in_weight, conv_weight, tail, response)
    signal = jnp.concatenate([signal_a, signal_b], axis=1)
    signal, out_weight = lax.optimization_barrier((signal, out_weight))
    weight = feature_rows(out_weight, seq_count)
    gated = []
    for lo in range(0, chans, size):
        values = signal[lo : lo + size].reshape(seq_count, size // seq_count, tok_rows)
        values = lax.all_to_all(values, "seq", split_axis=0, concat_axis=0, tiled=True)
        longconv = lax.all_to_all(
            long_conv(values, response, lo // seq_count), "seq", split_axis=0, concat_axis=0, tiled=True
        ).reshape(size, tok_rows)
        gated.append(gate(longconv, skip, lo, (piece_a, piece_b)))
        if lo == 0:
            gated[0], weight = lax.optimization_barrier((gated[0], weight))
    slots = [slots_of(value, "chan") for value in gated]
    weight = gather_by_doubling(weight, "seq")
    total = None
    for j, lo in enumerate(range(0, chans, size)):
        dtype = jnp.bfloat16 if lo + size == chans else jnp.float32
        total = combine(slots[j], weight, lo, total, dtype)
    return total


def solution(mesh):
    placed = (
        P("seq", "chan"),
        P(None, None, "chan"),
        P(None, None, "chan"),
        P(None, "chan", "seq", None),
        P("chan"),
        P("chan", None),
    )
    return jax.shard_map(
        shards, mesh=mesh, in_specs=placed, out_specs=P("seq", "chan"), check_vma=False
    )
```

```python
import jax
import jax.numpy as jnp
import numpy as np
from jax import lax
from jax.experimental import pallas as pl
from jax.experimental.pallas import tpu as pltpu
from jax.sharding import PartitionSpec as P

TAPS = 3
LANES = 128
HALO = 16
DEPTH_STEP = 1024
CHAN_BLOCK = 16
CHUNKS = 2
VMEM_BYTES = 48 * 1024 * 1024


def from_behind(value, axis, by):
    size = lax.axis_size(axis)
    pairs = [(i, i + by) for i in range(size) if 0 <= i + by < size]
    return lax.ppermute(value, axis, pairs)


def shifted(value, axis, by):
    size = lax.axis_size(axis)
    return lax.ppermute(value, axis, [(i, (i + by) % size) for i in range(size)])


def gather_by_doubling(value, axis):
    size = lax.axis_size(axis)
    index = lax.axis_index(axis)
    held = value[None]
    bit = size // 2
    while bit >= 1:
        other = lax.ppermute(held, axis, [(i, i ^ bit) for i in range(size)])
        upper = (index // bit) % 2 == 1
        first = jnp.where(upper, other, held)
        second = jnp.where(upper, held, other)
        held = jnp.stack([first, second], axis=1).reshape((2 * held.shape[0],) + held.shape[1:])
        bit //= 2
    return held


def chunk_count(chans, seq_count):
    size = chans // CHUNKS
    return 1 if size % LANES or (size // seq_count) % CHAN_BLOCK else CHUNKS


def project_kernel(extras, tok_ref, w_ref, taps_ref, halo_ref, *rest):
    signal_ref, signal_t_ref, query_t_ref, acc = rest[extras:]
    step = pl.program_id(0)
    rows = signal_t_ref.shape[0]

    @pl.when(step == 0)
    def _():
        for p in range(3):
            acc[p, HALO:, :] = jnp.dot(tok_ref[...], w_ref[p], preferred_element_type=jnp.float32)

    @pl.when(step > 0)
    def _():
        for p in range(3):
            acc[p, HALO:, :] += jnp.dot(tok_ref[...], w_ref[p], preferred_element_type=jnp.float32)

    @pl.when(step == pl.num_programs(0) - 1)
    def _():
        for p in range(3):
            acc[p, :HALO, :] = halo_ref[p].astype(jnp.float32)
            acc[p, HALO:, :] = acc[p, HALO:, :].astype(jnp.bfloat16).astype(jnp.float32)
        for r in range(0, rows, LANES):
            streams = []
            for p in range(3):
                total = taps_ref[0, p][None, :] * acc[p, pl.ds(HALO + r, LANES), :]
                for j in range(1, TAPS):
                    total = total + taps_ref[j, p][None, :] * acc[p, pl.ds(HALO + r - j, LANES), :]
                streams.append(total)
            signal = streams[1] * streams[2]
            query_t_ref[r : r + LANES, :] = streams[0].astype(query_t_ref.dtype)
            signal_t_ref[r : r + LANES, :] = signal.astype(signal_t_ref.dtype)
            signal_ref[:, r : r + LANES] = signal.T.astype(signal_ref.dtype)


def project(gathered, in_weight, conv_weight, halo, lo, size, *after):
    rows, depth = gathered.shape
    step = min(DEPTH_STEP, depth)
    at = lo // size
    flat = jax.ShapeDtypeStruct((rows, size), jnp.bfloat16)
    return pl.pallas_call(
        lambda *refs: project_kernel(len(after), *refs),
        grid=(depth // step,),
        in_specs=[
            pl.BlockSpec((rows, step), lambda z: (0, z)),
            pl.BlockSpec((3, step, size), lambda z: (0, z, at)),
            pl.BlockSpec((TAPS, 3, size), lambda z: (0, 0, at)),
            pl.BlockSpec((3, HALO, size), lambda z: (0, 0, at)),
            *[pl.BlockSpec(memory_space=pl.ANY) for _ in after],
        ],
        out_specs=[
            pl.BlockSpec((size, rows), lambda z: (0, 0)),
            pl.BlockSpec((rows, size), lambda z: (0, 0)),
            pl.BlockSpec((rows, size), lambda z: (0, 0)),
        ],
        out_shape=[jax.ShapeDtypeStruct((size, rows), jnp.bfloat16), flat, flat],
        scratch_shapes=[pltpu.VMEM((3, HALO + rows, size), jnp.float32)],
        compiler_params=pltpu.CompilerParams(vmem_limit_bytes=VMEM_BYTES),
        cost_estimate=pl.CostEstimate(
            flops=2 * 3 * rows * depth * size,
            bytes_accessed=2 * depth * (3 * size + rows),
            transcendentals=0,
        ),
    )(gathered, in_weight, conv_weight, halo, *after)


def transform_tables(seq_count, tok_rows):
    runs = tok_rows // LANES
    wide = 2 * seq_count * runs
    fft_len = wide * LANES
    k1 = np.arange(seq_count + 1)[:, None]
    k2a = np.arange(runs)[None, :]
    ka = (k1 + 2 * seq_count * k2a).reshape(-1)
    a = np.arange(seq_count * runs)
    b = np.arange(LANES)
    outer = 2.0 * np.pi * ((ka[:, None] * a[None, :]) % wide) / wide
    first = np.concatenate([np.cos(outer), -np.sin(outer)], axis=0)
    last = first.T / fft_len
    turn = 2.0 * np.pi * ((ka[:, None] * b[None, :]) % fft_len) / fft_len
    inner = 2.0 * np.pi * ((b[:, None] * b[None, :]) % LANES) / LANES
    cos, sin = np.cos(inner), np.sin(inner)
    forward = np.block([[cos, -sin], [sin, cos]])
    backward = np.block([[cos, sin], [-sin, cos]])
    half = lambda table: jnp.asarray(table, jnp.bfloat16)
    full = lambda table: jnp.asarray(table, jnp.float32)
    return half(first), half(last), full(np.cos(turn)), full(np.sin(turn)), half(forward), half(backward)


def conv_kernel(signal_ref, resp_ref, first_ref, last_ref, cos_ref, sin_ref, fwd_ref, bwd_ref, out_ref, held, low, high):
    seq_count, block, tok_rows = signal_ref.shape
    runs = tok_rows // LANES
    span = seq_count * runs
    rows = cos_ref.shape[0]
    pair = 2 * rows
    for s in range(seq_count):
        for r in range(runs):
            piece = signal_ref[s, :, r * LANES : (r + 1) * LANES].astype(jnp.float32)
            held[pl.ds(s * runs + r, block, stride=span), :] = piece
    cos, sin = cos_ref[...], sin_ref[...]
    for c in range(0, block, 2):
        x = jnp.concatenate([held[c * span : (c + 1) * span, :], held[(c + 1) * span : (c + 2) * span, :]], axis=1)
        y = jnp.dot(first_ref[...], x.astype(jnp.bfloat16), preferred_element_type=jnp.float32)
        turned = []
        for half in (slice(0, LANES), slice(LANES, 2 * LANES)):
            re, im = y[:rows, half], y[rows:, half]
            turned.append(jnp.concatenate([re * cos + im * sin, im * cos - re * sin], axis=1))
        low[c * rows : c * rows + pair, :] = jnp.concatenate(turned, axis=0).astype(jnp.bfloat16)
    high[...] = jnp.dot(low[...], fwd_ref[...], preferred_element_type=jnp.float32)
    for c in range(0, block, 2):
        done = []
        for d in (c, c + 1):
            re = high[d * rows : (d + 1) * rows, :LANES]
            im = high[d * rows : (d + 1) * rows, LANES:]
            hr = resp_ref[0, d].astype(jnp.float32)
            hi = resp_ref[1, d].astype(jnp.float32)
            done.append(jnp.concatenate([re * hr - im * hi, re * hi + im * hr], axis=1))
        low[c * rows : c * rows + pair, :] = jnp.concatenate(done, axis=0).astype(jnp.bfloat16)
    high[...] = jnp.dot(low[...], bwd_ref[...], preferred_element_type=jnp.float32)
    for c in range(0, block, 2):
        turned = []
        for d in (c, c + 1):
            re = high[d * rows : (d + 1) * rows, :LANES]
            im = high[d * rows : (d + 1) * rows, LANES:]
            turned.append(jnp.concatenate([re * cos - im * sin, im * cos + re * sin], axis=0))
        w = jnp.concatenate(turned, axis=1).astype(jnp.bfloat16)
        y = jnp.dot(last_ref[...], w, preferred_element_type=jnp.float32)
        held[c * span : (c + 1) * span, :] = y[:, :LANES]
        held[(c + 1) * span : (c + 2) * span, :] = y[:, LANES:]
    for s in range(seq_count):
        for r in range(runs):
            piece = held[pl.ds(s * runs + r, block, stride=span), :]
            out_ref[s, :, r * LANES : (r + 1) * LANES] = piece.astype(out_ref.dtype)


def long_conv(values, response, start=0):
    seq_count, chans, tok_rows = values.shape
    rows = response.shape[2]
    block = min(CHAN_BLOCK, chans)
    tables = transform_tables(seq_count, tok_rows)
    fixed = [pl.BlockSpec(t.shape, lambda i: (0, 0)) for t in tables]
    span = seq_count * tok_rows // LANES
    flops = chans * 2 * (2 * 2 * rows * span * LANES + 2 * rows * 4 * LANES * LANES)
    moved = 2 * (2 * values.size + 2 * chans * rows * LANES)
    return pl.pallas_call(
        conv_kernel,
        grid=(chans // block,),
        in_specs=[
            pl.BlockSpec((seq_count, block, tok_rows), lambda i: (0, i, 0)),
            pl.BlockSpec((2, block, rows, LANES), lambda i: (0, start // block + i, 0, 0)),
            *fixed,
        ],
        out_specs=pl.BlockSpec((seq_count, block, tok_rows), lambda i: (0, i, 0)),
        out_shape=jax.ShapeDtypeStruct((seq_count, chans, tok_rows), jnp.bfloat16),
        scratch_shapes=[
            pltpu.VMEM((block * span, LANES), jnp.float32),
            pltpu.VMEM((block * rows, 2 * LANES), jnp.bfloat16),
            pltpu.VMEM((block * rows, 2 * LANES), jnp.float32),
        ],
        compiler_params=pltpu.CompilerParams(vmem_limit_bytes=VMEM_BYTES),
        cost_estimate=pl.CostEstimate(flops=flops, bytes_accessed=moved, transcendentals=0),
    )(values, response, *tables)


def gate_kernel(conv_ref, skip_ref, signal_ref, query_ref, out_ref):
    conv = conv_ref[...].astype(jnp.float32).T
    inner = conv + skip_ref[...] * signal_ref[...].astype(jnp.float32)
    out_ref[...] = (query_ref[...].astype(jnp.float32) * inner).astype(out_ref.dtype)


def gate(longconv, skip, lo, signal, query):
    chans, tok_rows = longconv.shape
    first = lo // LANES
    flat = pl.BlockSpec((tok_rows, LANES), lambda i: (0, i))
    return pl.pallas_call(
        gate_kernel,
        grid=(chans // LANES,),
        in_specs=[
            pl.BlockSpec((LANES, tok_rows), lambda i: (i, 0)),
            pl.BlockSpec((1, LANES), lambda i: (0, first + i)),
            flat,
            flat,
        ],
        out_specs=flat,
        out_shape=jax.ShapeDtypeStruct((tok_rows, chans), jnp.bfloat16),
        compiler_params=pltpu.CompilerParams(vmem_limit_bytes=VMEM_BYTES),
        cost_estimate=pl.CostEstimate(flops=4 * chans * tok_rows, bytes_accessed=8 * chans * tok_rows, transcendentals=0),
    )(longconv, skip[None, :], signal, query)


def reorder_kernel(spec_ref, order_ref, out_ref):
    each = out_ref.shape[3]
    x = spec_ref[0].astype(jnp.bfloat16)
    y = jnp.dot(x, order_ref[...], preferred_element_type=jnp.float32).astype(jnp.bfloat16)
    for d in range(out_ref.shape[0]):
        out_ref[d, 0, 0] = y[d * each : (d + 1) * each]


def fold_kernel(got_ref, out_ref, came, held):
    seq_count, pairs, tok_rows = got_ref.shape[0], got_ref.shape[3], got_ref.shape[4]
    chans = pairs // 2
    runs = tok_rows // LANES
    rows = (seq_count + 1) * runs
    for part in range(2):
        sign = 1.0 if part == 0 else -1.0
        for s in range(seq_count):
            for r in range(runs):
                at = (s * runs + r) * pairs
                lanes = slice(r * LANES, (r + 1) * LANES)
                came[at : at + pairs, :] = got_ref[s, part, 0, :, lanes].astype(jnp.float32)
        for k1 in range(seq_count + 1):
            other = 2 * seq_count - k1
            for r in range(runs):
                value = came[pl.ds((k1 // 2 * runs + r) * pairs + k1 % 2, chans, stride=2), :]
                if k1 == seq_count:
                    value = sign * value
                elif k1 > 0:
                    value = value + sign * came[pl.ds((other // 2 * runs + r) * pairs + other % 2, chans, stride=2), :]
                held[pl.ds(k1 * runs + r, chans, stride=rows), :] = value
        out_ref[part] = held[...].reshape(chans, rows, LANES).astype(out_ref.dtype)


def reordered_spectrum(spectrum, seq_count, chunks):
    parts, chans, own, tok_rows = spectrum.shape
    runs = tok_rows // LANES
    size = chans // chunks
    each = size // seq_count
    col = lax.broadcasted_iota(jnp.int32, (tok_rows, tok_rows), 1)
    row = lax.broadcasted_iota(jnp.int32, (tok_rows, tok_rows), 0)
    wanted = col // LANES + runs * (col % LANES)
    wanted = jnp.where(lax.axis_index("seq") >= seq_count // 2, tok_rows - 1 - wanted, wanted)
    order = (row == wanted).astype(jnp.bfloat16)
    shape = (seq_count, parts, chunks, own * each, tok_rows)
    return pl.pallas_call(
        reorder_kernel,
        grid=(parts, chunks),
        in_specs=[
            pl.BlockSpec((1, own * size, tok_rows), lambda p, j: (p, j, 0)),
            pl.BlockSpec((tok_rows, tok_rows), lambda p, j: (0, 0)),
        ],
        out_specs=pl.BlockSpec((seq_count, 1, 1, own * each, tok_rows), lambda p, j: (0, p, j, 0, 0)),
        out_shape=jax.ShapeDtypeStruct(shape, jnp.bfloat16),
        compiler_params=pltpu.CompilerParams(vmem_limit_bytes=VMEM_BYTES),
        cost_estimate=pl.CostEstimate(
            flops=2 * spectrum.size * tok_rows, bytes_accessed=6 * spectrum.size, transcendentals=0
        ),
    )(spectrum.reshape(parts, chans * own, tok_rows), order)


def folded_response(sent, own):
    seq_count, parts, chunks, pairs, tok_rows = sent.shape
    runs = tok_rows // LANES
    each = pairs // own
    got = lax.all_to_all(sent, "seq", split_axis=0, concat_axis=0, tiled=True)
    block = min(CHAN_BLOCK, each)
    rows = (seq_count + 1) * runs
    return pl.pallas_call(
        fold_kernel,
        grid=(chunks, each // block),
        in_specs=[pl.BlockSpec((seq_count, parts, 1, own * block, tok_rows), lambda j, i: (0, 0, j, i, 0))],
        out_specs=pl.BlockSpec((parts, block, rows, LANES), lambda j, i: (0, j * (each // block) + i, 0, 0)),
        out_shape=jax.ShapeDtypeStruct((parts, chunks * each, rows, LANES), jnp.bfloat16),
        scratch_shapes=[
            pltpu.VMEM((seq_count * runs * own * block, LANES), jnp.float32),
            pltpu.VMEM((block * rows, LANES), jnp.float32),
        ],
        compiler_params=pltpu.CompilerParams(vmem_limit_bytes=VMEM_BYTES),
        cost_estimate=pl.CostEstimate(flops=sent.size, bytes_accessed=3 * sent.size, transcendentals=0),
    )(got)


def feature_rows(out_weight, seq_count):
    each = out_weight.shape[0] // seq_count
    own = lax.dynamic_slice_in_dim(out_weight, lax.axis_index("seq") * each, each, axis=0)
    count = lax.axis_size("chan")
    me = lax.axis_index("chan")
    wide = out_weight.shape[1] // count
    pieces = []
    for by in range(count):
        piece = lax.dynamic_slice_in_dim(own, lax.rem(me + by, count) * wide, wide, axis=1)
        pieces.append(shifted(piece, "chan", by) if by else piece)
    return jnp.stack(pieces)


def combine_kernel(slots, me_ref, *refs):
    total_ref = refs[slots + 1] if len(refs) == slots + 3 else None
    w_ref, out_ref = refs[slots], refs[-1]
    total = None if total_ref is None else total_ref[...]
    for z in range(slots):
        weight = w_ref[:, z].reshape(refs[z].shape[1], out_ref.shape[1])
        term = jnp.dot(refs[z][...], weight, preferred_element_type=jnp.float32)
        total = term if total is None else total + term
    out_ref[...] = total.astype(out_ref.dtype)


def combine(gathered, weight, lo, total, dtype):
    tok_rows = gathered.shape[0]
    _, count, each, features = weight.shape
    size = gathered.shape[1] // count
    per = size // each
    first = lo // size
    tile = min(2 * LANES, features)
    block = pl.BlockSpec((tok_rows, tile), lambda i, me: (0, i))
    given = [] if total is None else [total]
    me = lax.axis_index("chan").astype(jnp.int32).reshape(1)

    def slot(k):
        return pl.BlockSpec((tok_rows, size), lambda i, me: (0, lax.rem(me[0] - k + count, count)))

    return pl.pallas_call(
        lambda *refs: combine_kernel(count, *refs),
        grid_spec=pltpu.PrefetchScalarGridSpec(
            num_scalar_prefetch=1,
            grid=(features // tile,),
            in_specs=[
                *[slot(k) for k in range(count)],
                pl.BlockSpec((per, count, each, tile), lambda i, me: (first, 0, 0, i)),
                *[block for _ in given],
            ],
            out_specs=block,
        ),
        out_shape=jax.ShapeDtypeStruct((tok_rows, features), dtype),
        compiler_params=pltpu.CompilerParams(vmem_limit_bytes=VMEM_BYTES),
        cost_estimate=pl.CostEstimate(
            flops=2 * tok_rows * size * count * features,
            bytes_accessed=2 * count * size * (tok_rows + features) + 6 * tok_rows * features,
            transcendentals=0,
        ),
    )(me, *[gathered] * count, weight, *given)


def shards(tokens, in_weight, conv_weight, spectrum, skip, out_weight):
    tok_rows, depth = tokens.shape
    seq_count = lax.axis_size("seq")
    chan_count = lax.axis_size("chan")
    chans = in_weight.shape[2]
    chunks = chunk_count(chans, seq_count)
    size = chans // chunks
    gathered = lax.all_gather(tokens, "chan", axis=1, tiled=True)
    halo = gather_by_doubling(from_behind(tokens[tok_rows - HALO :], "seq", 1), "chan")
    sent = reordered_spectrum(spectrum, seq_count, chunks)
    halo, sent, out_weight = lax.optimization_barrier((halo, sent, out_weight))
    response = folded_response(sent, spectrum.shape[2])
    weight = gather_by_doubling(feature_rows(out_weight, seq_count), "seq")
    halo = jnp.einsum(
        "ztd,pzdc->ptc",
        halo,
        in_weight.reshape(3, chan_count, depth, chans),
        preferred_element_type=jnp.float32,
    ).astype(jnp.bfloat16)
    total = None
    for lo in range(0, chans, size):
        signal, signal_t, query_t = project(
            gathered, in_weight, conv_weight, halo, lo, size, response, weight
        )
        values = signal.reshape(seq_count, size // seq_count, tok_rows)
        values = lax.all_to_all(values, "seq", split_axis=0, concat_axis=0, tiled=True)
        longconv = lax.all_to_all(
            long_conv(values, response, lo // seq_count), "seq", split_axis=0, concat_axis=0, tiled=True
        ).reshape(size, tok_rows)
        gated = lax.all_gather(gate(longconv, skip, lo, signal_t, query_t), "chan", axis=1, tiled=True)
        dtype = jnp.bfloat16 if lo + size == chans else jnp.float32
        total = combine(gated, weight, lo, total, dtype)
    return total


def solution(mesh):
    placed = (
        P("seq", "chan"),
        P(None, None, "chan"),
        P(None, None, "chan"),
        P(None, "chan", "seq", None),
        P("chan"),
        P("chan", None),
    )
    return jax.shard_map(
        shards, mesh=mesh, in_specs=placed, out_specs=P("seq", "chan"), check_vma=False
    )
```

```python
import jax
import jax.numpy as jnp
import numpy as np
from jax import lax
from jax.experimental import pallas as pl
from jax.experimental.pallas import tpu as pltpu
from jax.sharding import PartitionSpec as P

TAPS = 3
LANES = 128
HALO = 16
DEPTH_STEP = 1024
CHAN_BLOCK = 16
CHUNKS = 2
VMEM_BYTES = 48 * 1024 * 1024


def from_behind(value, axis, by):
    size = lax.axis_size(axis)
    pairs = [(i, i + by) for i in range(size) if 0 <= i + by < size]
    return lax.ppermute(value, axis, pairs)


def gather_by_doubling(value, axis):
    size = lax.axis_size(axis)
    index = lax.axis_index(axis)
    held = value[None]
    bit = size // 2
    while bit >= 1:
        other = lax.ppermute(held, axis, [(i, i ^ bit) for i in range(size)])
        upper = (index // bit) % 2 == 1
        first = jnp.where(upper, other, held)
        second = jnp.where(upper, held, other)
        held = jnp.stack([first, second], axis=1).reshape((2 * held.shape[0],) + held.shape[1:])
        bit //= 2
    return held


def chunk_count(chans, seq_count):
    size = chans // CHUNKS
    return 1 if size % LANES or (size // seq_count) % CHAN_BLOCK else CHUNKS


def project_kernel(streams, extras, tok_ref, *refs):
    w_refs, taps_ref, halo_ref = refs[: len(streams)], refs[len(streams)], refs[len(streams) + 1]
    outs, acc = refs[len(streams) + 2 + extras : -1], refs[-1]
    step = pl.program_id(0)
    last = pl.num_programs(0) - 1
    rows = acc.shape[1] - HALO

    def part(w_ref):
        return jnp.dot(tok_ref[...], w_ref[0], preferred_element_type=jnp.float32)

    @pl.when(step == 0)
    def _():
        for i, p in enumerate(streams):
            acc[i, :HALO, :] = halo_ref[p].astype(jnp.float32)
            acc[i, HALO:, :] = part(w_refs[i])

    @pl.when(jnp.logical_and(step > 0, step < last))
    def _():
        for i in range(len(streams)):
            acc[i, HALO:, :] += part(w_refs[i])

    @pl.when(step == last)
    def _():
        for i in range(len(streams)):
            acc[i, HALO:, :] = (acc[i, HALO:, :] + part(w_refs[i])).astype(jnp.bfloat16).astype(jnp.float32)
        for r in range(0, rows, LANES):
            made = {}
            for i, p in enumerate(streams):
                total = taps_ref[0, p][None, :] * acc[i, pl.ds(HALO + r, LANES), :]
                for j in range(1, TAPS):
                    total = total + taps_ref[j, p][None, :] * acc[i, pl.ds(HALO + r - j, LANES), :]
                made[p] = total
            if 0 in made:
                outs[0][r : r + LANES, :] = made[0].astype(outs[0].dtype)
            if 1 in made:
                signal = made[1] * made[2]
                outs[-1][r : r + LANES, :] = signal.astype(outs[-1].dtype)
                outs[-2][:, r : r + LANES] = signal.T.astype(outs[-2].dtype)


def project(streams, gathered, in_weight, conv_weight, halo, lo, size, *after):
    rows, depth = gathered.shape
    step = min(DEPTH_STEP, depth // 2)
    at = lo // size
    flat = jax.ShapeDtypeStruct((rows, size), jnp.bfloat16)
    shapes = ([flat] if 0 in streams else []) + (
        [jax.ShapeDtypeStruct((size, rows), jnp.bfloat16), flat] if 1 in streams else []
    )

    def weight_of(p):
        return pl.BlockSpec((1, step, size), lambda z: (p, z, at))

    return pl.pallas_call(
        lambda *refs: project_kernel(streams, len(after), *refs),
        grid=(depth // step,),
        in_specs=[
            pl.BlockSpec((rows, step), lambda z: (0, z)),
            *[weight_of(p) for p in streams],
            pl.BlockSpec((TAPS, 3, size), lambda z: (0, 0, at)),
            pl.BlockSpec((3, HALO, size), lambda z: (0, 0, at)),
            *[pl.BlockSpec(memory_space=pl.ANY) for _ in after],
        ],
        out_specs=[pl.BlockSpec(shape.shape, lambda z: (0, 0)) for shape in shapes],
        out_shape=shapes,
        scratch_shapes=[pltpu.VMEM((len(streams), HALO + rows, size), jnp.float32)],
        compiler_params=pltpu.CompilerParams(vmem_limit_bytes=VMEM_BYTES),
        cost_estimate=pl.CostEstimate(
            flops=2 * len(streams) * rows * depth * size,
            bytes_accessed=2 * depth * (len(streams) * size + rows),
            transcendentals=0,
        ),
    )(gathered, *[in_weight] * len(streams), conv_weight, halo, *after)


def transform_tables(seq_count, tok_rows):
    runs = tok_rows // LANES
    wide = 2 * seq_count * runs
    fft_len = wide * LANES
    k1 = np.arange(seq_count + 1)[:, None]
    k2a = np.arange(runs)[None, :]
    ka = (k1 + 2 * seq_count * k2a).reshape(-1)
    a = np.arange(seq_count * runs)
    b = np.arange(LANES)
    outer = 2.0 * np.pi * ((ka[:, None] * a[None, :]) % wide) / wide
    first = np.concatenate([np.cos(outer), -np.sin(outer)], axis=0)
    last = first.T / fft_len
    turn = 2.0 * np.pi * ((ka[:, None] * b[None, :]) % fft_len) / fft_len
    inner = 2.0 * np.pi * ((b[:, None] * b[None, :]) % LANES) / LANES
    cos, sin = np.cos(inner), np.sin(inner)
    forward = np.block([[cos, -sin], [sin, cos]])
    backward = np.block([[cos, sin], [-sin, cos]])
    half = lambda table: jnp.asarray(table, jnp.bfloat16)
    full = lambda table: jnp.asarray(table, jnp.float32)
    return half(first), half(last), full(np.cos(turn)), full(np.sin(turn)), half(forward), half(backward)


def conv_kernel(signal_ref, resp_ref, first_ref, last_ref, cos_ref, sin_ref, fwd_ref, bwd_ref, out_ref, held, low, high):
    seq_count, block, tok_rows = signal_ref.shape
    runs = tok_rows // LANES
    span = seq_count * runs
    rows = cos_ref.shape[0]
    pair = 2 * rows
    for s in range(seq_count):
        for r in range(runs):
            piece = signal_ref[s, :, r * LANES : (r + 1) * LANES].astype(jnp.float32)
            held[pl.ds(s * runs + r, block, stride=span), :] = piece
    cos, sin = cos_ref[...], sin_ref[...]
    for c in range(0, block, 2):
        x = jnp.concatenate([held[c * span : (c + 1) * span, :], held[(c + 1) * span : (c + 2) * span, :]], axis=1)
        y = jnp.dot(first_ref[...], x.astype(jnp.bfloat16), preferred_element_type=jnp.float32)
        turned = []
        for half in (slice(0, LANES), slice(LANES, 2 * LANES)):
            re, im = y[:rows, half], y[rows:, half]
            turned.append(jnp.concatenate([re * cos + im * sin, im * cos - re * sin], axis=1))
        low[c * rows : c * rows + pair, :] = jnp.concatenate(turned, axis=0).astype(jnp.bfloat16)
    high[...] = jnp.dot(low[...], fwd_ref[...], preferred_element_type=jnp.float32)
    for c in range(0, block, 2):
        done = []
        for d in (c, c + 1):
            re = high[d * rows : (d + 1) * rows, :LANES]
            im = high[d * rows : (d + 1) * rows, LANES:]
            hr = resp_ref[0, d].astype(jnp.float32)
            hi = resp_ref[1, d].astype(jnp.float32)
            done.append(jnp.concatenate([re * hr - im * hi, re * hi + im * hr], axis=1))
        low[c * rows : c * rows + pair, :] = jnp.concatenate(done, axis=0).astype(jnp.bfloat16)
    high[...] = jnp.dot(low[...], bwd_ref[...], preferred_element_type=jnp.float32)
    for c in range(0, block, 2):
        turned = []
        for d in (c, c + 1):
            re = high[d * rows : (d + 1) * rows, :LANES]
            im = high[d * rows : (d + 1) * rows, LANES:]
            turned.append(jnp.concatenate([re * cos - im * sin, im * cos + re * sin], axis=0))
        w = jnp.concatenate(turned, axis=1).astype(jnp.bfloat16)
        y = jnp.dot(last_ref[...], w, preferred_element_type=jnp.float32)
        held[c * span : (c + 1) * span, :] = y[:, :LANES]
        held[(c + 1) * span : (c + 2) * span, :] = y[:, LANES:]
    for s in range(seq_count):
        for r in range(runs):
            piece = held[pl.ds(s * runs + r, block, stride=span), :]
            out_ref[s, :, r * LANES : (r + 1) * LANES] = piece.astype(out_ref.dtype)


def long_conv(values, response, start=0):
    seq_count, chans, tok_rows = values.shape
    rows = response.shape[2]
    block = min(CHAN_BLOCK, chans)
    tables = transform_tables(seq_count, tok_rows)
    fixed = [pl.BlockSpec(t.shape, lambda i: (0, 0)) for t in tables]
    span = seq_count * tok_rows // LANES
    flops = chans * 2 * (2 * 2 * rows * span * LANES + 2 * rows * 4 * LANES * LANES)
    moved = 2 * (2 * values.size + 2 * chans * rows * LANES)
    return pl.pallas_call(
        conv_kernel,
        grid=(chans // block,),
        in_specs=[
            pl.BlockSpec((seq_count, block, tok_rows), lambda i: (0, i, 0)),
            pl.BlockSpec((2, block, rows, LANES), lambda i: (0, start // block + i, 0, 0)),
            *fixed,
        ],
        out_specs=pl.BlockSpec((seq_count, block, tok_rows), lambda i: (0, i, 0)),
        out_shape=jax.ShapeDtypeStruct((seq_count, chans, tok_rows), jnp.bfloat16),
        scratch_shapes=[
            pltpu.VMEM((block * span, LANES), jnp.float32),
            pltpu.VMEM((block * rows, 2 * LANES), jnp.bfloat16),
            pltpu.VMEM((block * rows, 2 * LANES), jnp.float32),
        ],
        compiler_params=pltpu.CompilerParams(vmem_limit_bytes=VMEM_BYTES),
        cost_estimate=pl.CostEstimate(flops=flops, bytes_accessed=moved, transcendentals=0),
    )(values, response, *tables)


def gate_kernel(conv_ref, skip_ref, signal_ref, query_ref, out_ref):
    conv = conv_ref[...].astype(jnp.float32).T
    inner = conv + skip_ref[...] * signal_ref[...].astype(jnp.float32)
    out_ref[...] = (query_ref[...].astype(jnp.float32) * inner).astype(out_ref.dtype)


def gate(longconv, skip, lo, signal, query):
    chans, tok_rows = longconv.shape
    first = lo // LANES
    flat = pl.BlockSpec((tok_rows, LANES), lambda i: (0, i))
    return pl.pallas_call(
        gate_kernel,
        grid=(chans // LANES,),
        in_specs=[
            pl.BlockSpec((LANES, tok_rows), lambda i: (i, 0)),
            pl.BlockSpec((1, LANES), lambda i: (0, first + i)),
            flat,
            flat,
        ],
        out_specs=flat,
        out_shape=jax.ShapeDtypeStruct((tok_rows, chans), jnp.bfloat16),
        compiler_params=pltpu.CompilerParams(vmem_limit_bytes=VMEM_BYTES),
        cost_estimate=pl.CostEstimate(flops=4 * chans * tok_rows, bytes_accessed=8 * chans * tok_rows, transcendentals=0),
    )(longconv, skip[None, :], signal, query)


def reorder_kernel(spec_ref, order_ref, out_ref):
    each = out_ref.shape[3]
    x = spec_ref[0].astype(jnp.bfloat16)
    y = jnp.dot(x, order_ref[...], preferred_element_type=jnp.float32).astype(jnp.bfloat16)
    for d in range(out_ref.shape[0]):
        out_ref[d, 0, 0] = y[d * each : (d + 1) * each]


def fold_kernel(got_ref, out_ref, came, held):
    seq_count, pairs, tok_rows = got_ref.shape[0], got_ref.shape[3], got_ref.shape[4]
    chans = pairs // 2
    runs = tok_rows // LANES
    rows = (seq_count + 1) * runs
    for part in range(2):
        sign = 1.0 if part == 0 else -1.0
        for s in range(seq_count):
            for r in range(runs):
                at = (s * runs + r) * pairs
                lanes = slice(r * LANES, (r + 1) * LANES)
                came[at : at + pairs, :] = got_ref[s, part, 0, :, lanes].astype(jnp.float32)
        for k1 in range(seq_count + 1):
            other = 2 * seq_count - k1
            for r in range(runs):
                value = came[pl.ds((k1 // 2 * runs + r) * pairs + k1 % 2, chans, stride=2), :]
                if k1 == seq_count:
                    value = sign * value
                elif k1 > 0:
                    value = value + sign * came[pl.ds((other // 2 * runs + r) * pairs + other % 2, chans, stride=2), :]
                held[pl.ds(k1 * runs + r, chans, stride=rows), :] = value
        out_ref[part] = held[...].reshape(chans, rows, LANES).astype(out_ref.dtype)


def reordered_spectrum(spectrum, seq_count, chunks):
    parts, chans, own, tok_rows = spectrum.shape
    runs = tok_rows // LANES
    size = chans // chunks
    each = size // seq_count
    col = lax.broadcasted_iota(jnp.int32, (tok_rows, tok_rows), 1)
    row = lax.broadcasted_iota(jnp.int32, (tok_rows, tok_rows), 0)
    wanted = col // LANES + runs * (col % LANES)
    wanted = jnp.where(lax.axis_index("seq") >= seq_count // 2, tok_rows - 1 - wanted, wanted)
    order = (row == wanted).astype(jnp.bfloat16)
    shape = (seq_count, parts, chunks, own * each, tok_rows)
    return pl.pallas_call(
        reorder_kernel,
        grid=(parts, chunks),
        in_specs=[
            pl.BlockSpec((1, own * size, tok_rows), lambda p, j: (p, j, 0)),
            pl.BlockSpec((tok_rows, tok_rows), lambda p, j: (0, 0)),
        ],
        out_specs=pl.BlockSpec((seq_count, 1, 1, own * each, tok_rows), lambda p, j: (0, p, j, 0, 0)),
        out_shape=jax.ShapeDtypeStruct(shape, jnp.bfloat16),
        compiler_params=pltpu.CompilerParams(vmem_limit_bytes=VMEM_BYTES),
        cost_estimate=pl.CostEstimate(
            flops=2 * spectrum.size * tok_rows, bytes_accessed=6 * spectrum.size, transcendentals=0
        ),
    )(spectrum.reshape(parts, chans * own, tok_rows), order)


def folded_response(sent, own):
    seq_count, parts, chunks, pairs, tok_rows = sent.shape
    runs = tok_rows // LANES
    each = pairs // own
    got = lax.all_to_all(sent, "seq", split_axis=0, concat_axis=0, tiled=True)
    block = min(CHAN_BLOCK, each)
    rows = (seq_count + 1) * runs
    return pl.pallas_call(
        fold_kernel,
        grid=(chunks, each // block),
        in_specs=[pl.BlockSpec((seq_count, parts, 1, own * block, tok_rows), lambda j, i: (0, 0, j, i, 0))],
        out_specs=pl.BlockSpec((parts, block, rows, LANES), lambda j, i: (0, j * (each // block) + i, 0, 0)),
        out_shape=jax.ShapeDtypeStruct((parts, chunks * each, rows, LANES), jnp.bfloat16),
        scratch_shapes=[
            pltpu.VMEM((seq_count * runs * own * block, LANES), jnp.float32),
            pltpu.VMEM((block * rows, LANES), jnp.float32),
        ],
        compiler_params=pltpu.CompilerParams(vmem_limit_bytes=VMEM_BYTES),
        cost_estimate=pl.CostEstimate(flops=sent.size, bytes_accessed=3 * sent.size, transcendentals=0),
    )(got)


def feature_slice(out_weight, seq_count):
    each = out_weight.shape[0] // seq_count
    own = lax.dynamic_slice_in_dim(out_weight, lax.axis_index("seq") * each, each, axis=0)
    own = lax.all_to_all(own, "chan", split_axis=1, concat_axis=0, tiled=True)
    return gather_by_doubling(own.reshape(lax.axis_size("chan"), each, own.shape[1]), "seq")


def combine_kernel(gated_ref, w_ref, *refs):
    out_ref = refs[-1]
    per, count, each, tile = w_ref.shape
    weight = jnp.concatenate([w_ref[:, z].reshape(per * each, tile) for z in range(count)], axis=0)
    total = jnp.dot(gated_ref[...], weight, preferred_element_type=jnp.float32)
    if len(refs) == 2:
        total = total + refs[0][...]
    out_ref[...] = total.astype(out_ref.dtype)


def combine(gathered, weight, lo, total, dtype):
    tok_rows, depth = gathered.shape
    _, count, each, features = weight.shape
    size = depth // count
    per = size // each
    first = lo // size
    tile = min(2 * LANES, features)
    block = pl.BlockSpec((tok_rows, tile), lambda i: (0, i))
    given = [] if total is None else [total]
    return pl.pallas_call(
        combine_kernel,
        grid=(features // tile,),
        in_specs=[
            pl.BlockSpec((tok_rows, depth), lambda i: (0, 0)),
            pl.BlockSpec((per, count, each, tile), lambda i: (first, 0, 0, i)),
            *[block for _ in given],
        ],
        out_specs=block,
        out_shape=jax.ShapeDtypeStruct((tok_rows, features), dtype),
        compiler_params=pltpu.CompilerParams(vmem_limit_bytes=VMEM_BYTES),
        cost_estimate=pl.CostEstimate(
            flops=2 * tok_rows * depth * features,
            bytes_accessed=2 * depth * (tok_rows + features) + 6 * tok_rows * features,
            transcendentals=0,
        ),
    )(gathered, weight, *given)


def shards(tokens, in_weight, conv_weight, spectrum, skip, out_weight):
    tok_rows, depth = tokens.shape
    seq_count = lax.axis_size("seq")
    chan_count = lax.axis_size("chan")
    chans = in_weight.shape[2]
    chunks = chunk_count(chans, seq_count)
    size = chans // chunks
    gathered = lax.all_gather(tokens, "chan", axis=1, tiled=True)
    halo = gather_by_doubling(from_behind(tokens[tok_rows - HALO :], "seq", 1), "chan")
    sent = reordered_spectrum(spectrum, seq_count, chunks)
    halo, sent, out_weight = lax.optimization_barrier((halo, sent, out_weight))
    response = folded_response(sent, spectrum.shape[2])
    weight = feature_slice(out_weight, seq_count)
    halo = jnp.einsum(
        "ztd,pzdc->ptc",
        halo,
        in_weight.reshape(3, chan_count, depth, chans),
        preferred_element_type=jnp.float32,
    ).astype(jnp.bfloat16)
    total = None
    for lo in range(0, chans, size):
        given = (gathered, in_weight, conv_weight, halo, lo, size, response, weight)
        if lo == 0:
            signal, signal_t = project((1, 2), *given)
            (query_t,) = project((0,), *given)
        else:
            query_t, signal, signal_t = project((0, 1, 2), *given)
        values = signal.reshape(seq_count, size // seq_count, tok_rows)
        values = lax.all_to_all(values, "seq", split_axis=0, concat_axis=0, tiled=True)
        longconv = lax.all_to_all(
            long_conv(values, response, lo // seq_count), "seq", split_axis=0, concat_axis=0, tiled=True
        ).reshape(size, tok_rows)
        gated = lax.all_gather(gate(longconv, skip, lo, signal_t, query_t), "chan", axis=1, tiled=True)
        dtype = jnp.bfloat16 if lo + size == chans else jnp.float32
        total = combine(gated, weight, lo, total, dtype)
    return total


def solution(mesh):
    placed = (
        P("seq", "chan"),
        P(None, None, "chan"),
        P(None, None, "chan"),
        P(None, "chan", "seq", None),
        P("chan"),
        P("chan", None),
    )
    return jax.shard_map(
        shards, mesh=mesh, in_specs=placed, out_specs=P("seq", "chan"), check_vma=False
    )
```

```python
import jax
import jax.numpy as jnp
import numpy as np
from jax import lax
from jax.experimental import pallas as pl
from jax.experimental.pallas import tpu as pltpu
from jax.sharding import PartitionSpec as P

TAPS = 3
LANES = 128
HALO = 16
DEPTH_STEP = 1024
CHAN_BLOCK = 16
CHUNKS = 2
VMEM_BYTES = 60 * 1024 * 1024


def from_behind(value, axis, by):
    size = lax.axis_size(axis)
    pairs = [(i, i + by) for i in range(size) if 0 <= i + by < size]
    return lax.ppermute(value, axis, pairs)


def gather_by_doubling(value, axis):
    size = lax.axis_size(axis)
    index = lax.axis_index(axis)
    held = value[None]
    bit = size // 2
    while bit >= 1:
        other = lax.ppermute(held, axis, [(i, i ^ bit) for i in range(size)])
        upper = (index // bit) % 2 == 1
        first = jnp.where(upper, other, held)
        second = jnp.where(upper, held, other)
        held = jnp.stack([first, second], axis=1).reshape((2 * held.shape[0],) + held.shape[1:])
        bit //= 2
    return held


def chunk_count(chans, seq_count):
    size = chans // CHUNKS
    return 1 if size % LANES or (size // seq_count) % CHAN_BLOCK else CHUNKS


def project_kernel(streams, extras, tok_ref, *refs):
    w_refs, taps_ref, halo_ref = refs[: len(streams)], refs[len(streams)], refs[len(streams) + 1]
    outs, acc = refs[len(streams) + 2 + extras : -1], refs[-1]
    step = pl.program_id(0)
    last = pl.num_programs(0) - 1
    rows = acc.shape[1] - HALO

    def part(w_ref):
        return jnp.dot(tok_ref[...], w_ref[0], preferred_element_type=jnp.float32)

    @pl.when(step == 0)
    def _():
        for i, p in enumerate(streams):
            acc[i, :HALO, :] = halo_ref[p].astype(jnp.float32)
            acc[i, HALO:, :] = part(w_refs[i])

    @pl.when(jnp.logical_and(step > 0, step < last))
    def _():
        for i in range(len(streams)):
            acc[i, HALO:, :] += part(w_refs[i])

    @pl.when(step == last)
    def _():
        for i in range(len(streams)):
            acc[i, HALO:, :] = (acc[i, HALO:, :] + part(w_refs[i])).astype(jnp.bfloat16).astype(jnp.float32)
        for r in range(0, rows, LANES):
            made = {}
            for i, p in enumerate(streams):
                total = taps_ref[0, p][None, :] * acc[i, pl.ds(HALO + r, LANES), :]
                for j in range(1, TAPS):
                    total = total + taps_ref[j, p][None, :] * acc[i, pl.ds(HALO + r - j, LANES), :]
                made[p] = total
            if 0 in made:
                outs[0][r : r + LANES, :] = made[0].astype(outs[0].dtype)
            if 1 in made:
                signal = made[1] * made[2]
                outs[-1][r : r + LANES, :] = signal.astype(outs[-1].dtype)
                outs[-2][:, r : r + LANES] = signal.T.astype(outs[-2].dtype)


def project(streams, gathered, in_weight, conv_weight, halo, lo, size, *after):
    rows, depth = gathered.shape
    step = min(DEPTH_STEP, depth // 2)
    at = lo // size
    flat = jax.ShapeDtypeStruct((rows, size), jnp.bfloat16)
    shapes = ([flat] if 0 in streams else []) + (
        [jax.ShapeDtypeStruct((size, rows), jnp.bfloat16), flat] if 1 in streams else []
    )

    def weight_of(p):
        return pl.BlockSpec((1, step, size), lambda z: (p, z, at))

    return pl.pallas_call(
        lambda *refs: project_kernel(streams, len(after), *refs),
        grid=(depth // step,),
        in_specs=[
            pl.BlockSpec((rows, step), lambda z: (0, z)),
            *[weight_of(p) for p in streams],
            pl.BlockSpec((TAPS, 3, size), lambda z: (0, 0, at)),
            pl.BlockSpec((3, HALO, size), lambda z: (0, 0, at)),
            *[pl.BlockSpec(memory_space=pl.ANY) for _ in after],
        ],
        out_specs=[pl.BlockSpec(shape.shape, lambda z: (0, 0)) for shape in shapes],
        out_shape=shapes,
        scratch_shapes=[pltpu.VMEM((len(streams), HALO + rows, size), jnp.float32)],
        compiler_params=pltpu.CompilerParams(vmem_limit_bytes=VMEM_BYTES),
        cost_estimate=pl.CostEstimate(
            flops=2 * len(streams) * rows * depth * size,
            bytes_accessed=2 * depth * (len(streams) * size + rows),
            transcendentals=0,
        ),
    )(gathered, *[in_weight] * len(streams), conv_weight, halo, *after)


def transform_tables(seq_count, tok_rows):
    runs = tok_rows // LANES
    wide = 2 * seq_count * runs
    fft_len = wide * LANES
    k1 = np.arange(seq_count + 1)[:, None]
    k2a = np.arange(runs)[None, :]
    ka = (k1 + 2 * seq_count * k2a).reshape(-1)
    a = np.arange(seq_count * runs)
    b = np.arange(LANES)
    outer = 2.0 * np.pi * ((ka[:, None] * a[None, :]) % wide) / wide
    first = np.concatenate([np.cos(outer), -np.sin(outer)], axis=0)
    last = first.T / fft_len
    turn = 2.0 * np.pi * ((ka[:, None] * b[None, :]) % fft_len) / fft_len
    inner = 2.0 * np.pi * ((b[:, None] * b[None, :]) % LANES) / LANES
    cos, sin = np.cos(inner), np.sin(inner)
    forward = np.block([[cos, -sin], [sin, cos]])
    backward = np.block([[cos, sin], [-sin, cos]])
    half = lambda table: jnp.asarray(table, jnp.bfloat16)
    full = lambda table: jnp.asarray(table, jnp.float32)
    return half(first), half(last), full(np.cos(turn)), full(np.sin(turn)), half(forward), half(backward)


def conv_kernel(signal_ref, resp_ref, first_ref, last_ref, cos_ref, sin_ref, fwd_ref, bwd_ref, out_ref, held, low, high):
    seq_count, block, tok_rows = signal_ref.shape
    runs = tok_rows // LANES
    span = seq_count * runs
    rows = cos_ref.shape[0]
    pair = 2 * rows
    for s in range(seq_count):
        for r in range(runs):
            piece = signal_ref[s, :, r * LANES : (r + 1) * LANES].astype(jnp.float32)
            held[pl.ds(s * runs + r, block, stride=span), :] = piece
    cos, sin = cos_ref[...], sin_ref[...]
    for c in range(0, block, 2):
        x = jnp.concatenate([held[c * span : (c + 1) * span, :], held[(c + 1) * span : (c + 2) * span, :]], axis=1)
        y = jnp.dot(first_ref[...], x.astype(jnp.bfloat16), preferred_element_type=jnp.float32)
        turned = []
        for half in (slice(0, LANES), slice(LANES, 2 * LANES)):
            re, im = y[:rows, half], y[rows:, half]
            turned.append(jnp.concatenate([re * cos + im * sin, im * cos - re * sin], axis=1))
        low[c * rows : c * rows + pair, :] = jnp.concatenate(turned, axis=0).astype(jnp.bfloat16)
    high[...] = jnp.dot(low[...], fwd_ref[...], preferred_element_type=jnp.float32)
    for c in range(0, block, 2):
        done = []
        for d in (c, c + 1):
            re = high[d * rows : (d + 1) * rows, :LANES]
            im = high[d * rows : (d + 1) * rows, LANES:]
            hr = resp_ref[0, d].astype(jnp.float32)
            hi = resp_ref[1, d].astype(jnp.float32)
            done.append(jnp.concatenate([re * hr - im * hi, re * hi + im * hr], axis=1))
        low[c * rows : c * rows + pair, :] = jnp.concatenate(done, axis=0).astype(jnp.bfloat16)
    high[...] = jnp.dot(low[...], bwd_ref[...], preferred_element_type=jnp.float32)
    for c in range(0, block, 2):
        turned = []
        for d in (c, c + 1):
            re = high[d * rows : (d + 1) * rows, :LANES]
            im = high[d * rows : (d + 1) * rows, LANES:]
            turned.append(jnp.concatenate([re * cos - im * sin, im * cos + re * sin], axis=0))
        w = jnp.concatenate(turned, axis=1).astype(jnp.bfloat16)
        y = jnp.dot(last_ref[...], w, preferred_element_type=jnp.float32)
        held[c * span : (c + 1) * span, :] = y[:, :LANES]
        held[(c + 1) * span : (c + 2) * span, :] = y[:, LANES:]
    for s in range(seq_count):
        for r in range(runs):
            piece = held[pl.ds(s * runs + r, block, stride=span), :]
            out_ref[s, :, r * LANES : (r + 1) * LANES] = piece.astype(out_ref.dtype)


def long_conv(values, response, start=0):
    seq_count, chans, tok_rows = values.shape
    rows = response.shape[2]
    block = min(CHAN_BLOCK, chans)
    tables = transform_tables(seq_count, tok_rows)
    fixed = [pl.BlockSpec(t.shape, lambda i: (0, 0)) for t in tables]
    span = seq_count * tok_rows // LANES
    flops = chans * 2 * (2 * 2 * rows * span * LANES + 2 * rows * 4 * LANES * LANES)
    moved = 2 * (2 * values.size + 2 * chans * rows * LANES)
    return pl.pallas_call(
        conv_kernel,
        grid=(chans // block,),
        in_specs=[
            pl.BlockSpec((seq_count, block, tok_rows), lambda i: (0, i, 0)),
            pl.BlockSpec((2, block, rows, LANES), lambda i: (0, start // block + i, 0, 0)),
            *fixed,
        ],
        out_specs=pl.BlockSpec((seq_count, block, tok_rows), lambda i: (0, i, 0)),
        out_shape=jax.ShapeDtypeStruct((seq_count, chans, tok_rows), jnp.bfloat16),
        scratch_shapes=[
            pltpu.VMEM((block * span, LANES), jnp.float32),
            pltpu.VMEM((block * rows, 2 * LANES), jnp.bfloat16),
            pltpu.VMEM((block * rows, 2 * LANES), jnp.float32),
        ],
        compiler_params=pltpu.CompilerParams(vmem_limit_bytes=VMEM_BYTES),
        cost_estimate=pl.CostEstimate(flops=flops, bytes_accessed=moved, transcendentals=0),
    )(values, response, *tables)


def gate_kernel(conv_ref, skip_ref, signal_ref, query_ref, out_ref):
    conv = conv_ref[...].astype(jnp.float32).T
    inner = conv + skip_ref[...] * signal_ref[...].astype(jnp.float32)
    out_ref[...] = (query_ref[...].astype(jnp.float32) * inner).astype(out_ref.dtype)


def gate(longconv, skip, lo, signal, query):
    chans, tok_rows = longconv.shape
    first = lo // LANES
    flat = pl.BlockSpec((tok_rows, LANES), lambda i: (0, i))
    return pl.pallas_call(
        gate_kernel,
        grid=(chans // LANES,),
        in_specs=[
            pl.BlockSpec((LANES, tok_rows), lambda i: (i, 0)),
            pl.BlockSpec((1, LANES), lambda i: (0, first + i)),
            flat,
            flat,
        ],
        out_specs=flat,
        out_shape=jax.ShapeDtypeStruct((tok_rows, chans), jnp.bfloat16),
        compiler_params=pltpu.CompilerParams(vmem_limit_bytes=VMEM_BYTES),
        cost_estimate=pl.CostEstimate(flops=4 * chans * tok_rows, bytes_accessed=8 * chans * tok_rows, transcendentals=0),
    )(longconv, skip[None, :], signal, query)


def reorder_kernel(spec_ref, order_ref, out_ref):
    each = out_ref.shape[3]
    x = spec_ref[0].astype(jnp.bfloat16)
    y = jnp.dot(x, order_ref[...], preferred_element_type=jnp.float32).astype(jnp.bfloat16)
    for d in range(out_ref.shape[0]):
        out_ref[d, 0, 0] = y[d * each : (d + 1) * each]


def fold_kernel(got_ref, out_ref, came, held):
    seq_count, pairs, tok_rows = got_ref.shape[0], got_ref.shape[3], got_ref.shape[4]
    chans = pairs // 2
    runs = tok_rows // LANES
    rows = (seq_count + 1) * runs
    for part in range(2):
        sign = 1.0 if part == 0 else -1.0
        for s in range(seq_count):
            for r in range(runs):
                at = (s * runs + r) * pairs
                lanes = slice(r * LANES, (r + 1) * LANES)
                came[at : at + pairs, :] = got_ref[s, part, 0, :, lanes].astype(jnp.float32)
        for k1 in range(seq_count + 1):
            other = 2 * seq_count - k1
            for r in range(runs):
                value = came[pl.ds((k1 // 2 * runs + r) * pairs + k1 % 2, chans, stride=2), :]
                if k1 == seq_count:
                    value = sign * value
                elif k1 > 0:
                    value = value + sign * came[pl.ds((other // 2 * runs + r) * pairs + other % 2, chans, stride=2), :]
                held[pl.ds(k1 * runs + r, chans, stride=rows), :] = value
        out_ref[part] = held[...].reshape(chans, rows, LANES).astype(out_ref.dtype)


def reordered_spectrum(spectrum, seq_count, chunks):
    parts, chans, own, tok_rows = spectrum.shape
    runs = tok_rows // LANES
    size = chans // chunks
    each = size // seq_count
    col = lax.broadcasted_iota(jnp.int32, (tok_rows, tok_rows), 1)
    row = lax.broadcasted_iota(jnp.int32, (tok_rows, tok_rows), 0)
    wanted = col // LANES + runs * (col % LANES)
    wanted = jnp.where(lax.axis_index("seq") >= seq_count // 2, tok_rows - 1 - wanted, wanted)
    order = (row == wanted).astype(jnp.bfloat16)
    shape = (seq_count, parts, chunks, own * each, tok_rows)
    return pl.pallas_call(
        reorder_kernel,
        grid=(parts, chunks),
        in_specs=[
            pl.BlockSpec((1, own * size, tok_rows), lambda p, j: (p, j, 0)),
            pl.BlockSpec((tok_rows, tok_rows), lambda p, j: (0, 0)),
        ],
        out_specs=pl.BlockSpec((seq_count, 1, 1, own * each, tok_rows), lambda p, j: (0, p, j, 0, 0)),
        out_shape=jax.ShapeDtypeStruct(shape, jnp.bfloat16),
        compiler_params=pltpu.CompilerParams(vmem_limit_bytes=VMEM_BYTES),
        cost_estimate=pl.CostEstimate(
            flops=2 * spectrum.size * tok_rows, bytes_accessed=6 * spectrum.size, transcendentals=0
        ),
    )(spectrum.reshape(parts, chans * own, tok_rows), order)


def folded_response(sent, own):
    seq_count, parts, chunks, pairs, tok_rows = sent.shape
    runs = tok_rows // LANES
    each = pairs // own
    got = lax.all_to_all(sent, "seq", split_axis=0, concat_axis=0, tiled=True)
    block = min(CHAN_BLOCK, each)
    rows = (seq_count + 1) * runs
    return pl.pallas_call(
        fold_kernel,
        grid=(chunks, each // block),
        in_specs=[pl.BlockSpec((seq_count, parts, 1, own * block, tok_rows), lambda j, i: (0, 0, j, i, 0))],
        out_specs=pl.BlockSpec((parts, block, rows, LANES), lambda j, i: (0, j * (each // block) + i, 0, 0)),
        out_shape=jax.ShapeDtypeStruct((parts, chunks * each, rows, LANES), jnp.bfloat16),
        scratch_shapes=[
            pltpu.VMEM((seq_count * runs * own * block, LANES), jnp.float32),
            pltpu.VMEM((block * rows, LANES), jnp.float32),
        ],
        compiler_params=pltpu.CompilerParams(vmem_limit_bytes=VMEM_BYTES),
        cost_estimate=pl.CostEstimate(flops=sent.size, bytes_accessed=3 * sent.size, transcendentals=0),
    )(got)


def feature_rows(out_weight, seq_count):
    each = out_weight.shape[0] // seq_count
    own = lax.dynamic_slice_in_dim(out_weight, lax.axis_index("seq") * each, each, axis=0)
    own = lax.all_to_all(own, "chan", split_axis=1, concat_axis=0, tiled=True)
    return own.reshape(lax.axis_size("chan"), each, own.shape[1])


def combine_kernel(gated_ref, w_ref, *refs):
    out_ref = refs[-1]
    per, count, each, tile = w_ref.shape
    weight = jnp.concatenate([w_ref[:, z].reshape(per * each, tile) for z in range(count)], axis=0)
    total = jnp.dot(gated_ref[...], weight, preferred_element_type=jnp.float32)
    if len(refs) == 2:
        total = total + refs[0][...]
    out_ref[...] = total.astype(out_ref.dtype)


def combine(gathered, weight, lo, total, dtype):
    tok_rows, depth = gathered.shape
    _, count, each, features = weight.shape
    size = depth // count
    per = size // each
    first = lo // size
    tile = min(2 * LANES, features)
    block = pl.BlockSpec((tok_rows, tile), lambda i: (0, i))
    given = [] if total is None else [total]
    return pl.pallas_call(
        combine_kernel,
        grid=(features // tile,),
        in_specs=[
            pl.BlockSpec((tok_rows, depth), lambda i: (0, 0)),
            pl.BlockSpec((per, count, each, tile), lambda i: (first, 0, 0, i)),
            *[block for _ in given],
        ],
        out_specs=block,
        out_shape=jax.ShapeDtypeStruct((tok_rows, features), dtype),
        compiler_params=pltpu.CompilerParams(vmem_limit_bytes=VMEM_BYTES),
        cost_estimate=pl.CostEstimate(
            flops=2 * tok_rows * depth * features,
            bytes_accessed=2 * depth * (tok_rows + features) + 6 * tok_rows * features,
            transcendentals=0,
        ),
    )(gathered, weight, *given)


def shards(tokens, in_weight, conv_weight, spectrum, skip, out_weight):
    tok_rows, depth = tokens.shape
    seq_count = lax.axis_size("seq")
    chan_count = lax.axis_size("chan")
    chans = in_weight.shape[2]
    chunks = chunk_count(chans, seq_count)
    size = chans // chunks
    gathered = lax.all_gather(tokens, "chan", axis=1, tiled=True)
    weight = feature_rows(out_weight, seq_count)
    last_rows = tokens[tok_rows - HALO :]
    weight, last_rows, spectrum = lax.optimization_barrier((weight, last_rows, spectrum))
    halo = gather_by_doubling(from_behind(last_rows, "seq", 1), "chan")
    sent = reordered_spectrum(spectrum, seq_count, chunks)
    halo, sent, weight = lax.optimization_barrier((halo, sent, weight))
    response = folded_response(sent, spectrum.shape[2])
    weight = gather_by_doubling(weight, "seq")
    halo = jnp.einsum(
        "ztd,pzdc->ptc",
        halo,
        in_weight.reshape(3, chan_count, depth, chans),
        preferred_element_type=jnp.float32,
    ).astype(jnp.bfloat16)
    total = None
    for lo in range(0, chans, size):
        given = (gathered, in_weight, conv_weight, halo, lo, size, response, weight)
        query_t, signal, signal_t = project((0, 1, 2), *given)
        values = signal.reshape(seq_count, size // seq_count, tok_rows)
        values = lax.all_to_all(values, "seq", split_axis=0, concat_axis=0, tiled=True)
        longconv = lax.all_to_all(
            long_conv(values, response, lo // seq_count), "seq", split_axis=0, concat_axis=0, tiled=True
        ).reshape(size, tok_rows)
        gated = lax.all_gather(gate(longconv, skip, lo, signal_t, query_t), "chan", axis=1, tiled=True)
        dtype = jnp.bfloat16 if lo + size == chans else jnp.float32
        total = combine(gated, weight, lo, total, dtype)
    return total


def solution(mesh):
    placed = (
        P("seq", "chan"),
        P(None, None, "chan"),
        P(None, None, "chan"),
        P(None, "chan", "seq", None),
        P("chan"),
        P("chan", None),
    )
    return jax.shard_map(
        shards, mesh=mesh, in_specs=placed, out_specs=P("seq", "chan"), check_vma=False
    )
```

```python
import jax
import jax.numpy as jnp
import numpy as np
from jax import lax
from jax.experimental import pallas as pl
from jax.experimental.pallas import tpu as pltpu
from jax.sharding import PartitionSpec as P

TAPS = 3
LANES = 128
HALO = 16
DEPTH_STEP = 1024
CHAN_BLOCK = 16
CHUNKS = 2
MIB = 1024 * 1024


def from_behind(value, axis, by):
    size = lax.axis_size(axis)
    pairs = [(i, i + by) for i in range(size) if 0 <= i + by < size]
    return lax.ppermute(value, axis, pairs)


def gather_by_doubling(value, axis):
    size = lax.axis_size(axis)
    index = lax.axis_index(axis)
    held = value[None]
    bit = size // 2
    while bit >= 1:
        other = lax.ppermute(held, axis, [(i, i ^ bit) for i in range(size)])
        upper = (index // bit) % 2 == 1
        first = jnp.where(upper, other, held)
        second = jnp.where(upper, held, other)
        held = jnp.stack([first, second], axis=1).reshape((2 * held.shape[0],) + held.shape[1:])
        bit //= 2
    return held


def chunk_count(chans, seq_count):
    size = chans // CHUNKS
    return 1 if size % LANES or (size // seq_count) % CHAN_BLOCK else CHUNKS


def project_kernel(streams, extras, tok_ref, *refs):
    w_refs, taps_ref, halo_ref = refs[: len(streams)], refs[len(streams)], refs[len(streams) + 1]
    outs, acc = refs[len(streams) + 2 + extras : -1], refs[-1]
    step = pl.program_id(0)
    last = pl.num_programs(0) - 1
    rows = acc.shape[1] - HALO

    def part(w_ref):
        return jnp.dot(tok_ref[...], w_ref[0], preferred_element_type=jnp.float32)

    @pl.when(step == 0)
    def _():
        for i, p in enumerate(streams):
            acc[i, :HALO, :] = halo_ref[p].astype(jnp.float32)
            acc[i, HALO:, :] = part(w_refs[i])

    @pl.when(jnp.logical_and(step > 0, step < last))
    def _():
        for i in range(len(streams)):
            acc[i, HALO:, :] += part(w_refs[i])

    @pl.when(step == last)
    def _():
        for i in range(len(streams)):
            acc[i, HALO:, :] = (acc[i, HALO:, :] + part(w_refs[i])).astype(jnp.bfloat16).astype(jnp.float32)
        for r in range(0, rows, LANES):
            made = {}
            for i, p in enumerate(streams):
                total = taps_ref[0, p][None, :] * acc[i, pl.ds(HALO + r, LANES), :]
                for j in range(1, TAPS):
                    total = total + taps_ref[j, p][None, :] * acc[i, pl.ds(HALO + r - j, LANES), :]
                made[p] = total
            if 0 in made:
                outs[0][r : r + LANES, :] = made[0].astype(outs[0].dtype)
            if 1 in made:
                signal = made[1] * made[2]
                outs[-1][r : r + LANES, :] = signal.astype(outs[-1].dtype)
                outs[-2][:, r : r + LANES] = signal.T.astype(outs[-2].dtype)


def project(streams, gathered, in_weight, conv_weight, halo, lo, size, *after):
    rows, depth = gathered.shape
    step = min(DEPTH_STEP, depth // 2)
    at = lo // size
    flat = jax.ShapeDtypeStruct((rows, size), jnp.bfloat16)
    shapes = ([flat] if 0 in streams else []) + (
        [jax.ShapeDtypeStruct((size, rows), jnp.bfloat16), flat] if 1 in streams else []
    )

    def weight_of(p):
        return pl.BlockSpec((1, step, size), lambda z: (p, z, at))

    return pl.pallas_call(
        lambda *refs: project_kernel(streams, len(after), *refs),
        grid=(depth // step,),
        in_specs=[
            pl.BlockSpec((rows, step), lambda z: (0, z)),
            *[weight_of(p) for p in streams],
            pl.BlockSpec((TAPS, 3, size), lambda z: (0, 0, at)),
            pl.BlockSpec((3, HALO, size), lambda z: (0, 0, at)),
            *[pl.BlockSpec(memory_space=pl.ANY) for _ in after],
        ],
        out_specs=[pl.BlockSpec(shape.shape, lambda z: (0, 0)) for shape in shapes],
        out_shape=shapes,
        scratch_shapes=[pltpu.VMEM((len(streams), HALO + rows, size), jnp.float32)],
        compiler_params=pltpu.CompilerParams(vmem_limit_bytes=24 * MIB),
        cost_estimate=pl.CostEstimate(
            flops=2 * len(streams) * rows * depth * size,
            bytes_accessed=2 * depth * (len(streams) * size + rows),
            transcendentals=0,
        ),
    )(gathered, *[in_weight] * len(streams), conv_weight, halo, *after)


def transform_tables(seq_count, tok_rows):
    runs = tok_rows // LANES
    wide = 2 * seq_count * runs
    fft_len = wide * LANES
    k1 = np.arange(seq_count + 1)[:, None]
    k2a = np.arange(runs)[None, :]
    ka = (k1 + 2 * seq_count * k2a).reshape(-1)
    a = np.arange(seq_count * runs)
    b = np.arange(LANES)
    outer = 2.0 * np.pi * ((ka[:, None] * a[None, :]) % wide) / wide
    first = np.concatenate([np.cos(outer), -np.sin(outer)], axis=0)
    last = first.T / fft_len
    turn = 2.0 * np.pi * ((ka[:, None] * b[None, :]) % fft_len) / fft_len
    inner = 2.0 * np.pi * ((b[:, None] * b[None, :]) % LANES) / LANES
    cos, sin = np.cos(inner), np.sin(inner)
    forward = np.block([[cos, -sin], [sin, cos]])
    backward = np.block([[cos, sin], [-sin, cos]])
    half = lambda table: jnp.asarray(table, jnp.bfloat16)
    full = lambda table: jnp.asarray(table, jnp.float32)
    return half(first), half(last), full(np.cos(turn)), full(np.sin(turn)), half(forward), half(backward)


def conv_kernel(signal_ref, resp_ref, first_ref, last_ref, cos_ref, sin_ref, fwd_ref, bwd_ref, out_ref, held, low, high):
    seq_count, block, tok_rows = signal_ref.shape
    runs = tok_rows // LANES
    span = seq_count * runs
    rows = cos_ref.shape[0]
    pair = 2 * rows
    for s in range(seq_count):
        for r in range(runs):
            piece = signal_ref[s, :, r * LANES : (r + 1) * LANES].astype(jnp.float32)
            held[pl.ds(s * runs + r, block, stride=span), :] = piece
    cos, sin = cos_ref[...], sin_ref[...]
    for c in range(0, block, 2):
        x = jnp.concatenate([held[c * span : (c + 1) * span, :], held[(c + 1) * span : (c + 2) * span, :]], axis=1)
        y = jnp.dot(first_ref[...], x.astype(jnp.bfloat16), preferred_element_type=jnp.float32)
        turned = []
        for half in (slice(0, LANES), slice(LANES, 2 * LANES)):
            re, im = y[:rows, half], y[rows:, half]
            turned.append(jnp.concatenate([re * cos + im * sin, im * cos - re * sin], axis=1))
        low[c * rows : c * rows + pair, :] = jnp.concatenate(turned, axis=0).astype(jnp.bfloat16)
    high[...] = jnp.dot(low[...], fwd_ref[...], preferred_element_type=jnp.float32)
    for c in range(0, block, 2):
        done = []
        for d in (c, c + 1):
            re = high[d * rows : (d + 1) * rows, :LANES]
            im = high[d * rows : (d + 1) * rows, LANES:]
            hr = resp_ref[0, d].astype(jnp.float32)
            hi = resp_ref[1, d].astype(jnp.float32)
            done.append(jnp.concatenate([re * hr - im * hi, re * hi + im * hr], axis=1))
        low[c * rows : c * rows + pair, :] = jnp.concatenate(done, axis=0).astype(jnp.bfloat16)
    high[...] = jnp.dot(low[...], bwd_ref[...], preferred_element_type=jnp.float32)
    for c in range(0, block, 2):
        turned = []
        for d in (c, c + 1):
            re = high[d * rows : (d + 1) * rows, :LANES]
            im = high[d * rows : (d + 1) * rows, LANES:]
            turned.append(jnp.concatenate([re * cos - im * sin, im * cos + re * sin], axis=0))
        w = jnp.concatenate(turned, axis=1).astype(jnp.bfloat16)
        y = jnp.dot(last_ref[...], w, preferred_element_type=jnp.float32)
        held[c * span : (c + 1) * span, :] = y[:, :LANES]
        held[(c + 1) * span : (c + 2) * span, :] = y[:, LANES:]
    for s in range(seq_count):
        for r in range(runs):
            piece = held[pl.ds(s * runs + r, block, stride=span), :]
            out_ref[s, :, r * LANES : (r + 1) * LANES] = piece.astype(out_ref.dtype)


def long_conv(values, response, start=0):
    seq_count, chans, tok_rows = values.shape
    rows = response.shape[2]
    block = min(CHAN_BLOCK, chans)
    tables = transform_tables(seq_count, tok_rows)
    fixed = [pl.BlockSpec(t.shape, lambda i: (0, 0)) for t in tables]
    span = seq_count * tok_rows // LANES
    flops = chans * 2 * (2 * 2 * rows * span * LANES + 2 * rows * 4 * LANES * LANES)
    moved = 2 * (2 * values.size + 2 * chans * rows * LANES)
    return pl.pallas_call(
        conv_kernel,
        grid=(chans // block,),
        in_specs=[
            pl.BlockSpec((seq_count, block, tok_rows), lambda i: (0, i, 0)),
            pl.BlockSpec((2, block, rows, LANES), lambda i: (0, start // block + i, 0, 0)),
            *fixed,
        ],
        out_specs=pl.BlockSpec((seq_count, block, tok_rows), lambda i: (0, i, 0)),
        out_shape=jax.ShapeDtypeStruct((seq_count, chans, tok_rows), jnp.bfloat16),
        scratch_shapes=[
            pltpu.VMEM((block * span, LANES), jnp.float32),
            pltpu.VMEM((block * rows, 2 * LANES), jnp.bfloat16),
            pltpu.VMEM((block * rows, 2 * LANES), jnp.float32),
        ],
        compiler_params=pltpu.CompilerParams(vmem_limit_bytes=12 * MIB),
        cost_estimate=pl.CostEstimate(flops=flops, bytes_accessed=moved, transcendentals=0),
    )(values, response, *tables)


def gate_kernel(conv_ref, skip_ref, signal_ref, query_ref, out_ref):
    conv = conv_ref[...].astype(jnp.float32).T
    inner = conv + skip_ref[...] * signal_ref[...].astype(jnp.float32)
    out_ref[...] = (query_ref[...].astype(jnp.float32) * inner).astype(out_ref.dtype)


def gate(longconv, skip, lo, signal, query):
    chans, tok_rows = longconv.shape
    first = lo // LANES
    flat = pl.BlockSpec((tok_rows, LANES), lambda i: (0, i))
    return pl.pallas_call(
        gate_kernel,
        grid=(chans // LANES,),
        in_specs=[
            pl.BlockSpec((LANES, tok_rows), lambda i: (i, 0)),
            pl.BlockSpec((1, LANES), lambda i: (0, first + i)),
            flat,
            flat,
        ],
        out_specs=flat,
        out_shape=jax.ShapeDtypeStruct((tok_rows, chans), jnp.bfloat16),
        compiler_params=pltpu.CompilerParams(vmem_limit_bytes=8 * MIB),
        cost_estimate=pl.CostEstimate(flops=4 * chans * tok_rows, bytes_accessed=8 * chans * tok_rows, transcendentals=0),
    )(longconv, skip[None, :], signal, query)


def reorder_kernel(spec_ref, order_ref, out_ref):
    each = out_ref.shape[3]
    x = spec_ref[0].astype(jnp.bfloat16)
    y = jnp.dot(x, order_ref[...], preferred_element_type=jnp.float32).astype(jnp.bfloat16)
    for d in range(out_ref.shape[0]):
        out_ref[d, 0, 0] = y[d * each : (d + 1) * each]


def fold_kernel(got_ref, out_ref, came, held):
    seq_count, pairs, tok_rows = got_ref.shape[0], got_ref.shape[3], got_ref.shape[4]
    chans = pairs // 2
    runs = tok_rows // LANES
    rows = (seq_count + 1) * runs
    for part in range(2):
        sign = 1.0 if part == 0 else -1.0
        for s in range(seq_count):
            for r in range(runs):
                at = (s * runs + r) * pairs
                lanes = slice(r * LANES, (r + 1) * LANES)
                came[at : at + pairs, :] = got_ref[s, part, 0, :, lanes].astype(jnp.float32)
        for k1 in range(seq_count + 1):
            other = 2 * seq_count - k1
            for r in range(runs):
                value = came[pl.ds((k1 // 2 * runs + r) * pairs + k1 % 2, chans, stride=2), :]
                if k1 == seq_count:
                    value = sign * value
                elif k1 > 0:
                    value = value + sign * came[pl.ds((other // 2 * runs + r) * pairs + other % 2, chans, stride=2), :]
                held[pl.ds(k1 * runs + r, chans, stride=rows), :] = value
        out_ref[part] = held[...].reshape(chans, rows, LANES).astype(out_ref.dtype)


def reordered_spectrum(spectrum, seq_count, chunks):
    parts, chans, own, tok_rows = spectrum.shape
    runs = tok_rows // LANES
    size = chans // chunks
    each = size // seq_count
    col = lax.broadcasted_iota(jnp.int32, (tok_rows, tok_rows), 1)
    row = lax.broadcasted_iota(jnp.int32, (tok_rows, tok_rows), 0)
    wanted = col // LANES + runs * (col % LANES)
    wanted = jnp.where(lax.axis_index("seq") >= seq_count // 2, tok_rows - 1 - wanted, wanted)
    order = (row == wanted).astype(jnp.bfloat16)
    shape = (seq_count, parts, chunks, own * each, tok_rows)
    return pl.pallas_call(
        reorder_kernel,
        grid=(parts, chunks),
        in_specs=[
            pl.BlockSpec((1, own * size, tok_rows), lambda p, j: (p, j, 0)),
            pl.BlockSpec((tok_rows, tok_rows), lambda p, j: (0, 0)),
        ],
        out_specs=pl.BlockSpec((seq_count, 1, 1, own * each, tok_rows), lambda p, j: (0, p, j, 0, 0)),
        out_shape=jax.ShapeDtypeStruct(shape, jnp.bfloat16),
        compiler_params=pltpu.CompilerParams(vmem_limit_bytes=24 * MIB),
        cost_estimate=pl.CostEstimate(
            flops=2 * spectrum.size * tok_rows, bytes_accessed=6 * spectrum.size, transcendentals=0
        ),
    )(spectrum.reshape(parts, chans * own, tok_rows), order)


def folded_response(sent, own):
    seq_count, parts, chunks, pairs, tok_rows = sent.shape
    runs = tok_rows // LANES
    each = pairs // own
    got = lax.all_to_all(sent, "seq", split_axis=0, concat_axis=0, tiled=True)
    block = min(CHAN_BLOCK, each)
    rows = (seq_count + 1) * runs
    return pl.pallas_call(
        fold_kernel,
        grid=(chunks, each // block),
        in_specs=[pl.BlockSpec((seq_count, parts, 1, own * block, tok_rows), lambda j, i: (0, 0, j, i, 0))],
        out_specs=pl.BlockSpec((parts, block, rows, LANES), lambda j, i: (0, j * (each // block) + i, 0, 0)),
        out_shape=jax.ShapeDtypeStruct((parts, chunks * each, rows, LANES), jnp.bfloat16),
        scratch_shapes=[
            pltpu.VMEM((seq_count * runs * own * block, LANES), jnp.float32),
            pltpu.VMEM((block * rows, LANES), jnp.float32),
        ],
        compiler_params=pltpu.CompilerParams(vmem_limit_bytes=12 * MIB),
        cost_estimate=pl.CostEstimate(flops=sent.size, bytes_accessed=3 * sent.size, transcendentals=0),
    )(got)


def feature_rows(out_weight, seq_count):
    each = out_weight.shape[0] // seq_count
    own = lax.dynamic_slice_in_dim(out_weight, lax.axis_index("seq") * each, each, axis=0)
    own = lax.all_to_all(own, "chan", split_axis=1, concat_axis=0, tiled=True)
    return own.reshape(lax.axis_size("chan"), each, own.shape[1])


def combine_kernel(gated_ref, w_ref, *refs):
    out_ref = refs[-1]
    per, count, each, tile = w_ref.shape
    weight = jnp.concatenate([w_ref[:, z].reshape(per * each, tile) for z in range(count)], axis=0)
    total = jnp.dot(gated_ref[...], weight, preferred_element_type=jnp.float32)
    if len(refs) == 2:
        total = total + refs[0][...]
    out_ref[...] = total.astype(out_ref.dtype)


def combine(gathered, weight, lo, total, dtype):
    tok_rows, depth = gathered.shape
    _, count, each, features = weight.shape
    size = depth // count
    per = size // each
    first = lo // size
    tile = min(2 * LANES, features)
    block = pl.BlockSpec((tok_rows, tile), lambda i: (0, i))
    given = [] if total is None else [total]
    return pl.pallas_call(
        combine_kernel,
        grid=(features // tile,),
        in_specs=[
            pl.BlockSpec((tok_rows, depth), lambda i: (0, 0)),
            pl.BlockSpec((per, count, each, tile), lambda i: (first, 0, 0, i)),
            *[block for _ in given],
        ],
        out_specs=block,
        out_shape=jax.ShapeDtypeStruct((tok_rows, features), dtype),
        compiler_params=pltpu.CompilerParams(vmem_limit_bytes=20 * MIB),
        cost_estimate=pl.CostEstimate(
            flops=2 * tok_rows * depth * features,
            bytes_accessed=2 * depth * (tok_rows + features) + 6 * tok_rows * features,
            transcendentals=0,
        ),
    )(gathered, weight, *given)


def shards(tokens, in_weight, conv_weight, spectrum, skip, out_weight):
    tok_rows, depth = tokens.shape
    seq_count = lax.axis_size("seq")
    chan_count = lax.axis_size("chan")
    chans = in_weight.shape[2]
    chunks = chunk_count(chans, seq_count)
    size = chans // chunks
    gathered = lax.all_gather(tokens, "chan", axis=1, tiled=True)
    weight = feature_rows(out_weight, seq_count)
    last_rows = tokens[tok_rows - HALO :]
    weight, last_rows = lax.optimization_barrier((weight, last_rows))
    halo = gather_by_doubling(from_behind(last_rows, "seq", 1), "chan")
    sent = reordered_spectrum(spectrum, seq_count, chunks)
    halo, sent, weight = lax.optimization_barrier((halo, sent, weight))
    response = folded_response(sent, spectrum.shape[2])
    weight = gather_by_doubling(weight, "seq")
    halo = jnp.einsum(
        "ztd,pzdc->ptc",
        halo,
        in_weight.reshape(3, chan_count, depth, chans),
        preferred_element_type=jnp.float32,
    ).astype(jnp.bfloat16)
    total = None
    for lo in range(0, chans, size):
        given = (gathered, in_weight, conv_weight, halo, lo, size, response, weight)
        query_t, signal, signal_t = project((0, 1, 2), *given)
        values = signal.reshape(seq_count, size // seq_count, tok_rows)
        values = lax.all_to_all(values, "seq", split_axis=0, concat_axis=0, tiled=True)
        longconv = lax.all_to_all(
            long_conv(values, response, lo // seq_count), "seq", split_axis=0, concat_axis=0, tiled=True
        ).reshape(size, tok_rows)
        gated = lax.all_gather(gate(longconv, skip, lo, signal_t, query_t), "chan", axis=1, tiled=True)
        dtype = jnp.bfloat16 if lo + size == chans else jnp.float32
        total = combine(gated, weight, lo, total, dtype)
    return total


def solution(mesh):
    placed = (
        P("seq", "chan"),
        P(None, None, "chan"),
        P(None, None, "chan"),
        P(None, "chan", "seq", None),
        P("chan"),
        P("chan", None),
    )
    return jax.shard_map(
        shards, mesh=mesh, in_specs=placed, out_specs=P("seq", "chan"), check_vma=False
    )
```

```python
import jax
import jax.numpy as jnp
import numpy as np
from jax import lax
from jax.experimental import pallas as pl
from jax.experimental.pallas import tpu as pltpu
from jax.sharding import PartitionSpec as P

TAPS = 3
LANES = 128
HALO = 16
DEPTH_STEP = 512
CHAN_BLOCK = 16
CHUNKS = 2
MIB = 1024 * 1024


def from_behind(value, axis, by):
    size = lax.axis_size(axis)
    pairs = [(i, i + by) for i in range(size) if 0 <= i + by < size]
    return lax.ppermute(value, axis, pairs)


def gather_by_doubling(value, axis):
    size = lax.axis_size(axis)
    index = lax.axis_index(axis)
    held = value[None]
    bit = size // 2
    while bit >= 1:
        other = lax.ppermute(held, axis, [(i, i ^ bit) for i in range(size)])
        upper = (index // bit) % 2 == 1
        first = jnp.where(upper, other, held)
        second = jnp.where(upper, held, other)
        held = jnp.stack([first, second], axis=1).reshape((2 * held.shape[0],) + held.shape[1:])
        bit //= 2
    return held


def chunk_count(chans, seq_count):
    size = chans // CHUNKS
    return 1 if size % LANES or (size // seq_count) % CHAN_BLOCK else CHUNKS


def project_kernel(streams, extras, tok_ref, *refs):
    w_refs, taps_ref, halo_ref = refs[: len(streams)], refs[len(streams)], refs[len(streams) + 1]
    outs, acc = refs[len(streams) + 2 + extras : -1], refs[-1]
    step = pl.program_id(0)
    last = pl.num_programs(0) - 1
    rows = acc.shape[1] - HALO

    def part(w_ref):
        return jnp.dot(tok_ref[...], w_ref[0], preferred_element_type=jnp.float32)

    @pl.when(step == 0)
    def _():
        for i, p in enumerate(streams):
            acc[i, :HALO, :] = halo_ref[p].astype(jnp.float32)
            acc[i, HALO:, :] = part(w_refs[i])

    @pl.when(jnp.logical_and(step > 0, step < last))
    def _():
        for i in range(len(streams)):
            acc[i, HALO:, :] += part(w_refs[i])

    @pl.when(step == last)
    def _():
        for i in range(len(streams)):
            acc[i, HALO:, :] = (acc[i, HALO:, :] + part(w_refs[i])).astype(jnp.bfloat16).astype(jnp.float32)
        for r in range(0, rows, LANES):
            made = {}
            for i, p in enumerate(streams):
                total = taps_ref[0, p][None, :] * acc[i, pl.ds(HALO + r, LANES), :]
                for j in range(1, TAPS):
                    total = total + taps_ref[j, p][None, :] * acc[i, pl.ds(HALO + r - j, LANES), :]
                made[p] = total
            if 0 in made:
                outs[0][r : r + LANES, :] = made[0].astype(outs[0].dtype)
            if 1 in made:
                signal = made[1] * made[2]
                outs[-1][r : r + LANES, :] = signal.astype(outs[-1].dtype)
                outs[-2][:, r : r + LANES] = signal.T.astype(outs[-2].dtype)


def project(streams, gathered, in_weight, conv_weight, halo, lo, size, *after):
    rows, depth = gathered.shape
    step = min(DEPTH_STEP, depth // 2)
    at = lo // size
    flat = jax.ShapeDtypeStruct((rows, size), jnp.bfloat16)
    shapes = ([flat] if 0 in streams else []) + (
        [jax.ShapeDtypeStruct((size, rows), jnp.bfloat16), flat] if 1 in streams else []
    )

    def weight_of(p):
        return pl.BlockSpec((1, step, size), lambda z: (p, z, at))

    return pl.pallas_call(
        lambda *refs: project_kernel(streams, len(after), *refs),
        grid=(depth // step,),
        in_specs=[
            pl.BlockSpec((rows, step), lambda z: (0, z)),
            *[weight_of(p) for p in streams],
            pl.BlockSpec((TAPS, 3, size), lambda z: (0, 0, at)),
            pl.BlockSpec((3, HALO, size), lambda z: (0, 0, at)),
            *[pl.BlockSpec(memory_space=pl.ANY) for _ in after],
        ],
        out_specs=[pl.BlockSpec(shape.shape, lambda z: (0, 0)) for shape in shapes],
        out_shape=shapes,
        scratch_shapes=[pltpu.VMEM((len(streams), HALO + rows, size), jnp.float32)],
        compiler_params=pltpu.CompilerParams(vmem_limit_bytes=48 * MIB),
        cost_estimate=pl.CostEstimate(
            flops=2 * len(streams) * rows * depth * size,
            bytes_accessed=2 * depth * (len(streams) * size + rows),
            transcendentals=0,
        ),
    )(gathered, *[in_weight] * len(streams), conv_weight, halo, *after)


def transform_tables(seq_count, tok_rows):
    runs = tok_rows // LANES
    wide = 2 * seq_count * runs
    fft_len = wide * LANES
    k1 = np.arange(seq_count + 1)[:, None]
    k2a = np.arange(runs)[None, :]
    ka = (k1 + 2 * seq_count * k2a).reshape(-1)
    a = np.arange(seq_count * runs)
    b = np.arange(LANES)
    outer = 2.0 * np.pi * ((ka[:, None] * a[None, :]) % wide) / wide
    first = np.concatenate([np.cos(outer), -np.sin(outer)], axis=0)
    last = first.T / fft_len
    turn = 2.0 * np.pi * ((ka[:, None] * b[None, :]) % fft_len) / fft_len
    inner = 2.0 * np.pi * ((b[:, None] * b[None, :]) % LANES) / LANES
    cos, sin = np.cos(inner), np.sin(inner)
    forward = np.block([[cos, -sin], [sin, cos]])
    backward = np.block([[cos, sin], [-sin, cos]])
    half = lambda table: jnp.asarray(table, jnp.bfloat16)
    full = lambda table: jnp.asarray(table, jnp.float32)
    return half(first), half(last), full(np.cos(turn)), full(np.sin(turn)), half(forward), half(backward)


def conv_kernel(signal_ref, resp_ref, first_ref, last_ref, cos_ref, sin_ref, fwd_ref, bwd_ref, out_ref, held, low, high):
    seq_count, block, tok_rows = signal_ref.shape
    runs = tok_rows // LANES
    span = seq_count * runs
    rows = cos_ref.shape[0]
    pair = 2 * rows
    for s in range(seq_count):
        for r in range(runs):
            piece = signal_ref[s, :, r * LANES : (r + 1) * LANES].astype(jnp.float32)
            held[pl.ds(s * runs + r, block, stride=span), :] = piece
    cos, sin = cos_ref[...], sin_ref[...]
    for c in range(0, block, 2):
        x = jnp.concatenate([held[c * span : (c + 1) * span, :], held[(c + 1) * span : (c + 2) * span, :]], axis=1)
        y = jnp.dot(first_ref[...], x.astype(jnp.bfloat16), preferred_element_type=jnp.float32)
        turned = []
        for half in (slice(0, LANES), slice(LANES, 2 * LANES)):
            re, im = y[:rows, half], y[rows:, half]
            turned.append(jnp.concatenate([re * cos + im * sin, im * cos - re * sin], axis=1))
        low[c * rows : c * rows + pair, :] = jnp.concatenate(turned, axis=0).astype(jnp.bfloat16)
    high[...] = jnp.dot(low[...], fwd_ref[...], preferred_element_type=jnp.float32)
    for c in range(0, block, 2):
        done = []
        for d in (c, c + 1):
            re = high[d * rows : (d + 1) * rows, :LANES]
            im = high[d * rows : (d + 1) * rows, LANES:]
            hr = resp_ref[0, d].astype(jnp.float32)
            hi = resp_ref[1, d].astype(jnp.float32)
            done.append(jnp.concatenate([re * hr - im * hi, re * hi + im * hr], axis=1))
        low[c * rows : c * rows + pair, :] = jnp.concatenate(done, axis=0).astype(jnp.bfloat16)
    high[...] = jnp.dot(low[...], bwd_ref[...], preferred_element_type=jnp.float32)
    for c in range(0, block, 2):
        turned = []
        for d in (c, c + 1):
            re = high[d * rows : (d + 1) * rows, :LANES]
            im = high[d * rows : (d + 1) * rows, LANES:]
            turned.append(jnp.concatenate([re * cos - im * sin, im * cos + re * sin], axis=0))
        w = jnp.concatenate(turned, axis=1).astype(jnp.bfloat16)
        y = jnp.dot(last_ref[...], w, preferred_element_type=jnp.float32)
        held[c * span : (c + 1) * span, :] = y[:, :LANES]
        held[(c + 1) * span : (c + 2) * span, :] = y[:, LANES:]
    for s in range(seq_count):
        for r in range(runs):
            piece = held[pl.ds(s * runs + r, block, stride=span), :]
            out_ref[s, :, r * LANES : (r + 1) * LANES] = piece.astype(out_ref.dtype)


def long_conv(values, response, start=0):
    seq_count, chans, tok_rows = values.shape
    rows = response.shape[2]
    block = min(CHAN_BLOCK, chans)
    tables = transform_tables(seq_count, tok_rows)
    fixed = [pl.BlockSpec(t.shape, lambda i: (0, 0)) for t in tables]
    span = seq_count * tok_rows // LANES
    flops = chans * 2 * (2 * 2 * rows * span * LANES + 2 * rows * 4 * LANES * LANES)
    moved = 2 * (2 * values.size + 2 * chans * rows * LANES)
    return pl.pallas_call(
        conv_kernel,
        grid=(chans // block,),
        in_specs=[
            pl.BlockSpec((seq_count, block, tok_rows), lambda i: (0, i, 0)),
            pl.BlockSpec((2, block, rows, LANES), lambda i: (0, start // block + i, 0, 0)),
            *fixed,
        ],
        out_specs=pl.BlockSpec((seq_count, block, tok_rows), lambda i: (0, i, 0)),
        out_shape=jax.ShapeDtypeStruct((seq_count, chans, tok_rows), jnp.bfloat16),
        scratch_shapes=[
            pltpu.VMEM((block * span, LANES), jnp.float32),
            pltpu.VMEM((block * rows, 2 * LANES), jnp.bfloat16),
            pltpu.VMEM((block * rows, 2 * LANES), jnp.float32),
        ],
        compiler_params=pltpu.CompilerParams(vmem_limit_bytes=12 * MIB),
        cost_estimate=pl.CostEstimate(flops=flops, bytes_accessed=moved, transcendentals=0),
    )(values, response, *tables)


def gate_kernel(conv_ref, skip_ref, signal_ref, query_ref, out_ref):
    conv = conv_ref[...].astype(jnp.float32).T
    inner = conv + skip_ref[...] * signal_ref[...].astype(jnp.float32)
    out_ref[...] = (query_ref[...].astype(jnp.float32) * inner).astype(out_ref.dtype)


def gate(longconv, skip, lo, signal, query):
    chans, tok_rows = longconv.shape
    first = lo // LANES
    flat = pl.BlockSpec((tok_rows, LANES), lambda i: (0, i))
    return pl.pallas_call(
        gate_kernel,
        grid=(chans // LANES,),
        in_specs=[
            pl.BlockSpec((LANES, tok_rows), lambda i: (i, 0)),
            pl.BlockSpec((1, LANES), lambda i: (0, first + i)),
            flat,
            flat,
        ],
        out_specs=flat,
        out_shape=jax.ShapeDtypeStruct((tok_rows, chans), jnp.bfloat16),
        compiler_params=pltpu.CompilerParams(vmem_limit_bytes=8 * MIB),
        cost_estimate=pl.CostEstimate(flops=4 * chans * tok_rows, bytes_accessed=8 * chans * tok_rows, transcendentals=0),
    )(longconv, skip[None, :], signal, query)


def reorder_kernel(spec_ref, order_ref, out_ref):
    each = out_ref.shape[3]
    x = spec_ref[0].astype(jnp.bfloat16)
    y = jnp.dot(x, order_ref[...], preferred_element_type=jnp.float32).astype(jnp.bfloat16)
    for d in range(out_ref.shape[0]):
        out_ref[d, 0, 0] = y[d * each : (d + 1) * each]


def fold_kernel(got_ref, out_ref, came, held):
    seq_count, pairs, tok_rows = got_ref.shape[0], got_ref.shape[3], got_ref.shape[4]
    chans = pairs // 2
    runs = tok_rows // LANES
    rows = (seq_count + 1) * runs
    for part in range(2):
        sign = 1.0 if part == 0 else -1.0
        for s in range(seq_count):
            for r in range(runs):
                at = (s * runs + r) * pairs
                lanes = slice(r * LANES, (r + 1) * LANES)
                came[at : at + pairs, :] = got_ref[s, part, 0, :, lanes].astype(jnp.float32)
        for k1 in range(seq_count + 1):
            other = 2 * seq_count - k1
            for r in range(runs):
                value = came[pl.ds((k1 // 2 * runs + r) * pairs + k1 % 2, chans, stride=2), :]
                if k1 == seq_count:
                    value = sign * value
                elif k1 > 0:
                    value = value + sign * came[pl.ds((other // 2 * runs + r) * pairs + other % 2, chans, stride=2), :]
                held[pl.ds(k1 * runs + r, chans, stride=rows), :] = value
        out_ref[part] = held[...].reshape(chans, rows, LANES).astype(out_ref.dtype)


def reordered_spectrum(spectrum, seq_count, chunks):
    parts, chans, own, tok_rows = spectrum.shape
    runs = tok_rows // LANES
    size = chans // chunks
    each = size // seq_count
    col = lax.broadcasted_iota(jnp.int32, (tok_rows, tok_rows), 1)
    row = lax.broadcasted_iota(jnp.int32, (tok_rows, tok_rows), 0)
    wanted = col // LANES + runs * (col % LANES)
    wanted = jnp.where(lax.axis_index("seq") >= seq_count // 2, tok_rows - 1 - wanted, wanted)
    order = (row == wanted).astype(jnp.bfloat16)
    shape = (seq_count, parts, chunks, own * each, tok_rows)
    return pl.pallas_call(
        reorder_kernel,
        grid=(parts, chunks),
        in_specs=[
            pl.BlockSpec((1, own * size, tok_rows), lambda p, j: (p, j, 0)),
            pl.BlockSpec((tok_rows, tok_rows), lambda p, j: (0, 0)),
        ],
        out_specs=pl.BlockSpec((seq_count, 1, 1, own * each, tok_rows), lambda p, j: (0, p, j, 0, 0)),
        out_shape=jax.ShapeDtypeStruct(shape, jnp.bfloat16),
        compiler_params=pltpu.CompilerParams(vmem_limit_bytes=48 * MIB),
        cost_estimate=pl.CostEstimate(
            flops=2 * spectrum.size * tok_rows, bytes_accessed=6 * spectrum.size, transcendentals=0
        ),
    )(spectrum.reshape(parts, chans * own, tok_rows), order)


def folded_response(sent, own):
    seq_count, parts, chunks, pairs, tok_rows = sent.shape
    runs = tok_rows // LANES
    each = pairs // own
    got = lax.all_to_all(sent, "seq", split_axis=0, concat_axis=0, tiled=True)
    block = min(CHAN_BLOCK, each)
    rows = (seq_count + 1) * runs
    return pl.pallas_call(
        fold_kernel,
        grid=(chunks, each // block),
        in_specs=[pl.BlockSpec((seq_count, parts, 1, own * block, tok_rows), lambda j, i: (0, 0, j, i, 0))],
        out_specs=pl.BlockSpec((parts, block, rows, LANES), lambda j, i: (0, j * (each // block) + i, 0, 0)),
        out_shape=jax.ShapeDtypeStruct((parts, chunks * each, rows, LANES), jnp.bfloat16),
        scratch_shapes=[
            pltpu.VMEM((seq_count * runs * own * block, LANES), jnp.float32),
            pltpu.VMEM((block * rows, LANES), jnp.float32),
        ],
        compiler_params=pltpu.CompilerParams(vmem_limit_bytes=12 * MIB),
        cost_estimate=pl.CostEstimate(flops=sent.size, bytes_accessed=3 * sent.size, transcendentals=0),
    )(got)


def feature_rows(out_weight, seq_count):
    each = out_weight.shape[0] // seq_count
    own = lax.dynamic_slice_in_dim(out_weight, lax.axis_index("seq") * each, each, axis=0)
    own = lax.all_to_all(own, "chan", split_axis=1, concat_axis=0, tiled=True)
    return own.reshape(lax.axis_size("chan"), each, own.shape[1])


def combine_kernel(gated_ref, w_ref, *refs):
    out_ref = refs[-1]
    total = jnp.dot(gated_ref[...], w_ref[0], preferred_element_type=jnp.float32)
    if len(refs) == 2:
        total = total + refs[0][...]
    out_ref[...] = total.astype(out_ref.dtype)


def combine(gathered, weight, chunk, total, dtype):
    tok_rows, depth = gathered.shape
    features = weight.shape[2]
    tile = min(2 * LANES, features)
    block = pl.BlockSpec((tok_rows, tile), lambda i: (0, i))
    given = [] if total is None else [total]
    return pl.pallas_call(
        combine_kernel,
        grid=(features // tile,),
        in_specs=[
            pl.BlockSpec((tok_rows, depth), lambda i: (0, 0)),
            pl.BlockSpec((1, depth, tile), lambda i: (chunk, 0, i)),
            *[block for _ in given],
        ],
        out_specs=block,
        out_shape=jax.ShapeDtypeStruct((tok_rows, features), dtype),
        compiler_params=pltpu.CompilerParams(vmem_limit_bytes=60 * MIB),
        cost_estimate=pl.CostEstimate(
            flops=2 * tok_rows * depth * features,
            bytes_accessed=2 * depth * (tok_rows + features) + 6 * tok_rows * features,
            transcendentals=0,
        ),
    )(gathered, weight, *given)


def shards(tokens, in_weight, conv_weight, spectrum, skip, out_weight):
    tok_rows, depth = tokens.shape
    seq_count = lax.axis_size("seq")
    chan_count = lax.axis_size("chan")
    chans = in_weight.shape[2]
    chunks = chunk_count(chans, seq_count)
    size = chans // chunks
    gathered = lax.all_gather(tokens, "chan", axis=1, tiled=True)
    weight = feature_rows(out_weight, seq_count)
    last_rows = tokens[tok_rows - HALO :]
    weight, last_rows = lax.optimization_barrier((weight, last_rows))
    halo = gather_by_doubling(from_behind(last_rows, "seq", 1), "chan")
    sent = reordered_spectrum(spectrum, seq_count, chunks)
    halo, sent, weight = lax.optimization_barrier((halo, sent, weight))
    response = folded_response(sent, spectrum.shape[2])
    weight = gather_by_doubling(weight, "seq")
    weight = weight.reshape((chunks, seq_count // chunks) + weight.shape[1:]).transpose(0, 2, 1, 3, 4)
    weight = weight.reshape(chunks, chan_count * size, weight.shape[4])
    halo = jnp.einsum(
        "ztd,pzdc->ptc",
        halo,
        in_weight.reshape(3, chan_count, depth, chans),
        preferred_element_type=jnp.float32,
    ).astype(jnp.bfloat16)
    total = None
    for j, lo in enumerate(range(0, chans, size)):
        given = (gathered, in_weight, conv_weight, halo, lo, size, response, weight)
        query_t, signal, signal_t = project((0, 1, 2), *given)
        values = signal.reshape(seq_count, size // seq_count, tok_rows)
        values = lax.all_to_all(values, "seq", split_axis=0, concat_axis=0, tiled=True)
        longconv = lax.all_to_all(
            long_conv(values, response, lo // seq_count), "seq", split_axis=0, concat_axis=0, tiled=True
        ).reshape(size, tok_rows)
        gated = lax.all_gather(gate(longconv, skip, lo, signal_t, query_t), "chan", axis=1, tiled=True)
        dtype = jnp.bfloat16 if lo + size == chans else jnp.float32
        total = combine(gated, weight, j, total, dtype)
    return total


def solution(mesh):
    placed = (
        P("seq", "chan"),
        P(None, None, "chan"),
        P(None, None, "chan"),
        P(None, "chan", "seq", None),
        P("chan"),
        P("chan", None),
    )
    return jax.shard_map(
        shards, mesh=mesh, in_specs=placed, out_specs=P("seq", "chan"), check_vma=False
    )
```

```python
import jax
import jax.numpy as jnp
import numpy as np
from jax import lax
from jax.experimental import pallas as pl
from jax.experimental.pallas import tpu as pltpu
from jax.sharding import PartitionSpec as P

TAPS = 3
LANES = 128
HALO = 16
DEPTH_STEP = 1024
CHAN_BLOCK = 16
CHUNKS = 2
MIB = 1024 * 1024


def from_behind(value, axis, by):
    size = lax.axis_size(axis)
    pairs = [(i, i + by) for i in range(size) if 0 <= i + by < size]
    return lax.ppermute(value, axis, pairs)


def gather_by_doubling(value, axis):
    size = lax.axis_size(axis)
    index = lax.axis_index(axis)
    held = value[None]
    bit = size // 2
    while bit >= 1:
        other = lax.ppermute(held, axis, [(i, i ^ bit) for i in range(size)])
        upper = (index // bit) % 2 == 1
        first = jnp.where(upper, other, held)
        second = jnp.where(upper, held, other)
        held = jnp.stack([first, second], axis=1).reshape((2 * held.shape[0],) + held.shape[1:])
        bit //= 2
    return held


def chunk_count(chans, seq_count):
    size = chans // CHUNKS
    return 1 if size % LANES or (size // seq_count) % CHAN_BLOCK else CHUNKS


def project_kernel(streams, extras, tok_ref, *refs):
    w_refs, taps_ref, halo_ref = refs[: len(streams)], refs[len(streams)], refs[len(streams) + 1]
    outs, acc = refs[len(streams) + 2 + extras : -1], refs[-1]
    step = pl.program_id(0)
    last = pl.num_programs(0) - 1
    rows = acc.shape[1] - HALO

    def part(w_ref):
        return jnp.dot(tok_ref[...], w_ref[0], preferred_element_type=jnp.float32)

    @pl.when(step == 0)
    def _():
        for i, p in enumerate(streams):
            acc[i, :HALO, :] = halo_ref[p].astype(jnp.float32)
            acc[i, HALO:, :] = part(w_refs[i])

    @pl.when(jnp.logical_and(step > 0, step < last))
    def _():
        for i in range(len(streams)):
            acc[i, HALO:, :] += part(w_refs[i])

    @pl.when(step == last)
    def _():
        for i in range(len(streams)):
            acc[i, HALO:, :] = (acc[i, HALO:, :] + part(w_refs[i])).astype(jnp.bfloat16).astype(jnp.float32)
        for r in range(0, rows, LANES):
            made = {}
            for i, p in enumerate(streams):
                total = taps_ref[0, p][None, :] * acc[i, pl.ds(HALO + r, LANES), :]
                for j in range(1, TAPS):
                    total = total + taps_ref[j, p][None, :] * acc[i, pl.ds(HALO + r - j, LANES), :]
                made[p] = total
            if 0 in made:
                outs[0][r : r + LANES, :] = made[0].astype(outs[0].dtype)
            if 1 in made:
                signal = made[1] * made[2]
                outs[-1][:, r : r + LANES] = signal.T.astype(outs[-1].dtype)


def project(streams, gathered, in_weight, conv_weight, halo, lo, size, *after):
    rows, depth = gathered.shape
    step = min(DEPTH_STEP, depth // 2)
    at = lo // size
    shapes = [jax.ShapeDtypeStruct((rows, size), jnp.bfloat16)] if 0 in streams else []
    if 1 in streams:
        shapes.append(jax.ShapeDtypeStruct((size, rows), jnp.bfloat16))

    def weight_of(p):
        return pl.BlockSpec((1, step, size), lambda z: (p, z, at))

    return pl.pallas_call(
        lambda *refs: project_kernel(streams, len(after), *refs),
        grid=(depth // step,),
        in_specs=[
            pl.BlockSpec((rows, step), lambda z: (0, z)),
            *[weight_of(p) for p in streams],
            pl.BlockSpec((TAPS, 3, size), lambda z: (0, 0, at)),
            pl.BlockSpec((3, HALO, size), lambda z: (0, 0, at)),
            *[pl.BlockSpec(memory_space=pl.ANY) for _ in after],
        ],
        out_specs=[pl.BlockSpec(shape.shape, lambda z: (0, 0)) for shape in shapes],
        out_shape=shapes,
        scratch_shapes=[pltpu.VMEM((len(streams), HALO + rows, size), jnp.float32)],
        compiler_params=pltpu.CompilerParams(vmem_limit_bytes=48 * MIB),
        cost_estimate=pl.CostEstimate(
            flops=2 * len(streams) * rows * depth * size,
            bytes_accessed=2 * depth * (len(streams) * size + rows),
            transcendentals=0,
        ),
    )(gathered, *[in_weight] * len(streams), conv_weight, halo, *after)


def transform_tables(seq_count, tok_rows):
    runs = tok_rows // LANES
    wide = 2 * seq_count * runs
    fft_len = wide * LANES
    k1 = np.arange(seq_count + 1)[:, None]
    k2a = np.arange(runs)[None, :]
    ka = (k1 + 2 * seq_count * k2a).reshape(-1)
    a = np.arange(seq_count * runs)
    b = np.arange(LANES)
    outer = 2.0 * np.pi * ((ka[:, None] * a[None, :]) % wide) / wide
    first = np.concatenate([np.cos(outer), -np.sin(outer)], axis=0)
    last = first.T / fft_len
    turn = 2.0 * np.pi * ((ka[:, None] * b[None, :]) % fft_len) / fft_len
    inner = 2.0 * np.pi * ((b[:, None] * b[None, :]) % LANES) / LANES
    cos, sin = np.cos(inner), np.sin(inner)
    forward = np.block([[cos, -sin], [sin, cos]])
    backward = np.block([[cos, sin], [-sin, cos]])
    half = lambda table: jnp.asarray(table, jnp.bfloat16)
    full = lambda table: jnp.asarray(table, jnp.float32)
    return half(first), half(last), full(np.cos(turn)), full(np.sin(turn)), half(forward), half(backward)


def conv_kernel(signal_ref, resp_ref, first_ref, last_ref, cos_ref, sin_ref, fwd_ref, bwd_ref, out_ref, held, low, high):
    seq_count, block, tok_rows = signal_ref.shape
    runs = tok_rows // LANES
    span = seq_count * runs
    rows = cos_ref.shape[0]
    pair = 2 * rows
    for s in range(seq_count):
        for r in range(runs):
            piece = signal_ref[s, :, r * LANES : (r + 1) * LANES].astype(jnp.float32)
            held[pl.ds(s * runs + r, block, stride=span), :] = piece
    cos, sin = cos_ref[...], sin_ref[...]
    for c in range(0, block, 2):
        x = jnp.concatenate([held[c * span : (c + 1) * span, :], held[(c + 1) * span : (c + 2) * span, :]], axis=1)
        y = jnp.dot(first_ref[...], x.astype(jnp.bfloat16), preferred_element_type=jnp.float32)
        turned = []
        for half in (slice(0, LANES), slice(LANES, 2 * LANES)):
            re, im = y[:rows, half], y[rows:, half]
            turned.append(jnp.concatenate([re * cos + im * sin, im * cos - re * sin], axis=1))
        low[c * rows : c * rows + pair, :] = jnp.concatenate(turned, axis=0).astype(jnp.bfloat16)
    high[...] = jnp.dot(low[...], fwd_ref[...], preferred_element_type=jnp.float32)
    for c in range(0, block, 2):
        done = []
        for d in (c, c + 1):
            re = high[d * rows : (d + 1) * rows, :LANES]
            im = high[d * rows : (d + 1) * rows, LANES:]
            hr = resp_ref[0, d].astype(jnp.float32)
            hi = resp_ref[1, d].astype(jnp.float32)
            done.append(jnp.concatenate([re * hr - im * hi, re * hi + im * hr], axis=1))
        low[c * rows : c * rows + pair, :] = jnp.concatenate(done, axis=0).astype(jnp.bfloat16)
    high[...] = jnp.dot(low[...], bwd_ref[...], preferred_element_type=jnp.float32)
    for c in range(0, block, 2):
        turned = []
        for d in (c, c + 1):
            re = high[d * rows : (d + 1) * rows, :LANES]
            im = high[d * rows : (d + 1) * rows, LANES:]
            turned.append(jnp.concatenate([re * cos - im * sin, im * cos + re * sin], axis=0))
        w = jnp.concatenate(turned, axis=1).astype(jnp.bfloat16)
        y = jnp.dot(last_ref[...], w, preferred_element_type=jnp.float32)
        held[c * span : (c + 1) * span, :] = y[:, :LANES]
        held[(c + 1) * span : (c + 2) * span, :] = y[:, LANES:]
    for s in range(seq_count):
        for r in range(runs):
            piece = held[pl.ds(s * runs + r, block, stride=span), :]
            out_ref[s, :, r * LANES : (r + 1) * LANES] = piece.astype(out_ref.dtype)


def long_conv(values, response, start=0):
    seq_count, chans, tok_rows = values.shape
    rows = response.shape[2]
    block = min(CHAN_BLOCK, chans)
    tables = transform_tables(seq_count, tok_rows)
    fixed = [pl.BlockSpec(t.shape, lambda i: (0, 0)) for t in tables]
    span = seq_count * tok_rows // LANES
    flops = chans * 2 * (2 * 2 * rows * span * LANES + 2 * rows * 4 * LANES * LANES)
    moved = 2 * (2 * values.size + 2 * chans * rows * LANES)
    return pl.pallas_call(
        conv_kernel,
        grid=(chans // block,),
        in_specs=[
            pl.BlockSpec((seq_count, block, tok_rows), lambda i: (0, i, 0)),
            pl.BlockSpec((2, block, rows, LANES), lambda i: (0, start // block + i, 0, 0)),
            *fixed,
        ],
        out_specs=pl.BlockSpec((seq_count, block, tok_rows), lambda i: (0, i, 0)),
        out_shape=jax.ShapeDtypeStruct((seq_count, chans, tok_rows), jnp.bfloat16),
        scratch_shapes=[
            pltpu.VMEM((block * span, LANES), jnp.float32),
            pltpu.VMEM((block * rows, 2 * LANES), jnp.bfloat16),
            pltpu.VMEM((block * rows, 2 * LANES), jnp.float32),
        ],
        compiler_params=pltpu.CompilerParams(vmem_limit_bytes=12 * MIB),
        cost_estimate=pl.CostEstimate(flops=flops, bytes_accessed=moved, transcendentals=0),
    )(values, response, *tables)


def gate_kernel(conv_ref, skip_ref, signal_ref, query_ref, out_ref):
    inner = conv_ref[...].astype(jnp.float32) + skip_ref[...] * signal_ref[...].astype(jnp.float32)
    out_ref[...] = (query_ref[...].astype(jnp.float32) * inner.T).astype(out_ref.dtype)


def gate(longconv, skip, lo, signal, query):
    chans, tok_rows = longconv.shape
    first = lo // LANES
    rows = pl.BlockSpec((LANES, tok_rows), lambda i: (i, 0))
    flat = pl.BlockSpec((tok_rows, LANES), lambda i: (0, i))
    return pl.pallas_call(
        gate_kernel,
        grid=(chans // LANES,),
        in_specs=[rows, pl.BlockSpec((LANES, 1), lambda i: (first + i, 0)), rows, flat],
        out_specs=flat,
        out_shape=jax.ShapeDtypeStruct((tok_rows, chans), jnp.bfloat16),
        compiler_params=pltpu.CompilerParams(vmem_limit_bytes=8 * MIB),
        cost_estimate=pl.CostEstimate(flops=4 * chans * tok_rows, bytes_accessed=8 * chans * tok_rows, transcendentals=0),
    )(longconv, skip[:, None], signal, query)


def reorder_kernel(spec_ref, order_ref, out_ref):
    each = out_ref.shape[3]
    x = spec_ref[0].astype(jnp.bfloat16)
    y = jnp.dot(x, order_ref[...], preferred_element_type=jnp.float32).astype(jnp.bfloat16)
    for d in range(out_ref.shape[0]):
        out_ref[d, 0, 0] = y[d * each : (d + 1) * each]


def fold_kernel(got_ref, out_ref, came, held):
    seq_count, pairs, tok_rows = got_ref.shape[0], got_ref.shape[3], got_ref.shape[4]
    chans = pairs // 2
    runs = tok_rows // LANES
    rows = (seq_count + 1) * runs
    for part in range(2):
        sign = 1.0 if part == 0 else -1.0
        for s in range(seq_count):
            for r in range(runs):
                at = (s * runs + r) * pairs
                lanes = slice(r * LANES, (r + 1) * LANES)
                came[at : at + pairs, :] = got_ref[s, part, 0, :, lanes].astype(jnp.float32)
        for k1 in range(seq_count + 1):
            other = 2 * seq_count - k1
            for r in range(runs):
                value = came[pl.ds((k1 // 2 * runs + r) * pairs + k1 % 2, chans, stride=2), :]
                if k1 == seq_count:
                    value = sign * value
                elif k1 > 0:
                    value = value + sign * came[pl.ds((other // 2 * runs + r) * pairs + other % 2, chans, stride=2), :]
                held[pl.ds(k1 * runs + r, chans, stride=rows), :] = value
        out_ref[part] = held[...].reshape(chans, rows, LANES).astype(out_ref.dtype)


def reordered_spectrum(spectrum, seq_count, chunks):
    parts, chans, own, tok_rows = spectrum.shape
    runs = tok_rows // LANES
    size = chans // chunks
    each = size // seq_count
    col = lax.broadcasted_iota(jnp.int32, (tok_rows, tok_rows), 1)
    row = lax.broadcasted_iota(jnp.int32, (tok_rows, tok_rows), 0)
    wanted = col // LANES + runs * (col % LANES)
    wanted = jnp.where(lax.axis_index("seq") >= seq_count // 2, tok_rows - 1 - wanted, wanted)
    order = (row == wanted).astype(jnp.bfloat16)
    shape = (seq_count, parts, chunks, own * each, tok_rows)
    return pl.pallas_call(
        reorder_kernel,
        grid=(parts, chunks),
        in_specs=[
            pl.BlockSpec((1, own * size, tok_rows), lambda p, j: (p, j, 0)),
            pl.BlockSpec((tok_rows, tok_rows), lambda p, j: (0, 0)),
        ],
        out_specs=pl.BlockSpec((seq_count, 1, 1, own * each, tok_rows), lambda p, j: (0, p, j, 0, 0)),
        out_shape=jax.ShapeDtypeStruct(shape, jnp.bfloat16),
        compiler_params=pltpu.CompilerParams(vmem_limit_bytes=48 * MIB),
        cost_estimate=pl.CostEstimate(
            flops=2 * spectrum.size * tok_rows, bytes_accessed=6 * spectrum.size, transcendentals=0
        ),
    )(spectrum.reshape(parts, chans * own, tok_rows), order)


def folded_response(sent, own):
    seq_count, parts, chunks, pairs, tok_rows = sent.shape
    runs = tok_rows // LANES
    each = pairs // own
    got = lax.all_to_all(sent, "seq", split_axis=0, concat_axis=0, tiled=True)
    block = min(CHAN_BLOCK, each)
    rows = (seq_count + 1) * runs
    return pl.pallas_call(
        fold_kernel,
        grid=(chunks, each // block),
        in_specs=[pl.BlockSpec((seq_count, parts, 1, own * block, tok_rows), lambda j, i: (0, 0, j, i, 0))],
        out_specs=pl.BlockSpec((parts, block, rows, LANES), lambda j, i: (0, j * (each // block) + i, 0, 0)),
        out_shape=jax.ShapeDtypeStruct((parts, chunks * each, rows, LANES), jnp.bfloat16),
        scratch_shapes=[
            pltpu.VMEM((seq_count * runs * own * block, LANES), jnp.float32),
            pltpu.VMEM((block * rows, LANES), jnp.float32),
        ],
        compiler_params=pltpu.CompilerParams(vmem_limit_bytes=12 * MIB),
        cost_estimate=pl.CostEstimate(flops=sent.size, bytes_accessed=3 * sent.size, transcendentals=0),
    )(got)


def feature_rows(out_weight, seq_count):
    each = out_weight.shape[0] // seq_count
    own = lax.dynamic_slice_in_dim(out_weight, lax.axis_index("seq") * each, each, axis=0)
    own = lax.all_to_all(own, "chan", split_axis=1, concat_axis=0, tiled=True)
    return own.reshape(lax.axis_size("chan"), each, own.shape[1])


def combine_kernel(gated_ref, w_ref, *refs):
    out_ref = refs[-1]
    total = jnp.dot(gated_ref[...], w_ref[0], preferred_element_type=jnp.float32)
    if len(refs) == 2:
        total = total + refs[0][...]
    out_ref[...] = total.astype(out_ref.dtype)


def combine(gathered, weight, chunk, total, dtype):
    tok_rows, depth = gathered.shape
    features = weight.shape[2]
    tile = min(4 * LANES, features)
    block = pl.BlockSpec((tok_rows, tile), lambda i: (0, i))
    given = [] if total is None else [total]
    return pl.pallas_call(
        combine_kernel,
        grid=(features // tile,),
        in_specs=[
            pl.BlockSpec((tok_rows, depth), lambda i: (0, 0)),
            pl.BlockSpec((1, depth, tile), lambda i: (chunk, 0, i)),
            *[block for _ in given],
        ],
        out_specs=block,
        out_shape=jax.ShapeDtypeStruct((tok_rows, features), dtype),
        compiler_params=pltpu.CompilerParams(vmem_limit_bytes=60 * MIB),
        cost_estimate=pl.CostEstimate(
            flops=2 * tok_rows * depth * features,
            bytes_accessed=2 * depth * (tok_rows + features) + 6 * tok_rows * features,
            transcendentals=0,
        ),
    )(gathered, weight, *given)


def shards(tokens, in_weight, conv_weight, spectrum, skip, out_weight):
    tok_rows, depth = tokens.shape
    seq_count = lax.axis_size("seq")
    chan_count = lax.axis_size("chan")
    chans = in_weight.shape[2]
    chunks = chunk_count(chans, seq_count)
    size = chans // chunks
    gathered = lax.all_gather(tokens, "chan", axis=1, tiled=True)
    weight = feature_rows(out_weight, seq_count)
    last_rows = tokens[tok_rows - HALO :]
    weight, last_rows = lax.optimization_barrier((weight, last_rows))
    halo = gather_by_doubling(from_behind(last_rows, "seq", 1), "chan")
    sent = reordered_spectrum(spectrum, seq_count, chunks)
    halo, sent, weight = lax.optimization_barrier((halo, sent, weight))
    response = folded_response(sent, spectrum.shape[2])
    weight = gather_by_doubling(weight, "seq")
    weight = weight.reshape((chunks, seq_count // chunks) + weight.shape[1:]).transpose(0, 2, 1, 3, 4)
    weight = weight.reshape(chunks, chan_count * size, weight.shape[4])
    halo = jnp.einsum(
        "ztd,pzdc->ptc",
        halo,
        in_weight.reshape(3, chan_count, depth, chans),
        preferred_element_type=jnp.float32,
    ).astype(jnp.bfloat16)
    total = None
    for j, lo in enumerate(range(0, chans, size)):
        given = (gathered, in_weight, conv_weight, halo, lo, size, response, weight)
        query, signal = project((0, 1, 2), *given)
        values = signal.reshape(seq_count, size // seq_count, tok_rows)
        values = lax.all_to_all(values, "seq", split_axis=0, concat_axis=0, tiled=True)
        longconv = lax.all_to_all(
            long_conv(values, response, lo // seq_count), "seq", split_axis=0, concat_axis=0, tiled=True
        ).reshape(size, tok_rows)
        gated = lax.all_gather(gate(longconv, skip, lo, signal, query), "chan", axis=1, tiled=True)
        dtype = jnp.bfloat16 if lo + size == chans else jnp.float32
        total = combine(gated, weight, j, total, dtype)
    return total


def solution(mesh):
    placed = (
        P("seq", "chan"),
        P(None, None, "chan"),
        P(None, None, "chan"),
        P(None, "chan", "seq", None),
        P("chan"),
        P("chan", None),
    )
    return jax.shard_map(
        shards, mesh=mesh, in_specs=placed, out_specs=P("seq", "chan"), check_vma=False
    )
```

```python
import jax
import jax.numpy as jnp
import numpy as np
from jax import lax
from jax.experimental import pallas as pl
from jax.experimental.pallas import tpu as pltpu
from jax.sharding import PartitionSpec as P

TAPS = 3
LANES = 128
HALO = 16
CHAN_BLOCK = 16
CHUNKS = 2
MIB = 1024 * 1024


def from_behind(value, axis, by):
    size = lax.axis_size(axis)
    pairs = [(i, i + by) for i in range(size) if 0 <= i + by < size]
    return lax.ppermute(value, axis, pairs)


def gather_by_doubling(value, axis):
    size = lax.axis_size(axis)
    index = lax.axis_index(axis)
    held = value[None]
    bit = size // 2
    while bit >= 1:
        other = lax.ppermute(held, axis, [(i, i ^ bit) for i in range(size)])
        upper = (index // bit) % 2 == 1
        first = jnp.where(upper, other, held)
        second = jnp.where(upper, held, other)
        held = jnp.stack([first, second], axis=1).reshape((2 * held.shape[0],) + held.shape[1:])
        bit //= 2
    return held


def chunk_count(chans, seq_count):
    size = chans // CHUNKS
    return 1 if size % LANES or (size // seq_count) % CHAN_BLOCK else CHUNKS


def project_kernel(streams, extras, tok_ref, *refs):
    w_refs, taps_ref, halo_ref = refs[: len(streams)], refs[len(streams)], refs[len(streams) + 1]
    outs, acc = refs[len(streams) + 2 + extras : -1], refs[-1]
    step = pl.program_id(0)
    last = pl.num_programs(0) - 1
    rows = acc.shape[1] - HALO

    def part(w_ref):
        return jnp.dot(tok_ref[0], w_ref[0], preferred_element_type=jnp.float32)

    @pl.when(step == 0)
    def _():
        for i, p in enumerate(streams):
            acc[i, :HALO, :] = halo_ref[p].astype(jnp.float32)
            acc[i, HALO:, :] = part(w_refs[i])

    @pl.when(jnp.logical_and(step > 0, step < last))
    def _():
        for i in range(len(streams)):
            acc[i, HALO:, :] += part(w_refs[i])

    @pl.when(step == last)
    def _():
        for i in range(len(streams)):
            acc[i, HALO:, :] = (acc[i, HALO:, :] + part(w_refs[i])).astype(jnp.bfloat16).astype(jnp.float32)
        for r in range(0, rows, LANES):
            made = {}
            for i, p in enumerate(streams):
                total = taps_ref[0, p][None, :] * acc[i, pl.ds(HALO + r, LANES), :]
                for j in range(1, TAPS):
                    total = total + taps_ref[j, p][None, :] * acc[i, pl.ds(HALO + r - j, LANES), :]
                made[p] = total
            if 0 in made:
                outs[0][r : r + LANES, :] = made[0].astype(outs[0].dtype)
            if 1 in made:
                signal = made[1] * made[2]
                outs[-1][r : r + LANES, :] = signal.astype(outs[-1].dtype)
                outs[-2][:, r : r + LANES] = signal.T.astype(outs[-2].dtype)


def project(streams, gathered, in_weight, conv_weight, halo, lo, size, *after):
    count, rows, step = gathered.shape
    depth = count * step
    at = lo // size
    flat = jax.ShapeDtypeStruct((rows, size), jnp.bfloat16)
    shapes = ([flat] if 0 in streams else []) + (
        [jax.ShapeDtypeStruct((size, rows), jnp.bfloat16), flat] if 1 in streams else []
    )

    def weight_of(p):
        return pl.BlockSpec((1, step, size), lambda z: (p, z, at))

    return pl.pallas_call(
        lambda *refs: project_kernel(streams, len(after), *refs),
        grid=(count,),
        in_specs=[
            pl.BlockSpec((1, rows, step), lambda z: (z, 0, 0)),
            *[weight_of(p) for p in streams],
            pl.BlockSpec((TAPS, 3, size), lambda z: (0, 0, at)),
            pl.BlockSpec((3, HALO, size), lambda z: (0, 0, at)),
            *[pl.BlockSpec(memory_space=pl.ANY) for _ in after],
        ],
        out_specs=[pl.BlockSpec(shape.shape, lambda z: (0, 0)) for shape in shapes],
        out_shape=shapes,
        scratch_shapes=[pltpu.VMEM((len(streams), HALO + rows, size), jnp.float32)],
        compiler_params=pltpu.CompilerParams(vmem_limit_bytes=48 * MIB),
        cost_estimate=pl.CostEstimate(
            flops=2 * len(streams) * rows * depth * size,
            bytes_accessed=2 * depth * (len(streams) * size + rows),
            transcendentals=0,
        ),
    )(gathered, *[in_weight] * len(streams), conv_weight, halo, *after)


def transform_tables(seq_count, tok_rows):
    runs = tok_rows // LANES
    wide = 2 * seq_count * runs
    fft_len = wide * LANES
    k1 = np.arange(seq_count + 1)[:, None]
    k2a = np.arange(runs)[None, :]
    ka = (k1 + 2 * seq_count * k2a).reshape(-1)
    a = np.arange(seq_count * runs)
    b = np.arange(LANES)
    outer = 2.0 * np.pi * ((ka[:, None] * a[None, :]) % wide) / wide
    first = np.concatenate([np.cos(outer), -np.sin(outer)], axis=0)
    last = first.T / fft_len
    turn = 2.0 * np.pi * ((ka[:, None] * b[None, :]) % fft_len) / fft_len
    inner = 2.0 * np.pi * ((b[:, None] * b[None, :]) % LANES) / LANES
    cos, sin = np.cos(inner), np.sin(inner)
    forward = np.block([[cos, -sin], [sin, cos]])
    backward = np.block([[cos, sin], [-sin, cos]])
    half = lambda table: jnp.asarray(table, jnp.bfloat16)
    full = lambda table: jnp.asarray(table, jnp.float32)
    return half(first), half(last), full(np.cos(turn)), full(np.sin(turn)), half(forward), half(backward)


def conv_kernel(signal_ref, resp_ref, first_ref, last_ref, cos_ref, sin_ref, fwd_ref, bwd_ref, out_ref, held, low, high):
    seq_count, block, tok_rows = signal_ref.shape
    runs = tok_rows // LANES
    span = seq_count * runs
    rows = cos_ref.shape[0]
    pair = 2 * rows
    for s in range(seq_count):
        for r in range(runs):
            piece = signal_ref[s, :, r * LANES : (r + 1) * LANES].astype(jnp.float32)
            held[pl.ds(s * runs + r, block, stride=span), :] = piece
    cos, sin = cos_ref[...], sin_ref[...]
    for c in range(0, block, 2):
        x = jnp.concatenate([held[c * span : (c + 1) * span, :], held[(c + 1) * span : (c + 2) * span, :]], axis=1)
        y = jnp.dot(first_ref[...], x.astype(jnp.bfloat16), preferred_element_type=jnp.float32)
        turned = []
        for half in (slice(0, LANES), slice(LANES, 2 * LANES)):
            re, im = y[:rows, half], y[rows:, half]
            turned.append(jnp.concatenate([re * cos + im * sin, im * cos - re * sin], axis=1))
        low[c * rows : c * rows + pair, :] = jnp.concatenate(turned, axis=0).astype(jnp.bfloat16)
    high[...] = jnp.dot(low[...], fwd_ref[...], preferred_element_type=jnp.float32)
    for c in range(0, block, 2):
        done = []
        for d in (c, c + 1):
            re = high[d * rows : (d + 1) * rows, :LANES]
            im = high[d * rows : (d + 1) * rows, LANES:]
            hr = resp_ref[0, d].astype(jnp.float32)
            hi = resp_ref[1, d].astype(jnp.float32)
            done.append(jnp.concatenate([re * hr - im * hi, re * hi + im * hr], axis=1))
        low[c * rows : c * rows + pair, :] = jnp.concatenate(done, axis=0).astype(jnp.bfloat16)
    high[...] = jnp.dot(low[...], bwd_ref[...], preferred_element_type=jnp.float32)
    for c in range(0, block, 2):
        turned = []
        for d in (c, c + 1):
            re = high[d * rows : (d + 1) * rows, :LANES]
            im = high[d * rows : (d + 1) * rows, LANES:]
            turned.append(jnp.concatenate([re * cos - im * sin, im * cos + re * sin], axis=0))
        w = jnp.concatenate(turned, axis=1).astype(jnp.bfloat16)
        y = jnp.dot(last_ref[...], w, preferred_element_type=jnp.float32)
        held[c * span : (c + 1) * span, :] = y[:, :LANES]
        held[(c + 1) * span : (c + 2) * span, :] = y[:, LANES:]
    for s in range(seq_count):
        for r in range(runs):
            piece = held[pl.ds(s * runs + r, block, stride=span), :]
            out_ref[s, :, r * LANES : (r + 1) * LANES] = piece.astype(out_ref.dtype)


def long_conv(values, response, start=0):
    seq_count, chans, tok_rows = values.shape
    rows = response.shape[2]
    block = min(CHAN_BLOCK, chans)
    tables = transform_tables(seq_count, tok_rows)
    fixed = [pl.BlockSpec(t.shape, lambda i: (0, 0)) for t in tables]
    span = seq_count * tok_rows // LANES
    flops = chans * 2 * (2 * 2 * rows * span * LANES + 2 * rows * 4 * LANES * LANES)
    moved = 2 * (2 * values.size + 2 * chans * rows * LANES)
    return pl.pallas_call(
        conv_kernel,
        grid=(chans // block,),
        in_specs=[
            pl.BlockSpec((seq_count, block, tok_rows), lambda i: (0, i, 0)),
            pl.BlockSpec((2, block, rows, LANES), lambda i: (0, start // block + i, 0, 0)),
            *fixed,
        ],
        out_specs=pl.BlockSpec((seq_count, block, tok_rows), lambda i: (0, i, 0)),
        out_shape=jax.ShapeDtypeStruct((seq_count, chans, tok_rows), jnp.bfloat16),
        scratch_shapes=[
            pltpu.VMEM((block * span, LANES), jnp.float32),
            pltpu.VMEM((block * rows, 2 * LANES), jnp.bfloat16),
            pltpu.VMEM((block * rows, 2 * LANES), jnp.float32),
        ],
        compiler_params=pltpu.CompilerParams(vmem_limit_bytes=12 * MIB),
        cost_estimate=pl.CostEstimate(flops=flops, bytes_accessed=moved, transcendentals=0),
    )(values, response, *tables)


def gate_kernel(conv_ref, skip_ref, signal_ref, query_ref, out_ref):
    conv = conv_ref[...].astype(jnp.float32).T
    inner = conv + skip_ref[...] * signal_ref[...].astype(jnp.float32)
    out_ref[...] = (query_ref[...].astype(jnp.float32) * inner).astype(out_ref.dtype)


def gate(longconv, skip, lo, signal, query):
    chans, tok_rows = longconv.shape
    first = lo // LANES
    flat = pl.BlockSpec((tok_rows, LANES), lambda i: (0, i))
    return pl.pallas_call(
        gate_kernel,
        grid=(chans // LANES,),
        in_specs=[
            pl.BlockSpec((LANES, tok_rows), lambda i: (i, 0)),
            pl.BlockSpec((1, LANES), lambda i: (0, first + i)),
            flat,
            flat,
        ],
        out_specs=flat,
        out_shape=jax.ShapeDtypeStruct((tok_rows, chans), jnp.bfloat16),
        compiler_params=pltpu.CompilerParams(vmem_limit_bytes=8 * MIB),
        cost_estimate=pl.CostEstimate(flops=4 * chans * tok_rows, bytes_accessed=8 * chans * tok_rows, transcendentals=0),
    )(longconv, skip[None, :], signal, query)


def reorder_kernel(spec_ref, order_ref, out_ref):
    each = out_ref.shape[3]
    x = spec_ref[0].astype(jnp.bfloat16)
    y = jnp.dot(x, order_ref[...], preferred_element_type=jnp.float32).astype(jnp.bfloat16)
    for d in range(out_ref.shape[0]):
        out_ref[d, 0, 0] = y[d * each : (d + 1) * each]


def fold_kernel(got_ref, out_ref, came, held):
    seq_count, pairs, tok_rows = got_ref.shape[0], got_ref.shape[3], got_ref.shape[4]
    chans = pairs // 2
    runs = tok_rows // LANES
    rows = (seq_count + 1) * runs
    for part in range(2):
        sign = 1.0 if part == 0 else -1.0
        for s in range(seq_count):
            for r in range(runs):
                at = (s * runs + r) * pairs
                lanes = slice(r * LANES, (r + 1) * LANES)
                came[at : at + pairs, :] = got_ref[s, part, 0, :, lanes].astype(jnp.float32)
        for k1 in range(seq_count + 1):
            other = 2 * seq_count - k1
            for r in range(runs):
                value = came[pl.ds((k1 // 2 * runs + r) * pairs + k1 % 2, chans, stride=2), :]
                if k1 == seq_count:
                    value = sign * value
                elif k1 > 0:
                    value = value + sign * came[pl.ds((other // 2 * runs + r) * pairs + other % 2, chans, stride=2), :]
                held[pl.ds(k1 * runs + r, chans, stride=rows), :] = value
        out_ref[part] = held[...].reshape(chans, rows, LANES).astype(out_ref.dtype)


def reordered_spectrum(spectrum, seq_count, chunks):
    parts, chans, own, tok_rows = spectrum.shape
    runs = tok_rows // LANES
    size = chans // chunks
    each = size // seq_count
    col = lax.broadcasted_iota(jnp.int32, (tok_rows, tok_rows), 1)
    row = lax.broadcasted_iota(jnp.int32, (tok_rows, tok_rows), 0)
    wanted = col // LANES + runs * (col % LANES)
    wanted = jnp.where(lax.axis_index("seq") >= seq_count // 2, tok_rows - 1 - wanted, wanted)
    order = (row == wanted).astype(jnp.bfloat16)
    shape = (seq_count, parts, chunks, own * each, tok_rows)
    return pl.pallas_call(
        reorder_kernel,
        grid=(parts, chunks),
        in_specs=[
            pl.BlockSpec((1, own * size, tok_rows), lambda p, j: (p, j, 0)),
            pl.BlockSpec((tok_rows, tok_rows), lambda p, j: (0, 0)),
        ],
        out_specs=pl.BlockSpec((seq_count, 1, 1, own * each, tok_rows), lambda p, j: (0, p, j, 0, 0)),
        out_shape=jax.ShapeDtypeStruct(shape, jnp.bfloat16),
        compiler_params=pltpu.CompilerParams(vmem_limit_bytes=48 * MIB),
        cost_estimate=pl.CostEstimate(
            flops=2 * spectrum.size * tok_rows, bytes_accessed=6 * spectrum.size, transcendentals=0
        ),
    )(spectrum.reshape(parts, chans * own, tok_rows), order)


def folded_response(sent, own):
    seq_count, parts, chunks, pairs, tok_rows = sent.shape
    runs = tok_rows // LANES
    each = pairs // own
    got = lax.all_to_all(sent, "seq", split_axis=0, concat_axis=0, tiled=True)
    block = min(CHAN_BLOCK, each)
    rows = (seq_count + 1) * runs
    return pl.pallas_call(
        fold_kernel,
        grid=(chunks, each // block),
        in_specs=[pl.BlockSpec((seq_count, parts, 1, own * block, tok_rows), lambda j, i: (0, 0, j, i, 0))],
        out_specs=pl.BlockSpec((parts, block, rows, LANES), lambda j, i: (0, j * (each // block) + i, 0, 0)),
        out_shape=jax.ShapeDtypeStruct((parts, chunks * each, rows, LANES), jnp.bfloat16),
        scratch_shapes=[
            pltpu.VMEM((seq_count * runs * own * block, LANES), jnp.float32),
            pltpu.VMEM((block * rows, LANES), jnp.float32),
        ],
        compiler_params=pltpu.CompilerParams(vmem_limit_bytes=12 * MIB),
        cost_estimate=pl.CostEstimate(flops=sent.size, bytes_accessed=3 * sent.size, transcendentals=0),
    )(got)


def feature_rows(out_weight, seq_count):
    each = out_weight.shape[0] // seq_count
    own = lax.dynamic_slice_in_dim(out_weight, lax.axis_index("seq") * each, each, axis=0)
    own = lax.all_to_all(own, "chan", split_axis=1, concat_axis=0, tiled=True)
    return own.reshape(lax.axis_size("chan"), each, own.shape[1])


def combine_kernel(gated_ref, w_ref, *refs):
    out_ref = refs[-1]
    gated = jnp.concatenate([gated_ref[z] for z in range(gated_ref.shape[0])], axis=1)
    total = jnp.dot(gated, w_ref[0], preferred_element_type=jnp.float32)
    if len(refs) == 2:
        total = total + refs[0][...]
    out_ref[...] = total.astype(out_ref.dtype)


def combine(gathered, weight, chunk, total, dtype):
    count, tok_rows, size = gathered.shape
    depth = count * size
    features = weight.shape[2]
    tile = min(4 * LANES, features)
    block = pl.BlockSpec((tok_rows, tile), lambda i: (0, i))
    given = [] if total is None else [total]
    return pl.pallas_call(
        combine_kernel,
        grid=(features // tile,),
        in_specs=[
            pl.BlockSpec((count, tok_rows, size), lambda i: (0, 0, 0)),
            pl.BlockSpec((1, depth, tile), lambda i: (chunk, 0, i)),
            *[block for _ in given],
        ],
        out_specs=block,
        out_shape=jax.ShapeDtypeStruct((tok_rows, features), dtype),
        compiler_params=pltpu.CompilerParams(vmem_limit_bytes=60 * MIB),
        cost_estimate=pl.CostEstimate(
            flops=2 * tok_rows * depth * features,
            bytes_accessed=2 * depth * (tok_rows + features) + 6 * tok_rows * features,
            transcendentals=0,
        ),
    )(gathered, weight, *given)


def shards(tokens, in_weight, conv_weight, spectrum, skip, out_weight):
    tok_rows, depth = tokens.shape
    seq_count = lax.axis_size("seq")
    chan_count = lax.axis_size("chan")
    chans = in_weight.shape[2]
    chunks = chunk_count(chans, seq_count)
    size = chans // chunks
    gathered = lax.all_gather(tokens, "chan")
    weight = feature_rows(out_weight, seq_count)
    last_rows = tokens[tok_rows - HALO :]
    weight, last_rows = lax.optimization_barrier((weight, last_rows))
    halo = gather_by_doubling(from_behind(last_rows, "seq", 1), "chan")
    sent = reordered_spectrum(spectrum, seq_count, chunks)
    halo, sent, weight = lax.optimization_barrier((halo, sent, weight))
    response = folded_response(sent, spectrum.shape[2])
    weight = gather_by_doubling(weight, "seq")
    weight = weight.reshape((chunks, seq_count // chunks) + weight.shape[1:]).transpose(0, 2, 1, 3, 4)
    weight = weight.reshape(chunks, chan_count * size, weight.shape[4])
    halo = jnp.einsum(
        "ztd,pzdc->ptc",
        halo,
        in_weight.reshape(3, chan_count, depth, chans),
        preferred_element_type=jnp.float32,
    ).astype(jnp.bfloat16)
    total = None
    for j, lo in enumerate(range(0, chans, size)):
        given = (gathered, in_weight, conv_weight, halo, lo, size, response, weight)
        query_t, signal, signal_t = project((0, 1, 2), *given)
        values = signal.reshape(seq_count, size // seq_count, tok_rows)
        values = lax.all_to_all(values, "seq", split_axis=0, concat_axis=0, tiled=True)
        longconv = lax.all_to_all(
            long_conv(values, response, lo // seq_count), "seq", split_axis=0, concat_axis=0, tiled=True
        ).reshape(size, tok_rows)
        gated = lax.all_gather(gate(longconv, skip, lo, signal_t, query_t), "chan")
        dtype = jnp.bfloat16 if lo + size == chans else jnp.float32
        total = combine(gated, weight, j, total, dtype)
    return total


def solution(mesh):
    placed = (
        P("seq", "chan"),
        P(None, None, "chan"),
        P(None, None, "chan"),
        P(None, "chan", "seq", None),
        P("chan"),
        P("chan", None),
    )
    return jax.shard_map(
        shards, mesh=mesh, in_specs=placed, out_specs=P("seq", "chan"), check_vma=False
    )
```

```python
import jax
import jax.numpy as jnp
import numpy as np
from jax import lax
from jax.experimental import pallas as pl
from jax.experimental.pallas import tpu as pltpu
from jax.sharding import PartitionSpec as P

TAPS = 3
LANES = 128
HALO = 16
CHAN_BLOCK = 16
CHUNKS = 2
MIB = 1024 * 1024


def from_behind(value, axis, by):
    size = lax.axis_size(axis)
    pairs = [(i, i + by) for i in range(size) if 0 <= i + by < size]
    return lax.ppermute(value, axis, pairs)


def gather_by_doubling(value, axis):
    size = lax.axis_size(axis)
    index = lax.axis_index(axis)
    held = value[None]
    bit = size // 2
    while bit >= 1:
        other = lax.ppermute(held, axis, [(i, i ^ bit) for i in range(size)])
        upper = (index // bit) % 2 == 1
        first = jnp.where(upper, other, held)
        second = jnp.where(upper, held, other)
        held = jnp.stack([first, second], axis=1).reshape((2 * held.shape[0],) + held.shape[1:])
        bit //= 2
    return held


def chunk_count(chans, seq_count):
    size = chans // CHUNKS
    return 1 if size % LANES or (size // seq_count) % CHAN_BLOCK else CHUNKS


def project_kernel(extras, tok_ref, wq_ref, wk_ref, wv_ref, taps_ref, halo_ref, *rest):
    query_t_ref, signal_ref, signal_t_ref, acc = rest[extras:]
    step = pl.program_id(0)
    last = pl.num_programs(0) - 1
    rows, size = query_t_ref.shape

    def part():
        weight = jnp.concatenate([wq_ref[0], wk_ref[0], wv_ref[0]], axis=1)
        return jnp.dot(tok_ref[0], weight, preferred_element_type=jnp.float32)

    def filtered(p, r):
        lanes = slice(p * size, (p + 1) * size)
        total = taps_ref[0, p][None, :] * acc[pl.ds(HALO + r, LANES), lanes]
        for j in range(1, TAPS):
            total = total + taps_ref[j, p][None, :] * acc[pl.ds(HALO + r - j, LANES), lanes]
        return total

    @pl.when(step == 0)
    def _():
        for p in range(3):
            acc[:HALO, p * size : (p + 1) * size] = halo_ref[p].astype(jnp.float32)
        acc[HALO:, :] = part()

    @pl.when(jnp.logical_and(step > 0, step < last))
    def _():
        acc[HALO:, :] += part()

    @pl.when(step == last)
    def _():
        acc[HALO:, :] = (acc[HALO:, :] + part()).astype(jnp.bfloat16).astype(jnp.float32)
        for r in range(0, rows, LANES):
            query_t_ref[r : r + LANES, :] = filtered(0, r).astype(query_t_ref.dtype)
            signal = filtered(1, r) * filtered(2, r)
            signal_t_ref[r : r + LANES, :] = signal.astype(signal_t_ref.dtype)
            signal_ref[:, r : r + LANES] = signal.T.astype(signal_ref.dtype)


def project(gathered, in_weight, conv_weight, halo, lo, size, *after):
    count, rows, step = gathered.shape
    at = lo // size
    flat = jax.ShapeDtypeStruct((rows, size), jnp.bfloat16)
    shapes = [flat, jax.ShapeDtypeStruct((size, rows), jnp.bfloat16), flat]

    def weight_of(p):
        return pl.BlockSpec((1, step, size), lambda z: (p, z, at))

    return pl.pallas_call(
        lambda *refs: project_kernel(len(after), *refs),
        grid=(count,),
        in_specs=[
            pl.BlockSpec((1, rows, step), lambda z: (z, 0, 0)),
            *[weight_of(p) for p in range(3)],
            pl.BlockSpec((TAPS, 3, size), lambda z: (0, 0, at)),
            pl.BlockSpec((3, HALO, size), lambda z: (0, 0, at)),
            *[pl.BlockSpec(memory_space=pl.ANY) for _ in after],
        ],
        out_specs=[pl.BlockSpec(shape.shape, lambda z: (0, 0)) for shape in shapes],
        out_shape=shapes,
        scratch_shapes=[pltpu.VMEM((HALO + rows, 3 * size), jnp.float32)],
        compiler_params=pltpu.CompilerParams(vmem_limit_bytes=48 * MIB),
        cost_estimate=pl.CostEstimate(
            flops=2 * 3 * rows * count * step * size,
            bytes_accessed=2 * count * step * (3 * size + rows),
            transcendentals=0,
        ),
    )(gathered, in_weight, in_weight, in_weight, conv_weight, halo, *after)


def transform_tables(seq_count, tok_rows):
    runs = tok_rows // LANES
    wide = 2 * seq_count * runs
    fft_len = wide * LANES
    k1 = np.arange(seq_count + 1)[:, None]
    k2a = np.arange(runs)[None, :]
    ka = (k1 + 2 * seq_count * k2a).reshape(-1)
    a = np.arange(seq_count * runs)
    b = np.arange(LANES)
    outer = 2.0 * np.pi * ((ka[:, None] * a[None, :]) % wide) / wide
    first = np.concatenate([np.cos(outer), -np.sin(outer)], axis=0)
    last = first.T / fft_len
    turn = 2.0 * np.pi * ((ka[:, None] * b[None, :]) % fft_len) / fft_len
    inner = 2.0 * np.pi * ((b[:, None] * b[None, :]) % LANES) / LANES
    cos, sin = np.cos(inner), np.sin(inner)
    forward = np.block([[cos, -sin], [sin, cos]])
    backward = np.block([[cos, sin], [-sin, cos]])
    half = lambda table: jnp.asarray(table, jnp.bfloat16)
    full = lambda table: jnp.asarray(table, jnp.float32)
    return half(first), half(last), full(np.cos(turn)), full(np.sin(turn)), half(forward), half(backward)


def conv_kernel(signal_ref, resp_ref, first_ref, last_ref, cos_ref, sin_ref, fwd_ref, bwd_ref, out_ref, held, low, high):
    seq_count, block, tok_rows = signal_ref.shape
    runs = tok_rows // LANES
    span = seq_count * runs
    rows = cos_ref.shape[0]
    pair = 2 * rows
    for s in range(seq_count):
        for r in range(runs):
            piece = signal_ref[s, :, r * LANES : (r + 1) * LANES].astype(jnp.float32)
            held[pl.ds(s * runs + r, block, stride=span), :] = piece
    cos, sin = cos_ref[...], sin_ref[...]
    for c in range(0, block, 2):
        x = jnp.concatenate([held[c * span : (c + 1) * span, :], held[(c + 1) * span : (c + 2) * span, :]], axis=1)
        y = jnp.dot(first_ref[...], x.astype(jnp.bfloat16), preferred_element_type=jnp.float32)
        turned = []
        for half in (slice(0, LANES), slice(LANES, 2 * LANES)):
            re, im = y[:rows, half], y[rows:, half]
            turned.append(jnp.concatenate([re * cos + im * sin, im * cos - re * sin], axis=1))
        low[c * rows : c * rows + pair, :] = jnp.concatenate(turned, axis=0).astype(jnp.bfloat16)
    high[...] = jnp.dot(low[...], fwd_ref[...], preferred_element_type=jnp.float32)
    for c in range(0, block, 2):
        done = []
        for d in (c, c + 1):
            re = high[d * rows : (d + 1) * rows, :LANES]
            im = high[d * rows : (d + 1) * rows, LANES:]
            hr = resp_ref[0, d].astype(jnp.float32)
            hi = resp_ref[1, d].astype(jnp.float32)
            done.append(jnp.concatenate([re * hr - im * hi, re * hi + im * hr], axis=1))
        low[c * rows : c * rows + pair, :] = jnp.concatenate(done, axis=0).astype(jnp.bfloat16)
    high[...] = jnp.dot(low[...], bwd_ref[...], preferred_element_type=jnp.float32)
    for c in range(0, block, 2):
        turned = []
        for d in (c, c + 1):
            re = high[d * rows : (d + 1) * rows, :LANES]
            im = high[d * rows : (d + 1) * rows, LANES:]
            turned.append(jnp.concatenate([re * cos - im * sin, im * cos + re * sin], axis=0))
        w = jnp.concatenate(turned, axis=1).astype(jnp.bfloat16)
        y = jnp.dot(last_ref[...], w, preferred_element_type=jnp.float32)
        held[c * span : (c + 1) * span, :] = y[:, :LANES]
        held[(c + 1) * span : (c + 2) * span, :] = y[:, LANES:]
    for s in range(seq_count):
        for r in range(runs):
            piece = held[pl.ds(s * runs + r, block, stride=span), :]
            out_ref[s, :, r * LANES : (r + 1) * LANES] = piece.astype(out_ref.dtype)


def long_conv(values, response, start=0):
    seq_count, chans, tok_rows = values.shape
    rows = response.shape[2]
    block = min(CHAN_BLOCK, chans)
    tables = transform_tables(seq_count, tok_rows)
    fixed = [pl.BlockSpec(t.shape, lambda i: (0, 0)) for t in tables]
    span = seq_count * tok_rows // LANES
    flops = chans * 2 * (2 * 2 * rows * span * LANES + 2 * rows * 4 * LANES * LANES)
    moved = 2 * (2 * values.size + 2 * chans * rows * LANES)
    return pl.pallas_call(
        conv_kernel,
        grid=(chans // block,),
        in_specs=[
            pl.BlockSpec((seq_count, block, tok_rows), lambda i: (0, i, 0)),
            pl.BlockSpec((2, block, rows, LANES), lambda i: (0, start // block + i, 0, 0)),
            *fixed,
        ],
        out_specs=pl.BlockSpec((seq_count, block, tok_rows), lambda i: (0, i, 0)),
        out_shape=jax.ShapeDtypeStruct((seq_count, chans, tok_rows), jnp.bfloat16),
        scratch_shapes=[
            pltpu.VMEM((block * span, LANES), jnp.float32),
            pltpu.VMEM((block * rows, 2 * LANES), jnp.bfloat16),
            pltpu.VMEM((block * rows, 2 * LANES), jnp.float32),
        ],
        compiler_params=pltpu.CompilerParams(vmem_limit_bytes=12 * MIB),
        cost_estimate=pl.CostEstimate(flops=flops, bytes_accessed=moved, transcendentals=0),
    )(values, response, *tables)


def gate_kernel(conv_ref, skip_ref, signal_ref, query_ref, out_ref):
    conv = conv_ref[...].astype(jnp.float32).T
    inner = conv + skip_ref[...] * signal_ref[...].astype(jnp.float32)
    out_ref[...] = (query_ref[...].astype(jnp.float32) * inner).astype(out_ref.dtype)


def gate(longconv, skip, lo, signal, query):
    chans, tok_rows = longconv.shape
    first = lo // LANES
    flat = pl.BlockSpec((tok_rows, LANES), lambda i: (0, i))
    return pl.pallas_call(
        gate_kernel,
        grid=(chans // LANES,),
        in_specs=[
            pl.BlockSpec((LANES, tok_rows), lambda i: (i, 0)),
            pl.BlockSpec((1, LANES), lambda i: (0, first + i)),
            flat,
            flat,
        ],
        out_specs=flat,
        out_shape=jax.ShapeDtypeStruct((tok_rows, chans), jnp.bfloat16),
        compiler_params=pltpu.CompilerParams(vmem_limit_bytes=8 * MIB),
        cost_estimate=pl.CostEstimate(flops=4 * chans * tok_rows, bytes_accessed=8 * chans * tok_rows, transcendentals=0),
    )(longconv, skip[None, :], signal, query)


def reorder_kernel(spec_ref, order_ref, out_ref):
    each = out_ref.shape[3]
    x = spec_ref[0].astype(jnp.bfloat16)
    y = jnp.dot(x, order_ref[...], preferred_element_type=jnp.float32).astype(jnp.bfloat16)
    for d in range(out_ref.shape[0]):
        out_ref[d, 0, 0] = y[d * each : (d + 1) * each]


def fold_kernel(got_ref, out_ref, came, held):
    seq_count, pairs, tok_rows = got_ref.shape[0], got_ref.shape[3], got_ref.shape[4]
    chans = pairs // 2
    runs = tok_rows // LANES
    rows = (seq_count + 1) * runs
    for part in range(2):
        sign = 1.0 if part == 0 else -1.0
        for s in range(seq_count):
            for r in range(runs):
                at = (s * runs + r) * pairs
                lanes = slice(r * LANES, (r + 1) * LANES)
                came[at : at + pairs, :] = got_ref[s, part, 0, :, lanes].astype(jnp.float32)
        for k1 in range(seq_count + 1):
            other = 2 * seq_count - k1
            for r in range(runs):
                value = came[pl.ds((k1 // 2 * runs + r) * pairs + k1 % 2, chans, stride=2), :]
                if k1 == seq_count:
                    value = sign * value
                elif k1 > 0:
                    value = value + sign * came[pl.ds((other // 2 * runs + r) * pairs + other % 2, chans, stride=2), :]
                held[pl.ds(k1 * runs + r, chans, stride=rows), :] = value
        out_ref[part] = held[...].reshape(chans, rows, LANES).astype(out_ref.dtype)


def reordered_spectrum(spectrum, seq_count, chunks):
    parts, chans, own, tok_rows = spectrum.shape
    runs = tok_rows // LANES
    size = chans // chunks
    each = size // seq_count
    col = lax.broadcasted_iota(jnp.int32, (tok_rows, tok_rows), 1)
    row = lax.broadcasted_iota(jnp.int32, (tok_rows, tok_rows), 0)
    wanted = col // LANES + runs * (col % LANES)
    wanted = jnp.where(lax.axis_index("seq") >= seq_count // 2, tok_rows - 1 - wanted, wanted)
    order = (row == wanted).astype(jnp.bfloat16)
    shape = (seq_count, parts, chunks, own * each, tok_rows)
    return pl.pallas_call(
        reorder_kernel,
        grid=(parts, chunks),
        in_specs=[
            pl.BlockSpec((1, own * size, tok_rows), lambda p, j: (p, j, 0)),
            pl.BlockSpec((tok_rows, tok_rows), lambda p, j: (0, 0)),
        ],
        out_specs=pl.BlockSpec((seq_count, 1, 1, own * each, tok_rows), lambda p, j: (0, p, j, 0, 0)),
        out_shape=jax.ShapeDtypeStruct(shape, jnp.bfloat16),
        compiler_params=pltpu.CompilerParams(vmem_limit_bytes=48 * MIB),
        cost_estimate=pl.CostEstimate(
            flops=2 * spectrum.size * tok_rows, bytes_accessed=6 * spectrum.size, transcendentals=0
        ),
    )(spectrum.reshape(parts, chans * own, tok_rows), order)


def folded_response(sent, own):
    seq_count, parts, chunks, pairs, tok_rows = sent.shape
    runs = tok_rows // LANES
    each = pairs // own
    got = lax.all_to_all(sent, "seq", split_axis=0, concat_axis=0, tiled=True)
    block = min(CHAN_BLOCK, each)
    rows = (seq_count + 1) * runs
    return pl.pallas_call(
        fold_kernel,
        grid=(chunks, each // block),
        in_specs=[pl.BlockSpec((seq_count, parts, 1, own * block, tok_rows), lambda j, i: (0, 0, j, i, 0))],
        out_specs=pl.BlockSpec((parts, block, rows, LANES), lambda j, i: (0, j * (each // block) + i, 0, 0)),
        out_shape=jax.ShapeDtypeStruct((parts, chunks * each, rows, LANES), jnp.bfloat16),
        scratch_shapes=[
            pltpu.VMEM((seq_count * runs * own * block, LANES), jnp.float32),
            pltpu.VMEM((block * rows, LANES), jnp.float32),
        ],
        compiler_params=pltpu.CompilerParams(vmem_limit_bytes=12 * MIB),
        cost_estimate=pl.CostEstimate(flops=sent.size, bytes_accessed=3 * sent.size, transcendentals=0),
    )(got)


def feature_rows(out_weight, seq_count):
    each = out_weight.shape[0] // seq_count
    own = lax.dynamic_slice_in_dim(out_weight, lax.axis_index("seq") * each, each, axis=0)
    own = lax.all_to_all(own, "chan", split_axis=1, concat_axis=0, tiled=True)
    return own.reshape(lax.axis_size("chan"), each, own.shape[1])


def combine_kernel(gated_ref, w_ref, *refs):
    out_ref = refs[-1]
    gated = jnp.concatenate([gated_ref[z] for z in range(gated_ref.shape[0])], axis=1)
    total = jnp.dot(gated, w_ref[0], preferred_element_type=jnp.float32)
    if len(refs) == 2:
        total = total + refs[0][...]
    out_ref[...] = total.astype(out_ref.dtype)


def combine(gathered, weight, chunk, total, dtype):
    count, tok_rows, size = gathered.shape
    depth = count * size
    features = weight.shape[2]
    tile = min(4 * LANES, features)
    block = pl.BlockSpec((tok_rows, tile), lambda i: (0, i))
    given = [] if total is None else [total]
    return pl.pallas_call(
        combine_kernel,
        grid=(features // tile,),
        in_specs=[
            pl.BlockSpec((count, tok_rows, size), lambda i: (0, 0, 0)),
            pl.BlockSpec((1, depth, tile), lambda i: (chunk, 0, i)),
            *[block for _ in given],
        ],
        out_specs=block,
        out_shape=jax.ShapeDtypeStruct((tok_rows, features), dtype),
        compiler_params=pltpu.CompilerParams(vmem_limit_bytes=60 * MIB),
        cost_estimate=pl.CostEstimate(
            flops=2 * tok_rows * depth * features,
            bytes_accessed=2 * depth * (tok_rows + features) + 6 * tok_rows * features,
            transcendentals=0,
        ),
    )(gathered, weight, *given)


def shards(tokens, in_weight, conv_weight, spectrum, skip, out_weight):
    tok_rows, depth = tokens.shape
    seq_count = lax.axis_size("seq")
    chan_count = lax.axis_size("chan")
    chans = in_weight.shape[2]
    chunks = chunk_count(chans, seq_count)
    size = chans // chunks
    gathered = lax.all_gather(tokens, "chan")
    weight = feature_rows(out_weight, seq_count)
    last_rows = tokens[tok_rows - HALO :]
    weight, last_rows = lax.optimization_barrier((weight, last_rows))
    halo = gather_by_doubling(from_behind(last_rows, "seq", 1), "chan")
    sent = reordered_spectrum(spectrum, seq_count, chunks)
    halo, sent, weight = lax.optimization_barrier((halo, sent, weight))
    response = folded_response(sent, spectrum.shape[2])
    weight = gather_by_doubling(weight, "seq")
    weight = weight.reshape((chunks, seq_count // chunks) + weight.shape[1:]).transpose(0, 2, 1, 3, 4)
    weight = weight.reshape(chunks, chan_count * size, weight.shape[4])
    halo = jnp.einsum(
        "ztd,pzdc->ptc",
        halo,
        in_weight.reshape(3, chan_count, depth, chans),
        preferred_element_type=jnp.float32,
    ).astype(jnp.bfloat16)
    total = None
    for j, lo in enumerate(range(0, chans, size)):
        given = (gathered, in_weight, conv_weight, halo, lo, size, response, weight)
        query_t, signal, signal_t = project(*given)
        values = signal.reshape(seq_count, size // seq_count, tok_rows)
        values = lax.all_to_all(values, "seq", split_axis=0, concat_axis=0, tiled=True)
        longconv = lax.all_to_all(
            long_conv(values, response, lo // seq_count), "seq", split_axis=0, concat_axis=0, tiled=True
        ).reshape(size, tok_rows)
        gated = lax.all_gather(gate(longconv, skip, lo, signal_t, query_t), "chan")
        dtype = jnp.bfloat16 if lo + size == chans else jnp.float32
        total = combine(gated, weight, j, total, dtype)
    return total


def solution(mesh):
    placed = (
        P("seq", "chan"),
        P(None, None, "chan"),
        P(None, None, "chan"),
        P(None, "chan", "seq", None),
        P("chan"),
        P("chan", None),
    )
    return jax.shard_map(
        shards, mesh=mesh, in_specs=placed, out_specs=P("seq", "chan"), check_vma=False
    )
```

```python
import jax
import jax.numpy as jnp
import numpy as np
from jax import lax
from jax.experimental import pallas as pl
from jax.experimental.pallas import tpu as pltpu
from jax.sharding import PartitionSpec as P

TAPS = 3
LANES = 128
HALO = 16
CHAN_BLOCK = 16
CHUNKS = 2
MIB = 1024 * 1024


def from_behind(value, axis, by):
    size = lax.axis_size(axis)
    pairs = [(i, i + by) for i in range(size) if 0 <= i + by < size]
    return lax.ppermute(value, axis, pairs)


def along_line(value, axis):
    size = lax.axis_size(axis)
    before, after = [value], [value]
    for k in range(1, size):
        before.append(lax.ppermute(before[-1], axis, [(i, i + 1) for i in range(k - 1, size - 1)]))
        after.append(lax.ppermute(after[-1], axis, [(i, i - 1) for i in range(1, size - k + 1)]))
    return before, after[1:]


def gather_by_doubling(value, axis):
    size = lax.axis_size(axis)
    index = lax.axis_index(axis)
    held = value[None]
    bit = size // 2
    while bit >= 1:
        other = lax.ppermute(held, axis, [(i, i ^ bit) for i in range(size)])
        upper = (index // bit) % 2 == 1
        first = jnp.where(upper, other, held)
        second = jnp.where(upper, held, other)
        held = jnp.stack([first, second], axis=1).reshape((2 * held.shape[0],) + held.shape[1:])
        bit //= 2
    return held


def chunk_count(chans, seq_count):
    size = chans // CHUNKS
    return 1 if size % LANES or (size // seq_count) % CHAN_BLOCK else CHUNKS


def project_kernel(count, extras, me_ref, *refs):
    before_refs, after_refs = refs[:count], refs[count : 2 * count - 1]
    wq_ref, wk_ref, wv_ref, taps_ref, halo_ref = refs[2 * count - 1 : 2 * count + 4]
    query_t_ref, signal_ref, signal_t_ref, before, after, acc, sems = refs[2 * count + 4 + extras :]
    step = pl.program_id(0)
    rows, size = query_t_ref.shape
    copies = []
    for k in range(count):
        given = [pltpu.make_async_copy(before_refs[k], before.at[k], sems.at[2 * k])]
        if k > 0:
            given.append(pltpu.make_async_copy(after_refs[count - k - 1], after.at[k - 1], sems.at[2 * k + 1]))
        copies.append(given)

    def part(tokens):
        weight = jnp.concatenate([wq_ref[0], wk_ref[0], wv_ref[0]], axis=1)
        return jnp.dot(tokens, weight, preferred_element_type=jnp.float32)

    def filtered(p, r):
        lanes = slice(p * size, (p + 1) * size)
        total = taps_ref[0, p][None, :] * acc[pl.ds(HALO + r, LANES), lanes]
        for j in range(1, TAPS):
            total = total + taps_ref[j, p][None, :] * acc[pl.ds(HALO + r - j, LANES), lanes]
        return total

    @pl.when(step == 0)
    def _():
        for given in copies:
            for copy in given:
                copy.start()
        for p in range(3):
            acc[:HALO, p * size : (p + 1) * size] = halo_ref[p].astype(jnp.float32)

    for k in range(count):

        @pl.when(step == k)
        def _():
            for copy in copies[k]:
                copy.wait()

    @pl.when(step == 0)
    def _():
        acc[HALO:, :] = part(before[0])

    @pl.when(step > 0)
    def _():
        acc[HALO:, :] += part(before[step] + after[step - 1])

    @pl.when(step == count - 1)
    def _():
        acc[HALO:, :] = acc[HALO:, :].astype(jnp.bfloat16).astype(jnp.float32)
        for r in range(0, rows, LANES):
            query_t_ref[r : r + LANES, :] = filtered(0, r).astype(query_t_ref.dtype)
            signal = filtered(1, r) * filtered(2, r)
            signal_t_ref[r : r + LANES, :] = signal.astype(signal_t_ref.dtype)
            signal_ref[:, r : r + LANES] = signal.T.astype(signal_ref.dtype)


def slot_owner(me, k, count):
    return lax.rem(me[0] - k + count, count)


def project(line, in_weight, conv_weight, halo, lo, size, *following):
    before, after = line
    count = len(before)
    rows, step = before[0].shape
    at = lo // size
    flat = jax.ShapeDtypeStruct((rows, size), jnp.bfloat16)
    shapes = [flat, jax.ShapeDtypeStruct((size, rows), jnp.bfloat16), flat]
    me = lax.axis_index("chan").astype(jnp.int32).reshape(1)

    def weight_of(p):
        return pl.BlockSpec((1, step, size), lambda z, me: (p, slot_owner(me, z, count), at))

    anywhere = pl.BlockSpec(memory_space=pl.ANY)
    return pl.pallas_call(
        lambda *refs: project_kernel(count, len(following), *refs),
        grid_spec=pltpu.PrefetchScalarGridSpec(
            num_scalar_prefetch=1,
            grid=(count,),
            in_specs=[
                *[anywhere] * (2 * count - 1),
                *[weight_of(p) for p in range(3)],
                pl.BlockSpec((TAPS, 3, size), lambda z, me: (0, 0, at)),
                pl.BlockSpec((3, HALO, size), lambda z, me: (0, 0, at)),
                *[anywhere] * len(following),
            ],
            out_specs=[pl.BlockSpec(shape.shape, lambda z, me: (0, 0)) for shape in shapes],
            scratch_shapes=[
                pltpu.VMEM((count, rows, step), jnp.bfloat16),
                pltpu.VMEM((count - 1, rows, step), jnp.bfloat16),
                pltpu.VMEM((HALO + rows, 3 * size), jnp.float32),
                pltpu.SemaphoreType.DMA((2 * count,)),
            ],
        ),
        out_shape=shapes,
        compiler_params=pltpu.CompilerParams(vmem_limit_bytes=56 * MIB),
        cost_estimate=pl.CostEstimate(
            flops=2 * 3 * rows * count * step * size,
            bytes_accessed=2 * count * step * (3 * size + rows),
            transcendentals=0,
        ),
    )(me, *before, *after, in_weight, in_weight, in_weight, conv_weight, halo, *following)


def transform_tables(seq_count, tok_rows):
    runs = tok_rows // LANES
    wide = 2 * seq_count * runs
    fft_len = wide * LANES
    k1 = np.arange(seq_count + 1)[:, None]
    k2a = np.arange(runs)[None, :]
    ka = (k1 + 2 * seq_count * k2a).reshape(-1)
    a = np.arange(seq_count * runs)
    b = np.arange(LANES)
    outer = 2.0 * np.pi * ((ka[:, None] * a[None, :]) % wide) / wide
    first = np.concatenate([np.cos(outer), -np.sin(outer)], axis=0)
    last = first.T / fft_len
    turn = 2.0 * np.pi * ((ka[:, None] * b[None, :]) % fft_len) / fft_len
    inner = 2.0 * np.pi * ((b[:, None] * b[None, :]) % LANES) / LANES
    cos, sin = np.cos(inner), np.sin(inner)
    forward = np.block([[cos, -sin], [sin, cos]])
    backward = np.block([[cos, sin], [-sin, cos]])
    half = lambda table: jnp.asarray(table, jnp.bfloat16)
    full = lambda table: jnp.asarray(table, jnp.float32)
    return half(first), half(last), full(np.cos(turn)), full(np.sin(turn)), half(forward), half(backward)


def conv_kernel(signal_ref, resp_ref, first_ref, last_ref, cos_ref, sin_ref, fwd_ref, bwd_ref, out_ref, held, low, high):
    seq_count, block, tok_rows = signal_ref.shape
    runs = tok_rows // LANES
    span = seq_count * runs
    rows = cos_ref.shape[0]
    pair = 2 * rows
    for s in range(seq_count):
        for r in range(runs):
            piece = signal_ref[s, :, r * LANES : (r + 1) * LANES].astype(jnp.float32)
            held[pl.ds(s * runs + r, block, stride=span), :] = piece
    cos, sin = cos_ref[...], sin_ref[...]
    for c in range(0, block, 2):
        x = jnp.concatenate([held[c * span : (c + 1) * span, :], held[(c + 1) * span : (c + 2) * span, :]], axis=1)
        y = jnp.dot(first_ref[...], x.astype(jnp.bfloat16), preferred_element_type=jnp.float32)
        turned = []
        for half in (slice(0, LANES), slice(LANES, 2 * LANES)):
            re, im = y[:rows, half], y[rows:, half]
            turned.append(jnp.concatenate([re * cos + im * sin, im * cos - re * sin], axis=1))
        low[c * rows : c * rows + pair, :] = jnp.concatenate(turned, axis=0).astype(jnp.bfloat16)
    high[...] = jnp.dot(low[...], fwd_ref[...], preferred_element_type=jnp.float32)
    for c in range(0, block, 2):
        done = []
        for d in (c, c + 1):
            re = high[d * rows : (d + 1) * rows, :LANES]
            im = high[d * rows : (d + 1) * rows, LANES:]
            hr = resp_ref[0, d].astype(jnp.float32)
            hi = resp_ref[1, d].astype(jnp.float32)
            done.append(jnp.concatenate([re * hr - im * hi, re * hi + im * hr], axis=1))
        low[c * rows : c * rows + pair, :] = jnp.concatenate(done, axis=0).astype(jnp.bfloat16)
    high[...] = jnp.dot(low[...], bwd_ref[...], preferred_element_type=jnp.float32)
    for c in range(0, block, 2):
        turned = []
        for d in (c, c + 1):
            re = high[d * rows : (d + 1) * rows, :LANES]
            im = high[d * rows : (d + 1) * rows, LANES:]
            turned.append(jnp.concatenate([re * cos - im * sin, im * cos + re * sin], axis=0))
        w = jnp.concatenate(turned, axis=1).astype(jnp.bfloat16)
        y = jnp.dot(last_ref[...], w, preferred_element_type=jnp.float32)
        held[c * span : (c + 1) * span, :] = y[:, :LANES]
        held[(c + 1) * span : (c + 2) * span, :] = y[:, LANES:]
    for s in range(seq_count):
        for r in range(runs):
            piece = held[pl.ds(s * runs + r, block, stride=span), :]
            out_ref[s, :, r * LANES : (r + 1) * LANES] = piece.astype(out_ref.dtype)


def long_conv(values, response, start=0):
    seq_count, chans, tok_rows = values.shape
    rows = response.shape[2]
    block = min(CHAN_BLOCK, chans)
    tables = transform_tables(seq_count, tok_rows)
    fixed = [pl.BlockSpec(t.shape, lambda i: (0, 0)) for t in tables]
    span = seq_count * tok_rows // LANES
    flops = chans * 2 * (2 * 2 * rows * span * LANES + 2 * rows * 4 * LANES * LANES)
    moved = 2 * (2 * values.size + 2 * chans * rows * LANES)
    return pl.pallas_call(
        conv_kernel,
        grid=(chans // block,),
        in_specs=[
            pl.BlockSpec((seq_count, block, tok_rows), lambda i: (0, i, 0)),
            pl.BlockSpec((2, block, rows, LANES), lambda i: (0, start // block + i, 0, 0)),
            *fixed,
        ],
        out_specs=pl.BlockSpec((seq_count, block, tok_rows), lambda i: (0, i, 0)),
        out_shape=jax.ShapeDtypeStruct((seq_count, chans, tok_rows), jnp.bfloat16),
        scratch_shapes=[
            pltpu.VMEM((block * span, LANES), jnp.float32),
            pltpu.VMEM((block * rows, 2 * LANES), jnp.bfloat16),
            pltpu.VMEM((block * rows, 2 * LANES), jnp.float32),
        ],
        compiler_params=pltpu.CompilerParams(vmem_limit_bytes=12 * MIB),
        cost_estimate=pl.CostEstimate(flops=flops, bytes_accessed=moved, transcendentals=0),
    )(values, response, *tables)


def gate_kernel(conv_ref, skip_ref, signal_ref, query_ref, out_ref):
    conv = conv_ref[...].astype(jnp.float32).T
    inner = conv + skip_ref[...] * signal_ref[...].astype(jnp.float32)
    out_ref[...] = (query_ref[...].astype(jnp.float32) * inner).astype(out_ref.dtype)


def gate(longconv, skip, lo, signal, query):
    chans, tok_rows = longconv.shape
    first = lo // LANES
    flat = pl.BlockSpec((tok_rows, LANES), lambda i: (0, i))
    return pl.pallas_call(
        gate_kernel,
        grid=(chans // LANES,),
        in_specs=[
            pl.BlockSpec((LANES, tok_rows), lambda i: (i, 0)),
            pl.BlockSpec((1, LANES), lambda i: (0, first + i)),
            flat,
            flat,
        ],
        out_specs=flat,
        out_shape=jax.ShapeDtypeStruct((tok_rows, chans), jnp.bfloat16),
        compiler_params=pltpu.CompilerParams(vmem_limit_bytes=8 * MIB),
        cost_estimate=pl.CostEstimate(flops=4 * chans * tok_rows, bytes_accessed=8 * chans * tok_rows, transcendentals=0),
    )(longconv, skip[None, :], signal, query)


def reorder_kernel(spec_ref, order_ref, out_ref):
    each = out_ref.shape[3]
    x = spec_ref[0].astype(jnp.bfloat16)
    y = jnp.dot(x, order_ref[...], preferred_element_type=jnp.float32).astype(jnp.bfloat16)
    for d in range(out_ref.shape[0]):
        out_ref[d, 0, 0] = y[d * each : (d + 1) * each]


def fold_kernel(got_ref, out_ref, came, held):
    seq_count, pairs, tok_rows = got_ref.shape[0], got_ref.shape[3], got_ref.shape[4]
    chans = pairs // 2
    runs = tok_rows // LANES
    rows = (seq_count + 1) * runs
    for part in range(2):
        sign = 1.0 if part == 0 else -1.0
        for s in range(seq_count):
            for r in range(runs):
                at = (s * runs + r) * pairs
                lanes = slice(r * LANES, (r + 1) * LANES)
                came[at : at + pairs, :] = got_ref[s, part, 0, :, lanes].astype(jnp.float32)
        for k1 in range(seq_count + 1):
            other = 2 * seq_count - k1
            for r in range(runs):
                value = came[pl.ds((k1 // 2 * runs + r) * pairs + k1 % 2, chans, stride=2), :]
                if k1 == seq_count:
                    value = sign * value
                elif k1 > 0:
                    value = value + sign * came[pl.ds((other // 2 * runs + r) * pairs + other % 2, chans, stride=2), :]
                held[pl.ds(k1 * runs + r, chans, stride=rows), :] = value
        out_ref[part] = held[...].reshape(chans, rows, LANES).astype(out_ref.dtype)


def reordered_spectrum(spectrum, seq_count, chunks):
    parts, chans, own, tok_rows = spectrum.shape
    runs = tok_rows // LANES
    size = chans // chunks
    each = size // seq_count
    col = lax.broadcasted_iota(jnp.int32, (tok_rows, tok_rows), 1)
    row = lax.broadcasted_iota(jnp.int32, (tok_rows, tok_rows), 0)
    wanted = col // LANES + runs * (col % LANES)
    wanted = jnp.where(lax.axis_index("seq") >= seq_count // 2, tok_rows - 1 - wanted, wanted)
    order = (row == wanted).astype(jnp.bfloat16)
    shape = (seq_count, parts, chunks, own * each, tok_rows)
    return pl.pallas_call(
        reorder_kernel,
        grid=(parts, chunks),
        in_specs=[
            pl.BlockSpec((1, own * size, tok_rows), lambda p, j: (p, j, 0)),
            pl.BlockSpec((tok_rows, tok_rows), lambda p, j: (0, 0)),
        ],
        out_specs=pl.BlockSpec((seq_count, 1, 1, own * each, tok_rows), lambda p, j: (0, p, j, 0, 0)),
        out_shape=jax.ShapeDtypeStruct(shape, jnp.bfloat16),
        compiler_params=pltpu.CompilerParams(vmem_limit_bytes=48 * MIB),
        cost_estimate=pl.CostEstimate(
            flops=2 * spectrum.size * tok_rows, bytes_accessed=6 * spectrum.size, transcendentals=0
        ),
    )(spectrum.reshape(parts, chans * own, tok_rows), order)


def folded_response(sent, own):
    seq_count, parts, chunks, pairs, tok_rows = sent.shape
    runs = tok_rows // LANES
    each = pairs // own
    got = lax.all_to_all(sent, "seq", split_axis=0, concat_axis=0, tiled=True)
    block = min(CHAN_BLOCK, each)
    rows = (seq_count + 1) * runs
    return pl.pallas_call(
        fold_kernel,
        grid=(chunks, each // block),
        in_specs=[pl.BlockSpec((seq_count, parts, 1, own * block, tok_rows), lambda j, i: (0, 0, j, i, 0))],
        out_specs=pl.BlockSpec((parts, block, rows, LANES), lambda j, i: (0, j * (each // block) + i, 0, 0)),
        out_shape=jax.ShapeDtypeStruct((parts, chunks * each, rows, LANES), jnp.bfloat16),
        scratch_shapes=[
            pltpu.VMEM((seq_count * runs * own * block, LANES), jnp.float32),
            pltpu.VMEM((block * rows, LANES), jnp.float32),
        ],
        compiler_params=pltpu.CompilerParams(vmem_limit_bytes=12 * MIB),
        cost_estimate=pl.CostEstimate(flops=sent.size, bytes_accessed=3 * sent.size, transcendentals=0),
    )(got)


def feature_rows(out_weight, seq_count):
    each = out_weight.shape[0] // seq_count
    own = lax.dynamic_slice_in_dim(out_weight, lax.axis_index("seq") * each, each, axis=0)
    own = lax.all_to_all(own, "chan", split_axis=1, concat_axis=0, tiled=True)
    return own.reshape(lax.axis_size("chan"), each, own.shape[1])


def combine_kernel(count, me_ref, *refs):
    before, after, weights = refs[:count], refs[count : 2 * count - 1], refs[2 * count - 1 : 3 * count - 1]
    out_ref = refs[-1]
    gated = [before[0][...]] + [before[k][...] + after[count - k - 1][...] for k in range(1, count)]
    weight = jnp.concatenate([ref[0, 0] for ref in weights], axis=0)
    total = jnp.dot(jnp.concatenate(gated, axis=1), weight, preferred_element_type=jnp.float32)
    if len(refs) == 3 * count + 1:
        total = total + refs[-2][...]
    out_ref[...] = total.astype(out_ref.dtype)


def combine(line, weight, chunk, total, dtype):
    before, after = line
    count = len(before)
    tok_rows, size = before[0].shape
    features = weight.shape[3]
    tile = min(4 * LANES, features)
    whole = pl.BlockSpec((tok_rows, size), lambda i, me: (0, 0))
    block = pl.BlockSpec((tok_rows, tile), lambda i, me: (0, i))
    given = [] if total is None else [total]
    me = lax.axis_index("chan").astype(jnp.int32).reshape(1)

    def weight_of(k):
        return pl.BlockSpec((1, 1, size, tile), lambda i, me: (chunk, slot_owner(me, k, count), 0, i))

    return pl.pallas_call(
        lambda *refs: combine_kernel(count, *refs),
        grid_spec=pltpu.PrefetchScalarGridSpec(
            num_scalar_prefetch=1,
            grid=(features // tile,),
            in_specs=[
                *[whole] * (2 * count - 1),
                *[weight_of(k) for k in range(count)],
                *[block for _ in given],
            ],
            out_specs=block,
        ),
        out_shape=jax.ShapeDtypeStruct((tok_rows, features), dtype),
        compiler_params=pltpu.CompilerParams(vmem_limit_bytes=56 * MIB),
        cost_estimate=pl.CostEstimate(
            flops=2 * tok_rows * size * count * features,
            bytes_accessed=2 * size * count * (tok_rows + features) + 6 * tok_rows * features,
            transcendentals=0,
        ),
    )(me, *before, *after, *[weight] * count, *given)


def shards(tokens, in_weight, conv_weight, spectrum, skip, out_weight):
    tok_rows, depth = tokens.shape
    seq_count = lax.axis_size("seq")
    chan_count = lax.axis_size("chan")
    chans = in_weight.shape[2]
    chunks = chunk_count(chans, seq_count)
    size = chans // chunks
    before, after = along_line(tokens, "chan")
    near = (before[1], after[0])
    *near, out_weight, last_rows, spectrum = lax.optimization_barrier(
        (*near, out_weight, tokens[tok_rows - HALO :], spectrum)
    )
    before[1], after[0] = near
    weight = feature_rows(out_weight, seq_count)
    halo = gather_by_doubling(from_behind(last_rows, "seq", 1), "chan")
    sent = reordered_spectrum(spectrum, seq_count, chunks)
    halo, sent, weight = lax.optimization_barrier((halo, sent, weight))
    response = folded_response(sent, spectrum.shape[2])
    weight = gather_by_doubling(weight, "seq")
    weight = weight.reshape((chunks, seq_count // chunks) + weight.shape[1:]).transpose(0, 2, 1, 3, 4)
    weight = weight.reshape(chunks, chan_count, size, weight.shape[4])
    halo = jnp.einsum(
        "ztd,pzdc->ptc",
        halo,
        in_weight.reshape(3, chan_count, depth, chans),
        preferred_element_type=jnp.float32,
    ).astype(jnp.bfloat16)
    total = None
    for j, lo in enumerate(range(0, chans, size)):
        given = ((before, after), in_weight, conv_weight, halo, lo, size, response, weight)
        query_t, signal, signal_t = project(*given)
        values = signal.reshape(seq_count, size // seq_count, tok_rows)
        values = lax.all_to_all(values, "seq", split_axis=0, concat_axis=0, tiled=True)
        longconv = lax.all_to_all(
            long_conv(values, response, lo // seq_count), "seq", split_axis=0, concat_axis=0, tiled=True
        ).reshape(size, tok_rows)
        gated = along_line(gate(longconv, skip, lo, signal_t, query_t), "chan")
        dtype = jnp.bfloat16 if lo + size == chans else jnp.float32
        total = combine(gated, weight, j, total, dtype)
    return total


def solution(mesh):
    placed = (
        P("seq", "chan"),
        P(None, None, "chan"),
        P(None, None, "chan"),
        P(None, "chan", "seq", None),
        P("chan"),
        P("chan", None),
    )
    return jax.shard_map(
        shards, mesh=mesh, in_specs=placed, out_specs=P("seq", "chan"), check_vma=False
    )
```

```python
import jax
import jax.numpy as jnp
import numpy as np
from jax import lax
from jax.experimental import pallas as pl
from jax.experimental.pallas import tpu as pltpu
from jax.sharding import PartitionSpec as P

TAPS = 3
LANES = 128
HALO = 16
CHAN_BLOCK = 16
CHUNKS = 2
MIB = 1024 * 1024


def from_behind(value, axis, by):
    size = lax.axis_size(axis)
    pairs = [(i, i + by) for i in range(size) if 0 <= i + by < size]
    return lax.ppermute(value, axis, pairs)


def along_line(value, axis):
    size = lax.axis_size(axis)
    before, after = [value], [value]
    for k in range(1, size):
        before.append(lax.ppermute(before[-1], axis, [(i, i + 1) for i in range(k - 1, size - 1)]))
        after.append(lax.ppermute(after[-1], axis, [(i, i - 1) for i in range(1, size - k + 1)]))
    return before, after[1:]


def gather_by_doubling(value, axis):
    size = lax.axis_size(axis)
    index = lax.axis_index(axis)
    held = value[None]
    bit = size // 2
    while bit >= 1:
        other = lax.ppermute(held, axis, [(i, i ^ bit) for i in range(size)])
        upper = (index // bit) % 2 == 1
        first = jnp.where(upper, other, held)
        second = jnp.where(upper, held, other)
        held = jnp.stack([first, second], axis=1).reshape((2 * held.shape[0],) + held.shape[1:])
        bit //= 2
    return held


def chunk_count(chans, seq_count):
    size = chans // CHUNKS
    return 1 if size % LANES or (size // seq_count) % CHAN_BLOCK else CHUNKS


def project_kernel(count, extras, me_ref, *refs):
    before_refs, after_refs = refs[:count], refs[count : 2 * count - 1]
    wq_ref, wk_ref, wv_ref, taps_ref, halo_ref = refs[2 * count - 1 : 2 * count + 4]
    query_t_ref, signal_ref, signal_t_ref, before, after, acc, sems = refs[2 * count + 4 + extras :]
    step = pl.program_id(0)
    rows, size = query_t_ref.shape
    copies = []
    for k in range(count):
        given = [pltpu.make_async_copy(before_refs[k], before.at[k], sems.at[2 * k])]
        if k > 0:
            given.append(pltpu.make_async_copy(after_refs[count - k - 1], after.at[k - 1], sems.at[2 * k + 1]))
        copies.append(given)

    def part(tokens):
        weight = jnp.concatenate([wq_ref[0], wk_ref[0], wv_ref[0]], axis=1)
        return jnp.dot(tokens, weight, preferred_element_type=jnp.float32)

    def filtered(p, r):
        lanes = slice(p * size, (p + 1) * size)
        total = taps_ref[0, p][None, :] * acc[pl.ds(HALO + r, LANES), lanes]
        for j in range(1, TAPS):
            total = total + taps_ref[j, p][None, :] * acc[pl.ds(HALO + r - j, LANES), lanes]
        return total

    @pl.when(step == 0)
    def _():
        for given in copies:
            for copy in given:
                copy.start()
        for p in range(3):
            acc[:HALO, p * size : (p + 1) * size] = halo_ref[p].astype(jnp.float32)

    for k in range(count):

        @pl.when(step == k)
        def _():
            for copy in copies[k]:
                copy.wait()

    @pl.when(step == 0)
    def _():
        acc[HALO:, :] = part(before[0])

    @pl.when(step > 0)
    def _():
        acc[HALO:, :] += part(before[step] + after[step - 1])

    @pl.when(step == count - 1)
    def _():
        acc[HALO:, :] = acc[HALO:, :].astype(jnp.bfloat16).astype(jnp.float32)
        for r in range(0, rows, LANES):
            query_t_ref[r : r + LANES, :] = filtered(0, r).astype(query_t_ref.dtype)
            signal = filtered(1, r) * filtered(2, r)
            signal_t_ref[r : r + LANES, :] = signal.astype(signal_t_ref.dtype)
            signal_ref[:, r : r + LANES] = signal.T.astype(signal_ref.dtype)


def slot_owner(me, k, count):
    return lax.rem(me[0] - k + count, count)


def project(line, in_weight, conv_weight, halo, lo, size, *following):
    before, after = line
    count = len(before)
    rows, step = before[0].shape
    at = lo // size
    flat = jax.ShapeDtypeStruct((rows, size), jnp.bfloat16)
    shapes = [flat, jax.ShapeDtypeStruct((size, rows), jnp.bfloat16), flat]
    me = lax.axis_index("chan").astype(jnp.int32).reshape(1)

    def weight_of(p):
        return pl.BlockSpec((1, step, size), lambda z, me: (p, slot_owner(me, z, count), at))

    anywhere = pl.BlockSpec(memory_space=pl.ANY)
    return pl.pallas_call(
        lambda *refs: project_kernel(count, len(following), *refs),
        grid_spec=pltpu.PrefetchScalarGridSpec(
            num_scalar_prefetch=1,
            grid=(count,),
            in_specs=[
                *[anywhere] * (2 * count - 1),
                *[weight_of(p) for p in range(3)],
                pl.BlockSpec((TAPS, 3, size), lambda z, me: (0, 0, at)),
                pl.BlockSpec((3, HALO, size), lambda z, me: (0, 0, at)),
                *[anywhere] * len(following),
            ],
            out_specs=[pl.BlockSpec(shape.shape, lambda z, me: (0, 0)) for shape in shapes],
            scratch_shapes=[
                pltpu.VMEM((count, rows, step), jnp.bfloat16),
                pltpu.VMEM((count - 1, rows, step), jnp.bfloat16),
                pltpu.VMEM((HALO + rows, 3 * size), jnp.float32),
                pltpu.SemaphoreType.DMA((2 * count,)),
            ],
        ),
        out_shape=shapes,
        compiler_params=pltpu.CompilerParams(vmem_limit_bytes=56 * MIB),
        cost_estimate=pl.CostEstimate(
            flops=2 * 3 * rows * count * step * size,
            bytes_accessed=2 * count * step * (3 * size + rows),
            transcendentals=0,
        ),
    )(me, *before, *after, in_weight, in_weight, in_weight, conv_weight, halo, *following)


def transform_tables(seq_count, tok_rows):
    runs = tok_rows // LANES
    wide = 2 * seq_count * runs
    fft_len = wide * LANES
    k1 = np.arange(seq_count + 1)[:, None]
    k2a = np.arange(runs)[None, :]
    ka = (k1 + 2 * seq_count * k2a).reshape(-1)
    a = np.arange(seq_count * runs)
    b = np.arange(LANES)
    outer = 2.0 * np.pi * ((ka[:, None] * a[None, :]) % wide) / wide
    first = np.concatenate([np.cos(outer), -np.sin(outer)], axis=0)
    last = first.T / fft_len
    turn = 2.0 * np.pi * ((ka[:, None] * b[None, :]) % fft_len) / fft_len
    inner = 2.0 * np.pi * ((b[:, None] * b[None, :]) % LANES) / LANES
    cos, sin = np.cos(inner), np.sin(inner)
    forward = np.block([[cos, -sin], [sin, cos]])
    backward = np.block([[cos, sin], [-sin, cos]])
    half = lambda table: jnp.asarray(table, jnp.bfloat16)
    full = lambda table: jnp.asarray(table, jnp.float32)
    return half(first), half(last), full(np.cos(turn)), full(np.sin(turn)), half(forward), half(backward)


def conv_kernel(signal_ref, resp_ref, first_ref, last_ref, cos_ref, sin_ref, fwd_ref, bwd_ref, out_ref, held, low, high):
    seq_count, block, tok_rows = signal_ref.shape
    runs = tok_rows // LANES
    span = seq_count * runs
    rows = cos_ref.shape[0]
    pair = 2 * rows
    for s in range(seq_count):
        for r in range(runs):
            piece = signal_ref[s, :, r * LANES : (r + 1) * LANES].astype(jnp.float32)
            held[pl.ds(s * runs + r, block, stride=span), :] = piece
    cos, sin = cos_ref[...], sin_ref[...]
    for c in range(0, block, 2):
        x = jnp.concatenate([held[c * span : (c + 1) * span, :], held[(c + 1) * span : (c + 2) * span, :]], axis=1)
        y = jnp.dot(first_ref[...], x.astype(jnp.bfloat16), preferred_element_type=jnp.float32)
        turned = []
        for half in (slice(0, LANES), slice(LANES, 2 * LANES)):
            re, im = y[:rows, half], y[rows:, half]
            turned.append(jnp.concatenate([re * cos + im * sin, im * cos - re * sin], axis=1))
        low[c * rows : c * rows + pair, :] = jnp.concatenate(turned, axis=0).astype(jnp.bfloat16)
    high[...] = jnp.dot(low[...], fwd_ref[...], preferred_element_type=jnp.float32)
    for c in range(0, block, 2):
        done = []
        for d in (c, c + 1):
            re = high[d * rows : (d + 1) * rows, :LANES]
            im = high[d * rows : (d + 1) * rows, LANES:]
            hr = resp_ref[0, d].astype(jnp.float32)
            hi = resp_ref[1, d].astype(jnp.float32)
            done.append(jnp.concatenate([re * hr - im * hi, re * hi + im * hr], axis=1))
        low[c * rows : c * rows + pair, :] = jnp.concatenate(done, axis=0).astype(jnp.bfloat16)
    high[...] = jnp.dot(low[...], bwd_ref[...], preferred_element_type=jnp.float32)
    for c in range(0, block, 2):
        turned = []
        for d in (c, c + 1):
            re = high[d * rows : (d + 1) * rows, :LANES]
            im = high[d * rows : (d + 1) * rows, LANES:]
            turned.append(jnp.concatenate([re * cos - im * sin, im * cos + re * sin], axis=0))
        w = jnp.concatenate(turned, axis=1).astype(jnp.bfloat16)
        y = jnp.dot(last_ref[...], w, preferred_element_type=jnp.float32)
        held[c * span : (c + 1) * span, :] = y[:, :LANES]
        held[(c + 1) * span : (c + 2) * span, :] = y[:, LANES:]
    for s in range(seq_count):
        for r in range(runs):
            piece = held[pl.ds(s * runs + r, block, stride=span), :]
            out_ref[s, :, r * LANES : (r + 1) * LANES] = piece.astype(out_ref.dtype)


def long_conv(values, response, start=0):
    seq_count, chans, tok_rows = values.shape
    rows = response.shape[2]
    block = min(CHAN_BLOCK, chans)
    tables = transform_tables(seq_count, tok_rows)
    fixed = [pl.BlockSpec(t.shape, lambda i: (0, 0)) for t in tables]
    span = seq_count * tok_rows // LANES
    flops = chans * 2 * (2 * 2 * rows * span * LANES + 2 * rows * 4 * LANES * LANES)
    moved = 2 * (2 * values.size + 2 * chans * rows * LANES)
    return pl.pallas_call(
        conv_kernel,
        grid=(chans // block,),
        in_specs=[
            pl.BlockSpec((seq_count, block, tok_rows), lambda i: (0, i, 0)),
            pl.BlockSpec((2, block, rows, LANES), lambda i: (0, start // block + i, 0, 0)),
            *fixed,
        ],
        out_specs=pl.BlockSpec((seq_count, block, tok_rows), lambda i: (0, i, 0)),
        out_shape=jax.ShapeDtypeStruct((seq_count, chans, tok_rows), jnp.bfloat16),
        scratch_shapes=[
            pltpu.VMEM((block * span, LANES), jnp.float32),
            pltpu.VMEM((block * rows, 2 * LANES), jnp.bfloat16),
            pltpu.VMEM((block * rows, 2 * LANES), jnp.float32),
        ],
        compiler_params=pltpu.CompilerParams(vmem_limit_bytes=12 * MIB),
        cost_estimate=pl.CostEstimate(flops=flops, bytes_accessed=moved, transcendentals=0),
    )(values, response, *tables)


def gate_kernel(conv_ref, skip_ref, signal_ref, query_ref, out_ref):
    conv = conv_ref[...].astype(jnp.float32).T
    inner = conv + skip_ref[...] * signal_ref[...].astype(jnp.float32)
    out_ref[...] = (query_ref[...].astype(jnp.float32) * inner).astype(out_ref.dtype)


def gate(longconv, skip, lo, signal, query):
    chans, tok_rows = longconv.shape
    first = lo // LANES
    flat = pl.BlockSpec((tok_rows, LANES), lambda i: (0, i))
    return pl.pallas_call(
        gate_kernel,
        grid=(chans // LANES,),
        in_specs=[
            pl.BlockSpec((LANES, tok_rows), lambda i: (i, 0)),
            pl.BlockSpec((1, LANES), lambda i: (0, first + i)),
            flat,
            flat,
        ],
        out_specs=flat,
        out_shape=jax.ShapeDtypeStruct((tok_rows, chans), jnp.bfloat16),
        compiler_params=pltpu.CompilerParams(vmem_limit_bytes=8 * MIB),
        cost_estimate=pl.CostEstimate(flops=4 * chans * tok_rows, bytes_accessed=8 * chans * tok_rows, transcendentals=0),
    )(longconv, skip[None, :], signal, query)


def reorder_kernel(spec_ref, order_ref, out_ref):
    each = out_ref.shape[3]
    x = spec_ref[0].astype(jnp.bfloat16)
    y = jnp.dot(x, order_ref[...], preferred_element_type=jnp.float32).astype(jnp.bfloat16)
    for d in range(out_ref.shape[0]):
        out_ref[d, 0, 0] = y[d * each : (d + 1) * each]


def fold_kernel(got_ref, out_ref, came, held):
    seq_count, pairs, tok_rows = got_ref.shape[0], got_ref.shape[3], got_ref.shape[4]
    chans = pairs // 2
    runs = tok_rows // LANES
    rows = (seq_count + 1) * runs
    for part in range(2):
        sign = 1.0 if part == 0 else -1.0
        for s in range(seq_count):
            for r in range(runs):
                at = (s * runs + r) * pairs
                lanes = slice(r * LANES, (r + 1) * LANES)
                came[at : at + pairs, :] = got_ref[s, part, 0, :, lanes].astype(jnp.float32)
        for k1 in range(seq_count + 1):
            other = 2 * seq_count - k1
            for r in range(runs):
                value = came[pl.ds((k1 // 2 * runs + r) * pairs + k1 % 2, chans, stride=2), :]
                if k1 == seq_count:
                    value = sign * value
                elif k1 > 0:
                    value = value + sign * came[pl.ds((other // 2 * runs + r) * pairs + other % 2, chans, stride=2), :]
                held[pl.ds(k1 * runs + r, chans, stride=rows), :] = value
        out_ref[part] = held[...].reshape(chans, rows, LANES).astype(out_ref.dtype)


def reordered_spectrum(spectrum, seq_count, chunks):
    parts, chans, own, tok_rows = spectrum.shape
    runs = tok_rows // LANES
    size = chans // chunks
    each = size // seq_count
    col = lax.broadcasted_iota(jnp.int32, (tok_rows, tok_rows), 1)
    row = lax.broadcasted_iota(jnp.int32, (tok_rows, tok_rows), 0)
    wanted = col // LANES + runs * (col % LANES)
    wanted = jnp.where(lax.axis_index("seq") >= seq_count // 2, tok_rows - 1 - wanted, wanted)
    order = (row == wanted).astype(jnp.bfloat16)
    shape = (seq_count, parts, chunks, own * each, tok_rows)
    return pl.pallas_call(
        reorder_kernel,
        grid=(parts, chunks),
        in_specs=[
            pl.BlockSpec((1, own * size, tok_rows), lambda p, j: (p, j, 0)),
            pl.BlockSpec((tok_rows, tok_rows), lambda p, j: (0, 0)),
        ],
        out_specs=pl.BlockSpec((seq_count, 1, 1, own * each, tok_rows), lambda p, j: (0, p, j, 0, 0)),
        out_shape=jax.ShapeDtypeStruct(shape, jnp.bfloat16),
        compiler_params=pltpu.CompilerParams(vmem_limit_bytes=48 * MIB),
        cost_estimate=pl.CostEstimate(
            flops=2 * spectrum.size * tok_rows, bytes_accessed=6 * spectrum.size, transcendentals=0
        ),
    )(spectrum.reshape(parts, chans * own, tok_rows), order)


def folded_response(sent, own):
    seq_count, parts, chunks, pairs, tok_rows = sent.shape
    runs = tok_rows // LANES
    each = pairs // own
    got = lax.all_to_all(sent, "seq", split_axis=0, concat_axis=0, tiled=True)
    block = min(CHAN_BLOCK, each)
    rows = (seq_count + 1) * runs
    return pl.pallas_call(
        fold_kernel,
        grid=(chunks, each // block),
        in_specs=[pl.BlockSpec((seq_count, parts, 1, own * block, tok_rows), lambda j, i: (0, 0, j, i, 0))],
        out_specs=pl.BlockSpec((parts, block, rows, LANES), lambda j, i: (0, j * (each // block) + i, 0, 0)),
        out_shape=jax.ShapeDtypeStruct((parts, chunks * each, rows, LANES), jnp.bfloat16),
        scratch_shapes=[
            pltpu.VMEM((seq_count * runs * own * block, LANES), jnp.float32),
            pltpu.VMEM((block * rows, LANES), jnp.float32),
        ],
        compiler_params=pltpu.CompilerParams(vmem_limit_bytes=12 * MIB),
        cost_estimate=pl.CostEstimate(flops=sent.size, bytes_accessed=3 * sent.size, transcendentals=0),
    )(got)


def feature_rows(out_weight, seq_count):
    each = out_weight.shape[0] // seq_count
    own = lax.dynamic_slice_in_dim(out_weight, lax.axis_index("seq") * each, each, axis=0)
    own = lax.all_to_all(own, "chan", split_axis=1, concat_axis=0, tiled=True)
    return own.reshape(lax.axis_size("chan"), each, own.shape[1])


def combine_kernel(count, me_ref, *refs):
    before, after, weights = refs[:count], refs[count : 2 * count - 1], refs[2 * count - 1 : 3 * count - 1]
    out_ref = refs[-1]
    gated = [before[0][...]] + [before[k][...] + after[count - k - 1][...] for k in range(1, count)]
    weight = jnp.concatenate([ref[0, 0] for ref in weights], axis=0)
    total = jnp.dot(jnp.concatenate(gated, axis=1), weight, preferred_element_type=jnp.float32)
    if len(refs) == 3 * count + 1:
        total = total + refs[-2][...]
    out_ref[...] = total.astype(out_ref.dtype)


def combine(line, weight, chunk, total, dtype):
    before, after = line
    count = len(before)
    tok_rows, size = before[0].shape
    features = weight.shape[3]
    tile = min(4 * LANES, features)
    whole = pl.BlockSpec((tok_rows, size), lambda i, me: (0, 0))
    block = pl.BlockSpec((tok_rows, tile), lambda i, me: (0, i))
    given = [] if total is None else [total]
    me = lax.axis_index("chan").astype(jnp.int32).reshape(1)

    def weight_of(k):
        return pl.BlockSpec((1, 1, size, tile), lambda i, me: (chunk, slot_owner(me, k, count), 0, i))

    return pl.pallas_call(
        lambda *refs: combine_kernel(count, *refs),
        grid_spec=pltpu.PrefetchScalarGridSpec(
            num_scalar_prefetch=1,
            grid=(features // tile,),
            in_specs=[
                *[whole] * (2 * count - 1),
                *[weight_of(k) for k in range(count)],
                *[block for _ in given],
            ],
            out_specs=block,
        ),
        out_shape=jax.ShapeDtypeStruct((tok_rows, features), dtype),
        compiler_params=pltpu.CompilerParams(vmem_limit_bytes=56 * MIB),
        cost_estimate=pl.CostEstimate(
            flops=2 * tok_rows * size * count * features,
            bytes_accessed=2 * size * count * (tok_rows + features) + 6 * tok_rows * features,
            transcendentals=0,
        ),
    )(me, *before, *after, *[weight] * count, *given)


def shards(tokens, in_weight, conv_weight, spectrum, skip, out_weight):
    tok_rows, depth = tokens.shape
    seq_count = lax.axis_size("seq")
    chan_count = lax.axis_size("chan")
    chans = in_weight.shape[2]
    chunks = chunk_count(chans, seq_count)
    size = chans // chunks
    before, after = along_line(tokens, "chan")
    near = (before[1], after[0])
    weight = feature_rows(out_weight, seq_count)
    halo = gather_by_doubling(from_behind(tokens[tok_rows - HALO :], "seq", 1), "chan")
    *near, spectrum = lax.optimization_barrier((*near, spectrum))
    before[1], after[0] = near
    sent = reordered_spectrum(spectrum, seq_count, chunks)
    response = folded_response(sent, spectrum.shape[2])
    weight = gather_by_doubling(weight, "seq")
    weight = weight.reshape((chunks, seq_count // chunks) + weight.shape[1:]).transpose(0, 2, 1, 3, 4)
    weight = weight.reshape(chunks, chan_count, size, weight.shape[4])
    halo = jnp.einsum(
        "ztd,pzdc->ptc",
        halo,
        in_weight.reshape(3, chan_count, depth, chans),
        preferred_element_type=jnp.float32,
    ).astype(jnp.bfloat16)
    total = None
    for j, lo in enumerate(range(0, chans, size)):
        given = ((before, after), in_weight, conv_weight, halo, lo, size, response, weight)
        query_t, signal, signal_t = project(*given)
        values = signal.reshape(seq_count, size // seq_count, tok_rows)
        values = lax.all_to_all(values, "seq", split_axis=0, concat_axis=0, tiled=True)
        longconv = lax.all_to_all(
            long_conv(values, response, lo // seq_count), "seq", split_axis=0, concat_axis=0, tiled=True
        ).reshape(size, tok_rows)
        gated = along_line(gate(longconv, skip, lo, signal_t, query_t), "chan")
        dtype = jnp.bfloat16 if lo + size == chans else jnp.float32
        total = combine(gated, weight, j, total, dtype)
    return total


def solution(mesh):
    placed = (
        P("seq", "chan"),
        P(None, None, "chan"),
        P(None, None, "chan"),
        P(None, "chan", "seq", None),
        P("chan"),
        P("chan", None),
    )
    return jax.shard_map(
        shards, mesh=mesh, in_specs=placed, out_specs=P("seq", "chan"), check_vma=False
    )
```

```python
import jax
import jax.numpy as jnp
import numpy as np
from jax import lax
from jax.experimental import pallas as pl
from jax.experimental.pallas import tpu as pltpu
from jax.sharding import PartitionSpec as P

TAPS = 3
LANES = 128
HALO = 16
CHAN_BLOCK = 16
CHUNKS = 2
MIB = 1024 * 1024


def from_behind(value, axis, by):
    size = lax.axis_size(axis)
    pairs = [(i, i + by) for i in range(size) if 0 <= i + by < size]
    return lax.ppermute(value, axis, pairs)


def gather_by_doubling(value, axis):
    size = lax.axis_size(axis)
    index = lax.axis_index(axis)
    held = value[None]
    bit = size // 2
    while bit >= 1:
        other = lax.ppermute(held, axis, [(i, i ^ bit) for i in range(size)])
        upper = (index // bit) % 2 == 1
        first = jnp.where(upper, other, held)
        second = jnp.where(upper, held, other)
        held = jnp.stack([first, second], axis=1).reshape((2 * held.shape[0],) + held.shape[1:])
        bit //= 2
    return held


def chunk_count(chans, seq_count):
    size = chans // CHUNKS
    return 1 if size % LANES or (size // seq_count) % CHAN_BLOCK else CHUNKS


def project_kernel(streams, extras, tok_ref, *refs):
    w_refs, taps_ref, halo_ref = refs[: len(streams)], refs[len(streams)], refs[len(streams) + 1]
    outs, acc = refs[len(streams) + 2 + extras : -1], refs[-1]
    step = pl.program_id(0)
    last = pl.num_programs(0) - 1
    rows = acc.shape[1] - HALO

    def part(w_ref):
        return jnp.dot(tok_ref[0], w_ref[0], preferred_element_type=jnp.float32)

    @pl.when(step == 0)
    def _():
        for i, p in enumerate(streams):
            acc[i, :HALO, :] = halo_ref[p].astype(jnp.float32)
            acc[i, HALO:, :] = part(w_refs[i])

    @pl.when(jnp.logical_and(step > 0, step < last))
    def _():
        for i in range(len(streams)):
            acc[i, HALO:, :] += part(w_refs[i])

    @pl.when(step == last)
    def _():
        for i in range(len(streams)):
            acc[i, HALO:, :] = (acc[i, HALO:, :] + part(w_refs[i])).astype(jnp.bfloat16).astype(jnp.float32)
        for r in range(0, rows, LANES):
            made = {}
            for i, p in enumerate(streams):
                total = taps_ref[0, p][None, :] * acc[i, pl.ds(HALO + r, LANES), :]
                for j in range(1, TAPS):
                    total = total + taps_ref[j, p][None, :] * acc[i, pl.ds(HALO + r - j, LANES), :]
                made[p] = total
            if 0 in made:
                outs[0][r : r + LANES, :] = made[0].astype(outs[0].dtype)
            if 1 in made:
                signal = made[1] * made[2]
                outs[-1][r : r + LANES, :] = signal.astype(outs[-1].dtype)
                outs[-2][:, r : r + LANES] = signal.T.astype(outs[-2].dtype)


def project(streams, gathered, in_weight, conv_weight, halo, lo, size, *after):
    count, rows, step = gathered.shape
    depth = count * step
    at = lo // size
    flat = jax.ShapeDtypeStruct((rows, size), jnp.bfloat16)
    shapes = ([flat] if 0 in streams else []) + (
        [jax.ShapeDtypeStruct((size, rows), jnp.bfloat16), flat] if 1 in streams else []
    )

    def weight_of(p):
        return pl.BlockSpec((1, step, size), lambda z: (p, z, at))

    return pl.pallas_call(
        lambda *refs: project_kernel(streams, len(after), *refs),
        grid=(count,),
        in_specs=[
            pl.BlockSpec((1, rows, step), lambda z: (z, 0, 0)),
            *[weight_of(p) for p in streams],
            pl.BlockSpec((TAPS, 3, size), lambda z: (0, 0, at)),
            pl.BlockSpec((3, HALO, size), lambda z: (0, 0, at)),
            *[pl.BlockSpec(memory_space=pl.ANY) for _ in after],
        ],
        out_specs=[pl.BlockSpec(shape.shape, lambda z: (0, 0)) for shape in shapes],
        out_shape=shapes,
        scratch_shapes=[pltpu.VMEM((len(streams), HALO + rows, size), jnp.float32)],
        compiler_params=pltpu.CompilerParams(vmem_limit_bytes=48 * MIB),
        cost_estimate=pl.CostEstimate(
            flops=2 * len(streams) * rows * depth * size,
            bytes_accessed=2 * depth * (len(streams) * size + rows),
            transcendentals=0,
        ),
    )(gathered, *[in_weight] * len(streams), conv_weight, halo, *after)


def transform_tables(seq_count, tok_rows):
    runs = tok_rows // LANES
    wide = 2 * seq_count * runs
    fft_len = wide * LANES
    k1 = np.arange(seq_count + 1)[:, None]
    k2a = np.arange(runs)[None, :]
    ka = (k1 + 2 * seq_count * k2a).reshape(-1)
    a = np.arange(seq_count * runs)
    b = np.arange(LANES)
    outer = 2.0 * np.pi * ((ka[:, None] * a[None, :]) % wide) / wide
    first = np.concatenate([np.cos(outer), -np.sin(outer)], axis=0)
    last = first.T / fft_len
    turn = 2.0 * np.pi * ((ka[:, None] * b[None, :]) % fft_len) / fft_len
    inner = 2.0 * np.pi * ((b[:, None] * b[None, :]) % LANES) / LANES
    cos, sin = np.cos(inner), np.sin(inner)
    forward = np.block([[cos, -sin], [sin, cos]])
    backward = np.block([[cos, sin], [-sin, cos]])
    half = lambda table: jnp.asarray(table, jnp.bfloat16)
    full = lambda table: jnp.asarray(table, jnp.float32)
    return half(first), half(last), full(np.cos(turn)), full(np.sin(turn)), half(forward), half(backward)


def conv_kernel(signal_ref, resp_ref, first_ref, last_ref, cos_ref, sin_ref, fwd_ref, bwd_ref, out_ref, held, low, high):
    seq_count, block, tok_rows = signal_ref.shape
    runs = tok_rows // LANES
    span = seq_count * runs
    rows = cos_ref.shape[0]
    pair = 2 * rows
    for s in range(seq_count):
        for r in range(runs):
            piece = signal_ref[s, :, r * LANES : (r + 1) * LANES].astype(jnp.float32)
            held[pl.ds(s * runs + r, block, stride=span), :] = piece
    cos, sin = cos_ref[...], sin_ref[...]
    for c in range(0, block, 2):
        x = jnp.concatenate([held[c * span : (c + 1) * span, :], held[(c + 1) * span : (c + 2) * span, :]], axis=1)
        y = jnp.dot(first_ref[...], x.astype(jnp.bfloat16), preferred_element_type=jnp.float32)
        turned = []
        for half in (slice(0, LANES), slice(LANES, 2 * LANES)):
            re, im = y[:rows, half], y[rows:, half]
            turned.append(jnp.concatenate([re * cos + im * sin, im * cos - re * sin], axis=1))
        low[c * rows : c * rows + pair, :] = jnp.concatenate(turned, axis=0).astype(jnp.bfloat16)
    high[...] = jnp.dot(low[...], fwd_ref[...], preferred_element_type=jnp.float32)
    for c in range(0, block, 2):
        done = []
        for d in (c, c + 1):
            re = high[d * rows : (d + 1) * rows, :LANES]
            im = high[d * rows : (d + 1) * rows, LANES:]
            hr = resp_ref[0, d].astype(jnp.float32)
            hi = resp_ref[1, d].astype(jnp.float32)
            done.append(jnp.concatenate([re * hr - im * hi, re * hi + im * hr], axis=1))
        low[c * rows : c * rows + pair, :] = jnp.concatenate(done, axis=0).astype(jnp.bfloat16)
    high[...] = jnp.dot(low[...], bwd_ref[...], preferred_element_type=jnp.float32)
    for c in range(0, block, 2):
        turned = []
        for d in (c, c + 1):
            re = high[d * rows : (d + 1) * rows, :LANES]
            im = high[d * rows : (d + 1) * rows, LANES:]
            turned.append(jnp.concatenate([re * cos - im * sin, im * cos + re * sin], axis=0))
        w = jnp.concatenate(turned, axis=1).astype(jnp.bfloat16)
        y = jnp.dot(last_ref[...], w, preferred_element_type=jnp.float32)
        held[c * span : (c + 1) * span, :] = y[:, :LANES]
        held[(c + 1) * span : (c + 2) * span, :] = y[:, LANES:]
    for s in range(seq_count):
        for r in range(runs):
            piece = held[pl.ds(s * runs + r, block, stride=span), :]
            out_ref[s, :, r * LANES : (r + 1) * LANES] = piece.astype(out_ref.dtype)


def long_conv(values, response, start=0):
    seq_count, chans, tok_rows = values.shape
    rows = response.shape[2]
    block = min(CHAN_BLOCK, chans)
    tables = transform_tables(seq_count, tok_rows)
    fixed = [pl.BlockSpec(t.shape, lambda i: (0, 0)) for t in tables]
    span = seq_count * tok_rows // LANES
    flops = chans * 2 * (2 * 2 * rows * span * LANES + 2 * rows * 4 * LANES * LANES)
    moved = 2 * (2 * values.size + 2 * chans * rows * LANES)
    return pl.pallas_call(
        conv_kernel,
        grid=(chans // block,),
        in_specs=[
            pl.BlockSpec((seq_count, block, tok_rows), lambda i: (0, i, 0)),
            pl.BlockSpec((2, block, rows, LANES), lambda i: (0, start // block + i, 0, 0)),
            *fixed,
        ],
        out_specs=pl.BlockSpec((seq_count, block, tok_rows), lambda i: (0, i, 0)),
        out_shape=jax.ShapeDtypeStruct((seq_count, chans, tok_rows), jnp.bfloat16),
        scratch_shapes=[
            pltpu.VMEM((block * span, LANES), jnp.float32),
            pltpu.VMEM((block * rows, 2 * LANES), jnp.bfloat16),
            pltpu.VMEM((block * rows, 2 * LANES), jnp.float32),
        ],
        compiler_params=pltpu.CompilerParams(vmem_limit_bytes=12 * MIB),
        cost_estimate=pl.CostEstimate(flops=flops, bytes_accessed=moved, transcendentals=0),
    )(values, response, *tables)


def gate_kernel(conv_ref, skip_ref, signal_ref, query_ref, out_ref):
    conv = conv_ref[...].astype(jnp.float32).T
    inner = conv + skip_ref[...] * signal_ref[...].astype(jnp.float32)
    out_ref[...] = (query_ref[...].astype(jnp.float32) * inner).astype(out_ref.dtype)


def gate(longconv, skip, lo, signal, query):
    chans, tok_rows = longconv.shape
    first = lo // LANES
    flat = pl.BlockSpec((tok_rows, LANES), lambda i: (0, i))
    return pl.pallas_call(
        gate_kernel,
        grid=(chans // LANES,),
        in_specs=[
            pl.BlockSpec((LANES, tok_rows), lambda i: (i, 0)),
            pl.BlockSpec((1, LANES), lambda i: (0, first + i)),
            flat,
            flat,
        ],
        out_specs=flat,
        out_shape=jax.ShapeDtypeStruct((tok_rows, chans), jnp.bfloat16),
        compiler_params=pltpu.CompilerParams(vmem_limit_bytes=8 * MIB),
        cost_estimate=pl.CostEstimate(flops=4 * chans * tok_rows, bytes_accessed=8 * chans * tok_rows, transcendentals=0),
    )(longconv, skip[None, :], signal, query)


def reorder_kernel(spec_ref, order_ref, out_ref):
    each = out_ref.shape[3]
    x = spec_ref[0].astype(jnp.bfloat16)
    y = jnp.dot(x, order_ref[...], preferred_element_type=jnp.float32).astype(jnp.bfloat16)
    for d in range(out_ref.shape[0]):
        out_ref[d, 0, 0] = y[d * each : (d + 1) * each]


def fold_kernel(got_ref, out_ref, came, held):
    seq_count, pairs, tok_rows = got_ref.shape[0], got_ref.shape[3], got_ref.shape[4]
    chans = pairs // 2
    runs = tok_rows // LANES
    rows = (seq_count + 1) * runs
    for part in range(2):
        sign = 1.0 if part == 0 else -1.0
        for s in range(seq_count):
            for r in range(runs):
                at = (s * runs + r) * pairs
                lanes = slice(r * LANES, (r + 1) * LANES)
                came[at : at + pairs, :] = got_ref[s, part, 0, :, lanes].astype(jnp.float32)
        for k1 in range(seq_count + 1):
            other = 2 * seq_count - k1
            for r in range(runs):
                value = came[pl.ds((k1 // 2 * runs + r) * pairs + k1 % 2, chans, stride=2), :]
                if k1 == seq_count:
                    value = sign * value
                elif k1 > 0:
                    value = value + sign * came[pl.ds((other // 2 * runs + r) * pairs + other % 2, chans, stride=2), :]
                held[pl.ds(k1 * runs + r, chans, stride=rows), :] = value
        out_ref[part] = held[...].reshape(chans, rows, LANES).astype(out_ref.dtype)


def reordered_spectrum(spectrum, seq_count, chunks):
    parts, chans, own, tok_rows = spectrum.shape
    runs = tok_rows // LANES
    size = chans // chunks
    each = size // seq_count
    col = lax.broadcasted_iota(jnp.int32, (tok_rows, tok_rows), 1)
    row = lax.broadcasted_iota(jnp.int32, (tok_rows, tok_rows), 0)
    wanted = col // LANES + runs * (col % LANES)
    wanted = jnp.where(lax.axis_index("seq") >= seq_count // 2, tok_rows - 1 - wanted, wanted)
    order = (row == wanted).astype(jnp.bfloat16)
    shape = (seq_count, parts, chunks, own * each, tok_rows)
    return pl.pallas_call(
        reorder_kernel,
        grid=(parts, chunks),
        in_specs=[
            pl.BlockSpec((1, own * size, tok_rows), lambda p, j: (p, j, 0)),
            pl.BlockSpec((tok_rows, tok_rows), lambda p, j: (0, 0)),
        ],
        out_specs=pl.BlockSpec((seq_count, 1, 1, own * each, tok_rows), lambda p, j: (0, p, j, 0, 0)),
        out_shape=jax.ShapeDtypeStruct(shape, jnp.bfloat16),
        compiler_params=pltpu.CompilerParams(vmem_limit_bytes=48 * MIB),
        cost_estimate=pl.CostEstimate(
            flops=2 * spectrum.size * tok_rows, bytes_accessed=6 * spectrum.size, transcendentals=0
        ),
    )(spectrum.reshape(parts, chans * own, tok_rows), order)


def folded_response(sent, own):
    seq_count, parts, chunks, pairs, tok_rows = sent.shape
    runs = tok_rows // LANES
    each = pairs // own
    got = lax.all_to_all(sent, "seq", split_axis=0, concat_axis=0, tiled=True)
    block = min(CHAN_BLOCK, each)
    rows = (seq_count + 1) * runs
    return pl.pallas_call(
        fold_kernel,
        grid=(chunks, each // block),
        in_specs=[pl.BlockSpec((seq_count, parts, 1, own * block, tok_rows), lambda j, i: (0, 0, j, i, 0))],
        out_specs=pl.BlockSpec((parts, block, rows, LANES), lambda j, i: (0, j * (each // block) + i, 0, 0)),
        out_shape=jax.ShapeDtypeStruct((parts, chunks * each, rows, LANES), jnp.bfloat16),
        scratch_shapes=[
            pltpu.VMEM((seq_count * runs * own * block, LANES), jnp.float32),
            pltpu.VMEM((block * rows, LANES), jnp.float32),
        ],
        compiler_params=pltpu.CompilerParams(vmem_limit_bytes=12 * MIB),
        cost_estimate=pl.CostEstimate(flops=sent.size, bytes_accessed=3 * sent.size, transcendentals=0),
    )(got)


def feature_rows(out_weight, seq_count):
    each = out_weight.shape[0] // seq_count
    own = lax.dynamic_slice_in_dim(out_weight, lax.axis_index("seq") * each, each, axis=0)
    own = lax.all_to_all(own, "chan", split_axis=1, concat_axis=0, tiled=True)
    return own.reshape(lax.axis_size("chan"), each, own.shape[1])


def combine_kernel(gated_ref, w_ref, *refs):
    out_ref = refs[-1]
    gated = jnp.concatenate([gated_ref[z] for z in range(gated_ref.shape[0])], axis=1)
    total = jnp.dot(gated, w_ref[0], preferred_element_type=jnp.float32)
    if len(refs) == 2:
        total = total + refs[0][...].astype(jnp.float32)
    out_ref[...] = total.astype(out_ref.dtype)


def combine(gathered, weight, chunk, total):
    count, tok_rows, size = gathered.shape
    depth = count * size
    features = weight.shape[2]
    tile = min(4 * LANES, features)
    block = pl.BlockSpec((tok_rows, tile), lambda i: (0, i))
    given = [] if total is None else [total]
    return pl.pallas_call(
        combine_kernel,
        grid=(features // tile,),
        in_specs=[
            pl.BlockSpec((count, tok_rows, size), lambda i: (0, 0, 0)),
            pl.BlockSpec((1, depth, tile), lambda i: (chunk, 0, i)),
            *[block for _ in given],
        ],
        out_specs=block,
        out_shape=jax.ShapeDtypeStruct((tok_rows, features), jnp.bfloat16),
        compiler_params=pltpu.CompilerParams(vmem_limit_bytes=60 * MIB),
        cost_estimate=pl.CostEstimate(
            flops=2 * tok_rows * depth * features,
            bytes_accessed=2 * depth * (tok_rows + features) + 6 * tok_rows * features,
            transcendentals=0,
        ),
    )(gathered, weight, *given)


def shards(tokens, in_weight, conv_weight, spectrum, skip, out_weight):
    tok_rows, depth = tokens.shape
    seq_count = lax.axis_size("seq")
    chan_count = lax.axis_size("chan")
    chans = in_weight.shape[2]
    chunks = chunk_count(chans, seq_count)
    size = chans // chunks
    gathered = lax.all_gather(tokens, "chan")
    weight = feature_rows(out_weight, seq_count)
    last_rows = tokens[tok_rows - HALO :]
    weight, last_rows = lax.optimization_barrier((weight, last_rows))
    halo = gather_by_doubling(from_behind(last_rows, "seq", 1), "chan")
    sent = reordered_spectrum(spectrum, seq_count, chunks)
    halo, sent, weight = lax.optimization_barrier((halo, sent, weight))
    response = folded_response(sent, spectrum.shape[2])
    weight = gather_by_doubling(weight, "seq")
    weight = weight.reshape((chunks, seq_count // chunks) + weight.shape[1:]).transpose(0, 2, 1, 3, 4)
    weight = weight.reshape(chunks, chan_count * size, weight.shape[4])
    halo = jnp.einsum(
        "ztd,pzdc->ptc",
        halo,
        in_weight.reshape(3, chan_count, depth, chans),
        preferred_element_type=jnp.float32,
    ).astype(jnp.bfloat16)
    total = None
    for j, lo in enumerate(range(0, chans, size)):
        given = (gathered, in_weight, conv_weight, halo, lo, size, response, weight)
        if lo == 0 and chunks > 1:
            signal, signal_t = project((1, 2), *given)
            (query_t,) = project((0,), *given)
        else:
            query_t, signal, signal_t = project((0, 1, 2), *given)
        values = signal.reshape(seq_count, size // seq_count, tok_rows)
        values = lax.all_to_all(values, "seq", split_axis=0, concat_axis=0, tiled=True)
        longconv = lax.all_to_all(
            long_conv(values, response, lo // seq_count), "seq", split_axis=0, concat_axis=0, tiled=True
        ).reshape(size, tok_rows)
        gated = lax.all_gather(gate(longconv, skip, lo, signal_t, query_t), "chan")
        total = combine(gated, weight, j, total)
    return total


def solution(mesh):
    placed = (
        P("seq", "chan"),
        P(None, None, "chan"),
        P(None, None, "chan"),
        P(None, "chan", "seq", None),
        P("chan"),
        P("chan", None),
    )
    return jax.shard_map(
        shards, mesh=mesh, in_specs=placed, out_specs=P("seq", "chan"), check_vma=False
    )
```

```python
import jax
import jax.numpy as jnp
import numpy as np
from jax import lax
from jax.experimental import pallas as pl
from jax.experimental.pallas import tpu as pltpu
from jax.sharding import PartitionSpec as P

TAPS = 3
LANES = 128
HALO = 16
CHAN_BLOCK = 16
CHUNKS = 2
MIB = 1024 * 1024


def from_behind(value, axis, by):
    size = lax.axis_size(axis)
    pairs = [(i, i + by) for i in range(size) if 0 <= i + by < size]
    return lax.ppermute(value, axis, pairs)


def gather_by_doubling(value, axis):
    size = lax.axis_size(axis)
    index = lax.axis_index(axis)
    held = value[None]
    bit = size // 2
    while bit >= 1:
        other = lax.ppermute(held, axis, [(i, i ^ bit) for i in range(size)])
        upper = (index // bit) % 2 == 1
        first = jnp.where(upper, other, held)
        second = jnp.where(upper, held, other)
        held = jnp.stack([first, second], axis=1).reshape((2 * held.shape[0],) + held.shape[1:])
        bit //= 2
    return held


def chunk_count(chans, seq_count):
    size = chans // CHUNKS
    return 1 if size % LANES or (size // seq_count) % CHAN_BLOCK else CHUNKS


def project_kernel(extras, tok_ref, wq_ref, wk_ref, wv_ref, taps_ref, halo_ref, *rest):
    query_t_ref, signal_ref, signal_t_ref, acc = rest[extras:]
    step = pl.program_id(0)
    last = pl.num_programs(0) - 1
    rows, size = query_t_ref.shape

    def part():
        weight = jnp.concatenate([wq_ref[0], wk_ref[0], wv_ref[0]], axis=1)
        return jnp.dot(tok_ref[0], weight, preferred_element_type=jnp.float32)

    def filtered(p, r):
        lanes = slice(p * size, (p + 1) * size)
        total = taps_ref[0, p][None, :] * acc[pl.ds(HALO + r, LANES), lanes]
        for j in range(1, TAPS):
            total = total + taps_ref[j, p][None, :] * acc[pl.ds(HALO + r - j, LANES), lanes]
        return total

    @pl.when(step == 0)
    def _():
        for p in range(3):
            acc[:HALO, p * size : (p + 1) * size] = halo_ref[p].astype(jnp.float32)
        acc[HALO:, :] = part()

    @pl.when(jnp.logical_and(step > 0, step < last))
    def _():
        acc[HALO:, :] += part()

    @pl.when(step == last)
    def _():
        acc[HALO:, :] = (acc[HALO:, :] + part()).astype(jnp.bfloat16).astype(jnp.float32)
        for r in range(0, rows, LANES):
            query_t_ref[r : r + LANES, :] = filtered(0, r).astype(query_t_ref.dtype)
            signal = filtered(1, r) * filtered(2, r)
            signal_t_ref[r : r + LANES, :] = signal.astype(signal_t_ref.dtype)
            signal_ref[:, r : r + LANES] = signal.T.astype(signal_ref.dtype)


def project(gathered, in_weight, conv_weight, halo, lo, size, *after):
    count, rows, step = gathered.shape
    at = lo // size
    flat = jax.ShapeDtypeStruct((rows, size), jnp.bfloat16)
    shapes = [flat, jax.ShapeDtypeStruct((size, rows), jnp.bfloat16), flat]

    def weight_of(p):
        return pl.BlockSpec((1, step, size), lambda z: (p, z, at))

    return pl.pallas_call(
        lambda *refs: project_kernel(len(after), *refs),
        grid=(count,),
        in_specs=[
            pl.BlockSpec((1, rows, step), lambda z: (z, 0, 0)),
            *[weight_of(p) for p in range(3)],
            pl.BlockSpec((TAPS, 3, size), lambda z: (0, 0, at)),
            pl.BlockSpec((3, HALO, size), lambda z: (0, 0, at)),
            *[pl.BlockSpec(memory_space=pl.ANY) for _ in after],
        ],
        out_specs=[pl.BlockSpec(shape.shape, lambda z: (0, 0)) for shape in shapes],
        out_shape=shapes,
        scratch_shapes=[pltpu.VMEM((HALO + rows, 3 * size), jnp.float32)],
        compiler_params=pltpu.CompilerParams(vmem_limit_bytes=48 * MIB),
        cost_estimate=pl.CostEstimate(
            flops=2 * 3 * rows * count * step * size,
            bytes_accessed=2 * count * step * (3 * size + rows),
            transcendentals=0,
        ),
    )(gathered, in_weight, in_weight, in_weight, conv_weight, halo, *after)


def transform_tables(seq_count, tok_rows):
    runs = tok_rows // LANES
    wide = 2 * seq_count * runs
    fft_len = wide * LANES
    k1 = np.arange(seq_count + 1)[:, None]
    k2a = np.arange(runs)[None, :]
    ka = (k1 + 2 * seq_count * k2a).reshape(-1)
    a = np.arange(seq_count * runs)
    b = np.arange(LANES)
    outer = 2.0 * np.pi * ((ka[:, None] * a[None, :]) % wide) / wide
    first = np.concatenate([np.cos(outer), -np.sin(outer)], axis=0)
    last = first.T / fft_len
    turn = 2.0 * np.pi * ((ka[:, None] * b[None, :]) % fft_len) / fft_len
    inner = 2.0 * np.pi * ((b[:, None] * b[None, :]) % LANES) / LANES
    cos, sin = np.cos(inner), np.sin(inner)
    forward = np.block([[cos, -sin], [sin, cos]])
    backward = np.block([[cos, sin], [-sin, cos]])
    half = lambda table: jnp.asarray(table, jnp.bfloat16)
    full = lambda table: jnp.asarray(table, jnp.float32)
    return half(first), half(last), full(np.cos(turn)), full(np.sin(turn)), half(forward), half(backward)


def conv_kernel(signal_ref, resp_ref, first_ref, last_ref, cos_ref, sin_ref, fwd_ref, bwd_ref, out_ref, held, low, high):
    seq_count, block, tok_rows = signal_ref.shape
    runs = tok_rows // LANES
    span = seq_count * runs
    rows = cos_ref.shape[0]
    pair = 2 * rows
    for s in range(seq_count):
        for r in range(runs):
            piece = signal_ref[s, :, r * LANES : (r + 1) * LANES].astype(jnp.float32)
            held[pl.ds(s * runs + r, block, stride=span), :] = piece
    cos, sin = cos_ref[...], sin_ref[...]
    for c in range(0, block, 2):
        x = jnp.concatenate([held[c * span : (c + 1) * span, :], held[(c + 1) * span : (c + 2) * span, :]], axis=1)
        y = jnp.dot(first_ref[...], x.astype(jnp.bfloat16), preferred_element_type=jnp.float32)
        turned = []
        for half in (slice(0, LANES), slice(LANES, 2 * LANES)):
            re, im = y[:rows, half], y[rows:, half]
            turned.append(jnp.concatenate([re * cos + im * sin, im * cos - re * sin], axis=1))
        low[c * rows : c * rows + pair, :] = jnp.concatenate(turned, axis=0).astype(jnp.bfloat16)
    high[...] = jnp.dot(low[...], fwd_ref[...], preferred_element_type=jnp.float32)
    for c in range(0, block, 2):
        done = []
        for d in (c, c + 1):
            re = high[d * rows : (d + 1) * rows, :LANES]
            im = high[d * rows : (d + 1) * rows, LANES:]
            hr = resp_ref[0, d].astype(jnp.float32)
            hi = resp_ref[1, d].astype(jnp.float32)
            done.append(jnp.concatenate([re * hr - im * hi, re * hi + im * hr], axis=1))
        low[c * rows : c * rows + pair, :] = jnp.concatenate(done, axis=0).astype(jnp.bfloat16)
    high[...] = jnp.dot(low[...], bwd_ref[...], preferred_element_type=jnp.float32)
    for c in range(0, block, 2):
        turned = []
        for d in (c, c + 1):
            re = high[d * rows : (d + 1) * rows, :LANES]
            im = high[d * rows : (d + 1) * rows, LANES:]
            turned.append(jnp.concatenate([re * cos - im * sin, im * cos + re * sin], axis=0))
        w = jnp.concatenate(turned, axis=1).astype(jnp.bfloat16)
        y = jnp.dot(last_ref[...], w, preferred_element_type=jnp.float32)
        held[c * span : (c + 1) * span, :] = y[:, :LANES]
        held[(c + 1) * span : (c + 2) * span, :] = y[:, LANES:]
    for s in range(seq_count):
        for r in range(runs):
            piece = held[pl.ds(s * runs + r, block, stride=span), :]
            out_ref[s, :, r * LANES : (r + 1) * LANES] = piece.astype(out_ref.dtype)


def long_conv(values, response, start=0):
    seq_count, chans, tok_rows = values.shape
    rows = response.shape[2]
    block = min(CHAN_BLOCK, chans)
    tables = transform_tables(seq_count, tok_rows)
    fixed = [pl.BlockSpec(t.shape, lambda i: (0, 0)) for t in tables]
    span = seq_count * tok_rows // LANES
    flops = chans * 2 * (2 * 2 * rows * span * LANES + 2 * rows * 4 * LANES * LANES)
    moved = 2 * (2 * values.size + 2 * chans * rows * LANES)
    return pl.pallas_call(
        conv_kernel,
        grid=(chans // block,),
        in_specs=[
            pl.BlockSpec((seq_count, block, tok_rows), lambda i: (0, i, 0)),
            pl.BlockSpec((2, block, rows, LANES), lambda i: (0, start // block + i, 0, 0)),
            *fixed,
        ],
        out_specs=pl.BlockSpec((seq_count, block, tok_rows), lambda i: (0, i, 0)),
        out_shape=jax.ShapeDtypeStruct((seq_count, chans, tok_rows), jnp.bfloat16),
        scratch_shapes=[
            pltpu.VMEM((block * span + span, LANES), jnp.float32),
            pltpu.VMEM((block * rows, 2 * LANES), jnp.bfloat16),
            pltpu.VMEM((block * rows, 2 * LANES), jnp.float32),
        ],
        compiler_params=pltpu.CompilerParams(vmem_limit_bytes=12 * MIB),
        cost_estimate=pl.CostEstimate(flops=flops, bytes_accessed=moved, transcendentals=0),
    )(values, response, *tables)


def gate_kernel(conv_ref, skip_ref, signal_ref, query_ref, out_ref):
    conv = conv_ref[...].astype(jnp.float32).T
    inner = conv + skip_ref[...] * signal_ref[...].astype(jnp.float32)
    out_ref[...] = (query_ref[...].astype(jnp.float32) * inner).astype(out_ref.dtype)


def gate(longconv, skip, lo, signal, query):
    chans, tok_rows = longconv.shape
    first = lo // LANES
    flat = pl.BlockSpec((tok_rows, LANES), lambda i: (0, i))
    return pl.pallas_call(
        gate_kernel,
        grid=(chans // LANES,),
        in_specs=[
            pl.BlockSpec((LANES, tok_rows), lambda i: (i, 0)),
            pl.BlockSpec((1, LANES), lambda i: (0, first + i)),
            flat,
            flat,
        ],
        out_specs=flat,
        out_shape=jax.ShapeDtypeStruct((tok_rows, chans), jnp.bfloat16),
        compiler_params=pltpu.CompilerParams(vmem_limit_bytes=8 * MIB),
        cost_estimate=pl.CostEstimate(flops=4 * chans * tok_rows, bytes_accessed=8 * chans * tok_rows, transcendentals=0),
    )(longconv, skip[None, :], signal, query)


def reorder_kernel(spec_ref, order_ref, out_ref):
    each = out_ref.shape[3]
    x = spec_ref[0].astype(jnp.bfloat16)
    y = jnp.dot(x, order_ref[...], preferred_element_type=jnp.float32).astype(jnp.bfloat16)
    for d in range(out_ref.shape[0]):
        out_ref[d, 0, 0] = y[d * each : (d + 1) * each]


def fold_kernel(got_ref, out_ref, came, held):
    seq_count, pairs, tok_rows = got_ref.shape[0], got_ref.shape[3], got_ref.shape[4]
    chans = pairs // 2
    runs = tok_rows // LANES
    rows = (seq_count + 1) * runs
    for part in range(2):
        sign = 1.0 if part == 0 else -1.0
        for s in range(seq_count):
            for r in range(runs):
                at = (s * runs + r) * pairs
                lanes = slice(r * LANES, (r + 1) * LANES)
                came[at : at + pairs, :] = got_ref[s, part, 0, :, lanes].astype(jnp.float32)
        for k1 in range(seq_count + 1):
            other = 2 * seq_count - k1
            for r in range(runs):
                value = came[pl.ds((k1 // 2 * runs + r) * pairs + k1 % 2, chans, stride=2), :]
                if k1 == seq_count:
                    value = sign * value
                elif k1 > 0:
                    value = value + sign * came[pl.ds((other // 2 * runs + r) * pairs + other % 2, chans, stride=2), :]
                held[pl.ds(k1 * runs + r, chans, stride=rows), :] = value
        out_ref[part] = held[: chans * rows, :].reshape(chans, rows, LANES).astype(out_ref.dtype)


def reordered_spectrum(spectrum, seq_count, chunks):
    parts, chans, own, tok_rows = spectrum.shape
    runs = tok_rows // LANES
    size = chans // chunks
    each = size // seq_count
    col = lax.broadcasted_iota(jnp.int32, (tok_rows, tok_rows), 1)
    row = lax.broadcasted_iota(jnp.int32, (tok_rows, tok_rows), 0)
    wanted = col // LANES + runs * (col % LANES)
    wanted = jnp.where(lax.axis_index("seq") >= seq_count // 2, tok_rows - 1 - wanted, wanted)
    order = (row == wanted).astype(jnp.bfloat16)
    shape = (seq_count, parts, chunks, own * each, tok_rows)
    return pl.pallas_call(
        reorder_kernel,
        grid=(parts, chunks),
        in_specs=[
            pl.BlockSpec((1, own * size, tok_rows), lambda p, j: (p, j, 0)),
            pl.BlockSpec((tok_rows, tok_rows), lambda p, j: (0, 0)),
        ],
        out_specs=pl.BlockSpec((seq_count, 1, 1, own * each, tok_rows), lambda p, j: (0, p, j, 0, 0)),
        out_shape=jax.ShapeDtypeStruct(shape, jnp.bfloat16),
        compiler_params=pltpu.CompilerParams(vmem_limit_bytes=48 * MIB),
        cost_estimate=pl.CostEstimate(
            flops=2 * spectrum.size * tok_rows, bytes_accessed=6 * spectrum.size, transcendentals=0
        ),
    )(spectrum.reshape(parts, chans * own, tok_rows), order)


def folded_response(sent, own):
    seq_count, parts, chunks, pairs, tok_rows = sent.shape
    runs = tok_rows // LANES
    each = pairs // own
    got = lax.all_to_all(sent, "seq", split_axis=0, concat_axis=0, tiled=True)
    block = min(CHAN_BLOCK, each)
    rows = (seq_count + 1) * runs
    return pl.pallas_call(
        fold_kernel,
        grid=(chunks, each // block),
        in_specs=[pl.BlockSpec((seq_count, parts, 1, own * block, tok_rows), lambda j, i: (0, 0, j, i, 0))],
        out_specs=pl.BlockSpec((parts, block, rows, LANES), lambda j, i: (0, j * (each // block) + i, 0, 0)),
        out_shape=jax.ShapeDtypeStruct((parts, chunks * each, rows, LANES), jnp.bfloat16),
        scratch_shapes=[
            pltpu.VMEM((seq_count * runs * own * block + 8, LANES), jnp.float32),
            pltpu.VMEM((block * rows + rows, LANES), jnp.float32),
        ],
        compiler_params=pltpu.CompilerParams(vmem_limit_bytes=12 * MIB),
        cost_estimate=pl.CostEstimate(flops=sent.size, bytes_accessed=3 * sent.size, transcendentals=0),
    )(got)


def feature_rows(out_weight, seq_count):
    each = out_weight.shape[0] // seq_count
    own = lax.dynamic_slice_in_dim(out_weight, lax.axis_index("seq") * each, each, axis=0)
    own = lax.all_to_all(own, "chan", split_axis=1, concat_axis=0, tiled=True)
    return own.reshape(lax.axis_size("chan"), each, own.shape[1])


def combine_kernel(gated_ref, w_ref, *refs):
    out_ref = refs[-1]
    gated = jnp.concatenate([gated_ref[z] for z in range(gated_ref.shape[0])], axis=1)
    total = jnp.dot(gated, w_ref[0], preferred_element_type=jnp.float32)
    if len(refs) == 2:
        total = total + refs[0][...]
    out_ref[...] = total.astype(out_ref.dtype)


def combine(gathered, weight, chunk, total, dtype):
    count, tok_rows, size = gathered.shape
    depth = count * size
    features = weight.shape[2]
    tile = min(4 * LANES, features)
    block = pl.BlockSpec((tok_rows, tile), lambda i: (0, i))
    given = [] if total is None else [total]
    return pl.pallas_call(
        combine_kernel,
        grid=(features // tile,),
        in_specs=[
            pl.BlockSpec((count, tok_rows, size), lambda i: (0, 0, 0)),
            pl.BlockSpec((1, depth, tile), lambda i: (chunk, 0, i)),
            *[block for _ in given],
        ],
        out_specs=block,
        out_shape=jax.ShapeDtypeStruct((tok_rows, features), dtype),
        compiler_params=pltpu.CompilerParams(vmem_limit_bytes=60 * MIB),
        cost_estimate=pl.CostEstimate(
            flops=2 * tok_rows * depth * features,
            bytes_accessed=2 * depth * (tok_rows + features) + 6 * tok_rows * features,
            transcendentals=0,
        ),
    )(gathered, weight, *given)


def shards(tokens, in_weight, conv_weight, spectrum, skip, out_weight):
    tok_rows, depth = tokens.shape
    seq_count = lax.axis_size("seq")
    chan_count = lax.axis_size("chan")
    chans = in_weight.shape[2]
    chunks = chunk_count(chans, seq_count)
    size = chans // chunks
    gathered = lax.all_gather(tokens, "chan")
    weight = feature_rows(out_weight, seq_count)
    last_rows = tokens[tok_rows - HALO :]
    weight, last_rows = lax.optimization_barrier((weight, last_rows))
    halo = gather_by_doubling(from_behind(last_rows, "seq", 1), "chan")
    sent = reordered_spectrum(spectrum, seq_count, chunks)
    halo, sent, weight = lax.optimization_barrier((halo, sent, weight))
    response = folded_response(sent, spectrum.shape[2])
    weight = gather_by_doubling(weight, "seq")
    weight = weight.reshape((chunks, seq_count // chunks) + weight.shape[1:]).transpose(0, 2, 1, 3, 4)
    weight = weight.reshape(chunks, chan_count * size, weight.shape[4])
    halo = jnp.einsum(
        "ztd,pzdc->ptc",
        halo,
        in_weight.reshape(3, chan_count, depth, chans),
        preferred_element_type=jnp.float32,
    ).astype(jnp.bfloat16)
    total = None
    for j, lo in enumerate(range(0, chans, size)):
        given = (gathered, in_weight, conv_weight, halo, lo, size, response, weight)
        query_t, signal, signal_t = project(*given)
        values = signal.reshape(seq_count, size // seq_count, tok_rows)
        values = lax.all_to_all(values, "seq", split_axis=0, concat_axis=0, tiled=True)
        longconv = lax.all_to_all(
            long_conv(values, response, lo // seq_count), "seq", split_axis=0, concat_axis=0, tiled=True
        ).reshape(size, tok_rows)
        gated = lax.all_gather(gate(longconv, skip, lo, signal_t, query_t), "chan")
        dtype = jnp.bfloat16 if lo + size == chans else jnp.float32
        total = combine(gated, weight, j, total, dtype)
    return total


def solution(mesh):
    placed = (
        P("seq", "chan"),
        P(None, None, "chan"),
        P(None, None, "chan"),
        P(None, "chan", "seq", None),
        P("chan"),
        P("chan", None),
    )
    return jax.shard_map(
        shards, mesh=mesh, in_specs=placed, out_specs=P("seq", "chan"), check_vma=False
    )
```

```python
import jax
import jax.numpy as jnp
import numpy as np
from jax import lax
from jax.experimental import pallas as pl
from jax.experimental.pallas import tpu as pltpu
from jax.sharding import PartitionSpec as P

TAPS = 3
LANES = 128
HALO = 16
CHAN_BLOCK = 16
CHUNKS = 2
MIB = 1024 * 1024


def from_behind(value, axis, by):
    size = lax.axis_size(axis)
    pairs = [(i, i + by) for i in range(size) if 0 <= i + by < size]
    return lax.ppermute(value, axis, pairs)


def gather_by_doubling(value, axis):
    size = lax.axis_size(axis)
    index = lax.axis_index(axis)
    held = value[None]
    bit = size // 2
    while bit >= 1:
        other = lax.ppermute(held, axis, [(i, i ^ bit) for i in range(size)])
        upper = (index // bit) % 2 == 1
        first = jnp.where(upper, other, held)
        second = jnp.where(upper, held, other)
        held = jnp.stack([first, second], axis=1).reshape((2 * held.shape[0],) + held.shape[1:])
        bit //= 2
    return held


def chunk_count(chans, seq_count):
    size = chans // CHUNKS
    return 1 if size % LANES or (size // seq_count) % CHAN_BLOCK else CHUNKS


def project_kernel(extras, tok_ref, wq_ref, wk_ref, wv_ref, taps_ref, halo_ref, *rest):
    query_t_ref, signal_ref, signal_t_ref, acc = rest[extras:]
    step = pl.program_id(0)
    last = pl.num_programs(0) - 1
    rows, size = query_t_ref.shape

    def part(first=0, count=rows):
        weight = jnp.concatenate([wq_ref[0], wk_ref[0], wv_ref[0]], axis=1)
        return jnp.dot(tok_ref[0, first : first + count], weight, preferred_element_type=jnp.float32)

    def filtered(p, r):
        lanes = slice(p * size, (p + 1) * size)
        total = taps_ref[0, p][None, :] * acc[pl.ds(HALO + r, LANES), lanes]
        for j in range(1, TAPS):
            total = total + taps_ref[j, p][None, :] * acc[pl.ds(HALO + r - j, LANES), lanes]
        return total

    @pl.when(step == 0)
    def _():
        for p in range(3):
            acc[:HALO, p * size : (p + 1) * size] = halo_ref[p].astype(jnp.float32)
        acc[HALO:, :] = part()

    @pl.when(jnp.logical_and(step > 0, step < last))
    def _():
        acc[HALO:, :] += part()

    @pl.when(step == last)
    def _():
        half = rows // 2
        for first in (0, half):
            held = slice(HALO + first, HALO + first + half)
            acc[held, :] = (acc[held, :] + part(first, half)).astype(jnp.bfloat16).astype(jnp.float32)
            for r in range(first, first + half, LANES):
                query_t_ref[r : r + LANES, :] = filtered(0, r).astype(query_t_ref.dtype)
                signal = filtered(1, r) * filtered(2, r)
                signal_t_ref[r : r + LANES, :] = signal.astype(signal_t_ref.dtype)
                signal_ref[:, r : r + LANES] = signal.T.astype(signal_ref.dtype)


def project(gathered, in_weight, conv_weight, halo, lo, size, *after):
    count, rows, step = gathered.shape
    at = lo // size
    flat = jax.ShapeDtypeStruct((rows, size), jnp.bfloat16)
    shapes = [flat, jax.ShapeDtypeStruct((size, rows), jnp.bfloat16), flat]

    def weight_of(p):
        return pl.BlockSpec((1, step, size), lambda z: (p, z, at))

    return pl.pallas_call(
        lambda *refs: project_kernel(len(after), *refs),
        grid=(count,),
        in_specs=[
            pl.BlockSpec((1, rows, step), lambda z: (z, 0, 0)),
            *[weight_of(p) for p in range(3)],
            pl.BlockSpec((TAPS, 3, size), lambda z: (0, 0, at)),
            pl.BlockSpec((3, HALO, size), lambda z: (0, 0, at)),
            *[pl.BlockSpec(memory_space=pl.ANY) for _ in after],
        ],
        out_specs=[pl.BlockSpec(shape.shape, lambda z: (0, 0)) for shape in shapes],
        out_shape=shapes,
        scratch_shapes=[pltpu.VMEM((HALO + rows, 3 * size), jnp.float32)],
        compiler_params=pltpu.CompilerParams(vmem_limit_bytes=48 * MIB),
        cost_estimate=pl.CostEstimate(
            flops=2 * 3 * rows * count * step * size,
            bytes_accessed=2 * count * step * (3 * size + rows),
            transcendentals=0,
        ),
    )(gathered, in_weight, in_weight, in_weight, conv_weight, halo, *after)


def transform_tables(seq_count, tok_rows):
    runs = tok_rows // LANES
    wide = 2 * seq_count * runs
    fft_len = wide * LANES
    k1 = np.arange(seq_count + 1)[:, None]
    k2a = np.arange(runs)[None, :]
    ka = (k1 + 2 * seq_count * k2a).reshape(-1)
    a = np.arange(seq_count * runs)
    b = np.arange(LANES)
    outer = 2.0 * np.pi * ((ka[:, None] * a[None, :]) % wide) / wide
    first = np.concatenate([np.cos(outer), -np.sin(outer)], axis=0)
    last = first.T / fft_len
    turn = 2.0 * np.pi * ((ka[:, None] * b[None, :]) % fft_len) / fft_len
    inner = 2.0 * np.pi * ((b[:, None] * b[None, :]) % LANES) / LANES
    cos, sin = np.cos(inner), np.sin(inner)
    forward = np.block([[cos, -sin], [sin, cos]])
    backward = np.block([[cos, sin], [-sin, cos]])
    half = lambda table: jnp.asarray(table, jnp.bfloat16)
    full = lambda table: jnp.asarray(table, jnp.float32)
    return half(first), half(last), full(np.cos(turn)), full(np.sin(turn)), half(forward), half(backward)


def conv_kernel(signal_ref, resp_ref, first_ref, last_ref, cos_ref, sin_ref, fwd_ref, bwd_ref, out_ref, held, low, high):
    seq_count, block, tok_rows = signal_ref.shape
    runs = tok_rows // LANES
    span = seq_count * runs
    rows = cos_ref.shape[0]
    pair = 2 * rows
    for s in range(seq_count):
        for r in range(runs):
            piece = signal_ref[s, :, r * LANES : (r + 1) * LANES].astype(jnp.float32)
            held[pl.ds(s * runs + r, block, stride=span), :] = piece
    cos, sin = cos_ref[...], sin_ref[...]
    for c in range(0, block, 2):
        x = jnp.concatenate([held[c * span : (c + 1) * span, :], held[(c + 1) * span : (c + 2) * span, :]], axis=1)
        y = jnp.dot(first_ref[...], x.astype(jnp.bfloat16), preferred_element_type=jnp.float32)
        turned = []
        for half in (slice(0, LANES), slice(LANES, 2 * LANES)):
            re, im = y[:rows, half], y[rows:, half]
            turned.append(jnp.concatenate([re * cos + im * sin, im * cos - re * sin], axis=1))
        low[c * rows : c * rows + pair, :] = jnp.concatenate(turned, axis=0).astype(jnp.bfloat16)
    high[...] = jnp.dot(low[...], fwd_ref[...], preferred_element_type=jnp.float32)
    for c in range(0, block, 2):
        done = []
        for d in (c, c + 1):
            re = high[d * rows : (d + 1) * rows, :LANES]
            im = high[d * rows : (d + 1) * rows, LANES:]
            hr = resp_ref[0, d].astype(jnp.float32)
            hi = resp_ref[1, d].astype(jnp.float32)
            done.append(jnp.concatenate([re * hr - im * hi, re * hi + im * hr], axis=1))
        low[c * rows : c * rows + pair, :] = jnp.concatenate(done, axis=0).astype(jnp.bfloat16)
    high[...] = jnp.dot(low[...], bwd_ref[...], preferred_element_type=jnp.float32)
    for c in range(0, block, 2):
        turned = []
        for d in (c, c + 1):
            re = high[d * rows : (d + 1) * rows, :LANES]
            im = high[d * rows : (d + 1) * rows, LANES:]
            turned.append(jnp.concatenate([re * cos - im * sin, im * cos + re * sin], axis=0))
        w = jnp.concatenate(turned, axis=1).astype(jnp.bfloat16)
        y = jnp.dot(last_ref[...], w, preferred_element_type=jnp.float32)
        held[c * span : (c + 1) * span, :] = y[:, :LANES]
        held[(c + 1) * span : (c + 2) * span, :] = y[:, LANES:]
    for s in range(seq_count):
        for r in range(runs):
            piece = held[pl.ds(s * runs + r, block, stride=span), :]
            out_ref[s, :, r * LANES : (r + 1) * LANES] = piece.astype(out_ref.dtype)


def long_conv(values, response, start=0):
    seq_count, chans, tok_rows = values.shape
    rows = response.shape[2]
    block = min(CHAN_BLOCK, chans)
    tables = transform_tables(seq_count, tok_rows)
    fixed = [pl.BlockSpec(t.shape, lambda i: (0, 0)) for t in tables]
    span = seq_count * tok_rows // LANES
    flops = chans * 2 * (2 * 2 * rows * span * LANES + 2 * rows * 4 * LANES * LANES)
    moved = 2 * (2 * values.size + 2 * chans * rows * LANES)
    return pl.pallas_call(
        conv_kernel,
        grid=(chans // block,),
        in_specs=[
            pl.BlockSpec((seq_count, block, tok_rows), lambda i: (0, i, 0)),
            pl.BlockSpec((2, block, rows, LANES), lambda i: (0, start // block + i, 0, 0)),
            *fixed,
        ],
        out_specs=pl.BlockSpec((seq_count, block, tok_rows), lambda i: (0, i, 0)),
        out_shape=jax.ShapeDtypeStruct((seq_count, chans, tok_rows), jnp.bfloat16),
        scratch_shapes=[
            pltpu.VMEM((block * span + span, LANES), jnp.float32),
            pltpu.VMEM((block * rows, 2 * LANES), jnp.bfloat16),
            pltpu.VMEM((block * rows, 2 * LANES), jnp.float32),
        ],
        compiler_params=pltpu.CompilerParams(vmem_limit_bytes=12 * MIB),
        cost_estimate=pl.CostEstimate(flops=flops, bytes_accessed=moved, transcendentals=0),
    )(values, response, *tables)


def gate_kernel(conv_ref, skip_ref, signal_ref, query_ref, out_ref):
    conv = conv_ref[...].astype(jnp.float32).T
    inner = conv + skip_ref[...] * signal_ref[...].astype(jnp.float32)
    out_ref[...] = (query_ref[...].astype(jnp.float32) * inner).astype(out_ref.dtype)


def gate(longconv, skip, lo, signal, query):
    chans, tok_rows = longconv.shape
    first = lo // LANES
    flat = pl.BlockSpec((tok_rows, LANES), lambda i: (0, i))
    return pl.pallas_call(
        gate_kernel,
        grid=(chans // LANES,),
        in_specs=[
            pl.BlockSpec((LANES, tok_rows), lambda i: (i, 0)),
            pl.BlockSpec((1, LANES), lambda i: (0, first + i)),
            flat,
            flat,
        ],
        out_specs=flat,
        out_shape=jax.ShapeDtypeStruct((tok_rows, chans), jnp.bfloat16),
        compiler_params=pltpu.CompilerParams(vmem_limit_bytes=8 * MIB),
        cost_estimate=pl.CostEstimate(flops=4 * chans * tok_rows, bytes_accessed=8 * chans * tok_rows, transcendentals=0),
    )(longconv, skip[None, :], signal, query)


def reorder_kernel(spec_ref, order_ref, out_ref):
    each = out_ref.shape[3]
    x = spec_ref[0].astype(jnp.bfloat16)
    y = jnp.dot(x, order_ref[...], preferred_element_type=jnp.float32).astype(jnp.bfloat16)
    for d in range(out_ref.shape[0]):
        out_ref[d, 0, 0] = y[d * each : (d + 1) * each]


def fold_kernel(got_ref, out_ref, came, held):
    seq_count, pairs, tok_rows = got_ref.shape[0], got_ref.shape[3], got_ref.shape[4]
    chans = pairs // 2
    runs = tok_rows // LANES
    rows = (seq_count + 1) * runs
    for part in range(2):
        sign = 1.0 if part == 0 else -1.0
        for s in range(seq_count):
            for r in range(runs):
                at = (s * runs + r) * pairs
                lanes = slice(r * LANES, (r + 1) * LANES)
                came[at : at + pairs, :] = got_ref[s, part, 0, :, lanes].astype(jnp.float32)
        for k1 in range(seq_count + 1):
            other = 2 * seq_count - k1
            for r in range(runs):
                value = came[pl.ds((k1 // 2 * runs + r) * pairs + k1 % 2, chans, stride=2), :]
                if k1 == seq_count:
                    value = sign * value
                elif k1 > 0:
                    value = value + sign * came[pl.ds((other // 2 * runs + r) * pairs + other % 2, chans, stride=2), :]
                held[pl.ds(k1 * runs + r, chans, stride=rows), :] = value
        out_ref[part] = held[: chans * rows, :].reshape(chans, rows, LANES).astype(out_ref.dtype)


def reordered_spectrum(spectrum, seq_count, chunks):
    parts, chans, own, tok_rows = spectrum.shape
    runs = tok_rows // LANES
    size = chans // chunks
    each = size // seq_count
    col = lax.broadcasted_iota(jnp.int32, (tok_rows, tok_rows), 1)
    row = lax.broadcasted_iota(jnp.int32, (tok_rows, tok_rows), 0)
    wanted = col // LANES + runs * (col % LANES)
    wanted = jnp.where(lax.axis_index("seq") >= seq_count // 2, tok_rows - 1 - wanted, wanted)
    order = (row == wanted).astype(jnp.bfloat16)
    shape = (seq_count, parts, chunks, own * each, tok_rows)
    return pl.pallas_call(
        reorder_kernel,
        grid=(parts, chunks),
        in_specs=[
            pl.BlockSpec((1, own * size, tok_rows), lambda p, j: (p, j, 0)),
            pl.BlockSpec((tok_rows, tok_rows), lambda p, j: (0, 0)),
        ],
        out_specs=pl.BlockSpec((seq_count, 1, 1, own * each, tok_rows), lambda p, j: (0, p, j, 0, 0)),
        out_shape=jax.ShapeDtypeStruct(shape, jnp.bfloat16),
        compiler_params=pltpu.CompilerParams(vmem_limit_bytes=48 * MIB),
        cost_estimate=pl.CostEstimate(
            flops=2 * spectrum.size * tok_rows, bytes_accessed=6 * spectrum.size, transcendentals=0
        ),
    )(spectrum.reshape(parts, chans * own, tok_rows), order)


def folded_response(sent, own):
    seq_count, parts, chunks, pairs, tok_rows = sent.shape
    runs = tok_rows // LANES
    each = pairs // own
    got = lax.all_to_all(sent, "seq", split_axis=0, concat_axis=0, tiled=True)
    block = min(CHAN_BLOCK, each)
    rows = (seq_count + 1) * runs
    return pl.pallas_call(
        fold_kernel,
        grid=(chunks, each // block),
        in_specs=[pl.BlockSpec((seq_count, parts, 1, own * block, tok_rows), lambda j, i: (0, 0, j, i, 0))],
        out_specs=pl.BlockSpec((parts, block, rows, LANES), lambda j, i: (0, j * (each // block) + i, 0, 0)),
        out_shape=jax.ShapeDtypeStruct((parts, chunks * each, rows, LANES), jnp.bfloat16),
        scratch_shapes=[
            pltpu.VMEM((seq_count * runs * own * block + 8, LANES), jnp.float32),
            pltpu.VMEM((block * rows + rows, LANES), jnp.float32),
        ],
        compiler_params=pltpu.CompilerParams(vmem_limit_bytes=12 * MIB),
        cost_estimate=pl.CostEstimate(flops=sent.size, bytes_accessed=3 * sent.size, transcendentals=0),
    )(got)


def feature_rows(out_weight, seq_count):
    each = out_weight.shape[0] // seq_count
    own = lax.dynamic_slice_in_dim(out_weight, lax.axis_index("seq") * each, each, axis=0)
    own = lax.all_to_all(own, "chan", split_axis=1, concat_axis=0, tiled=True)
    return own.reshape(lax.axis_size("chan"), each, own.shape[1])


def combine_kernel(gated_ref, w_ref, *refs):
    out_ref = refs[-1]
    gated = jnp.concatenate([gated_ref[z] for z in range(gated_ref.shape[0])], axis=1)
    total = jnp.dot(gated, w_ref[0], preferred_element_type=jnp.float32)
    if len(refs) == 2:
        total = total + refs[0][...].astype(jnp.float32)
    out_ref[...] = total.astype(out_ref.dtype)


def combine(gathered, weight, chunk, total):
    count, tok_rows, size = gathered.shape
    depth = count * size
    features = weight.shape[2]
    tile = min(4 * LANES, features)
    block = pl.BlockSpec((tok_rows, tile), lambda i: (0, i))
    given = [] if total is None else [total]
    return pl.pallas_call(
        combine_kernel,
        grid=(features // tile,),
        in_specs=[
            pl.BlockSpec((count, tok_rows, size), lambda i: (0, 0, 0)),
            pl.BlockSpec((1, depth, tile), lambda i: (chunk, 0, i)),
            *[block for _ in given],
        ],
        out_specs=block,
        out_shape=jax.ShapeDtypeStruct((tok_rows, features), jnp.bfloat16),
        compiler_params=pltpu.CompilerParams(vmem_limit_bytes=60 * MIB),
        cost_estimate=pl.CostEstimate(
            flops=2 * tok_rows * depth * features,
            bytes_accessed=2 * depth * (tok_rows + features) + 6 * tok_rows * features,
            transcendentals=0,
        ),
    )(gathered, weight, *given)


def shards(tokens, in_weight, conv_weight, spectrum, skip, out_weight):
    tok_rows, depth = tokens.shape
    seq_count = lax.axis_size("seq")
    chan_count = lax.axis_size("chan")
    chans = in_weight.shape[2]
    chunks = chunk_count(chans, seq_count)
    size = chans // chunks
    gathered = lax.all_gather(tokens, "chan")
    weight = feature_rows(out_weight, seq_count)
    last_rows = tokens[tok_rows - HALO :]
    weight, last_rows = lax.optimization_barrier((weight, last_rows))
    halo = gather_by_doubling(from_behind(last_rows, "seq", 1), "chan")
    sent = reordered_spectrum(spectrum, seq_count, chunks)
    halo, sent, weight = lax.optimization_barrier((halo, sent, weight))
    response = folded_response(sent, spectrum.shape[2])
    weight = gather_by_doubling(weight, "seq")
    weight = weight.reshape((chunks, seq_count // chunks) + weight.shape[1:]).transpose(0, 2, 1, 3, 4)
    weight = weight.reshape(chunks, chan_count * size, weight.shape[4])
    halo = jnp.einsum(
        "ztd,pzdc->ptc",
        halo,
        in_weight.reshape(3, chan_count, depth, chans),
        preferred_element_type=jnp.float32,
    ).astype(jnp.bfloat16)
    total = None
    for j, lo in enumerate(range(0, chans, size)):
        given = (gathered, in_weight, conv_weight, halo, lo, size, response, weight)
        query_t, signal, signal_t = project(*given)
        values = signal.reshape(seq_count, size // seq_count, tok_rows)
        values = lax.all_to_all(values, "seq", split_axis=0, concat_axis=0, tiled=True)
        longconv = lax.all_to_all(
            long_conv(values, response, lo // seq_count), "seq", split_axis=0, concat_axis=0, tiled=True
        ).reshape(size, tok_rows)
        gated = lax.all_gather(gate(longconv, skip, lo, signal_t, query_t), "chan")
        total = combine(gated, weight, j, total)
    return total


def solution(mesh):
    placed = (
        P("seq", "chan"),
        P(None, None, "chan"),
        P(None, None, "chan"),
        P(None, "chan", "seq", None),
        P("chan"),
        P("chan", None),
    )
    return jax.shard_map(
        shards, mesh=mesh, in_specs=placed, out_specs=P("seq", "chan"), check_vma=False
    )
```

```python
import jax
import jax.numpy as jnp
import numpy as np
from jax import lax
from jax.experimental import pallas as pl
from jax.experimental.pallas import tpu as pltpu
from jax.sharding import PartitionSpec as P

TAPS = 3
LANES = 128
HALO = 16
CHAN_BLOCK = 16
CHUNKS = 2
MIB = 1024 * 1024


def from_behind(value, axis, by):
    size = lax.axis_size(axis)
    pairs = [(i, i + by) for i in range(size) if 0 <= i + by < size]
    return lax.ppermute(value, axis, pairs)


def gather_by_doubling(value, axis):
    size = lax.axis_size(axis)
    index = lax.axis_index(axis)
    held = value[None]
    bit = size // 2
    while bit >= 1:
        other = lax.ppermute(held, axis, [(i, i ^ bit) for i in range(size)])
        upper = (index // bit) % 2 == 1
        first = jnp.where(upper, other, held)
        second = jnp.where(upper, held, other)
        held = jnp.stack([first, second], axis=1).reshape((2 * held.shape[0],) + held.shape[1:])
        bit //= 2
    return held


def chunk_count(chans, seq_count):
    size = chans // CHUNKS
    return 1 if size % LANES or (size // seq_count) % CHAN_BLOCK else CHUNKS


def project_kernel(extras, tok_ref, wq_ref, wk_ref, wv_ref, taps_ref, halo_ref, *rest):
    query_t_ref, signal_ref, signal_t_ref, acc = rest[extras:]
    step = pl.program_id(0)
    last = pl.num_programs(0) - 1
    rows, size = query_t_ref.shape

    def part(first=0, count=rows):
        weight = jnp.concatenate([wq_ref[0], wk_ref[0], wv_ref[0]], axis=1)
        return jnp.dot(tok_ref[0, first : first + count], weight, preferred_element_type=jnp.float32)

    def filtered(p, r):
        lanes = slice(p * size, (p + 1) * size)
        total = taps_ref[0, p][None, :] * acc[pl.ds(HALO + r, LANES), lanes]
        for j in range(1, TAPS):
            total = total + taps_ref[j, p][None, :] * acc[pl.ds(HALO + r - j, LANES), lanes]
        return total

    @pl.when(step == 0)
    def _():
        for p in range(3):
            acc[:HALO, p * size : (p + 1) * size] = halo_ref[p].astype(jnp.float32)
        acc[HALO:, :] = part()

    @pl.when(jnp.logical_and(step > 0, step < last))
    def _():
        acc[HALO:, :] += part()

    @pl.when(step == last)
    def _():
        half = rows // 2
        for first in (0, half):
            held = slice(HALO + first, HALO + first + half)
            acc[held, :] = (acc[held, :] + part(first, half)).astype(jnp.bfloat16).astype(jnp.float32)
            for r in range(first, first + half, LANES):
                query_t_ref[r : r + LANES, :] = filtered(0, r).astype(query_t_ref.dtype)
                signal = filtered(1, r) * filtered(2, r)
                signal_t_ref[r : r + LANES, :] = signal.astype(signal_t_ref.dtype)
                signal_ref[:, r : r + LANES] = signal.T.astype(signal_ref.dtype)


def project(gathered, in_weight, conv_weight, halo, lo, size, *after):
    count, rows, step = gathered.shape
    at = lo // size
    flat = jax.ShapeDtypeStruct((rows, size), jnp.bfloat16)
    shapes = [flat, jax.ShapeDtypeStruct((size, rows), jnp.bfloat16), flat]

    def weight_of(p):
        return pl.BlockSpec((1, step, size), lambda z: (p, z, at))

    return pl.pallas_call(
        lambda *refs: project_kernel(len(after), *refs),
        grid=(count,),
        in_specs=[
            pl.BlockSpec((1, rows, step), lambda z: (z, 0, 0)),
            *[weight_of(p) for p in range(3)],
            pl.BlockSpec((TAPS, 3, size), lambda z: (0, 0, at)),
            pl.BlockSpec((3, HALO, size), lambda z: (0, 0, at)),
            *[pl.BlockSpec(memory_space=pl.ANY) for _ in after],
        ],
        out_specs=[pl.BlockSpec(shape.shape, lambda z: (0, 0)) for shape in shapes],
        out_shape=shapes,
        scratch_shapes=[pltpu.VMEM((HALO + rows, 3 * size), jnp.float32)],
        compiler_params=pltpu.CompilerParams(vmem_limit_bytes=48 * MIB),
        cost_estimate=pl.CostEstimate(
            flops=2 * 3 * rows * count * step * size,
            bytes_accessed=2 * count * step * (3 * size + rows),
            transcendentals=0,
        ),
    )(gathered, in_weight, in_weight, in_weight, conv_weight, halo, *after)


def transform_tables(seq_count, tok_rows):
    runs = tok_rows // LANES
    wide = 2 * seq_count * runs
    fft_len = wide * LANES
    k1 = np.arange(seq_count + 1)[:, None]
    k2a = np.arange(runs)[None, :]
    ka = (k1 + 2 * seq_count * k2a).reshape(-1)
    a = np.arange(seq_count * runs)
    b = np.arange(LANES)
    outer = 2.0 * np.pi * ((ka[:, None] * a[None, :]) % wide) / wide
    first = np.concatenate([np.cos(outer), -np.sin(outer)], axis=0)
    last = first.T / fft_len
    turn = 2.0 * np.pi * ((ka[:, None] * b[None, :]) % fft_len) / fft_len
    inner = 2.0 * np.pi * ((b[:, None] * b[None, :]) % LANES) / LANES
    cos, sin = np.cos(inner), np.sin(inner)
    forward = np.block([[cos, -sin], [sin, cos]])
    backward = np.block([[cos, sin], [-sin, cos]])
    half = lambda table: jnp.asarray(table, jnp.bfloat16)
    full = lambda table: jnp.asarray(table, jnp.float32)
    return half(first), half(last), full(np.cos(turn)), full(np.sin(turn)), half(forward), half(backward)


def conv_kernel(signal_ref, resp_ref, first_ref, last_ref, cos_ref, sin_ref, fwd_ref, bwd_ref, out_ref, held, low, high):
    seq_count, block, tok_rows = signal_ref.shape
    runs = tok_rows // LANES
    span = seq_count * runs
    rows = cos_ref.shape[0]
    pair = 2 * rows
    for s in range(seq_count):
        for r in range(runs):
            piece = signal_ref[s, :, r * LANES : (r + 1) * LANES].astype(jnp.float32)
            held[pl.ds(s * runs + r, block, stride=span), :] = piece
    cos, sin = cos_ref[...], sin_ref[...]
    for c in range(0, block, 2):
        x = jnp.concatenate([held[c * span : (c + 1) * span, :], held[(c + 1) * span : (c + 2) * span, :]], axis=1)
        y = jnp.dot(first_ref[...], x.astype(jnp.bfloat16), preferred_element_type=jnp.float32)
        turned = []
        for half in (slice(0, LANES), slice(LANES, 2 * LANES)):
            re, im = y[:rows, half], y[rows:, half]
            turned.append(jnp.concatenate([re * cos + im * sin, im * cos - re * sin], axis=1))
        low[c * rows : c * rows + pair, :] = jnp.concatenate(turned, axis=0).astype(jnp.bfloat16)
    high[...] = jnp.dot(low[...], fwd_ref[...], preferred_element_type=jnp.float32)
    for c in range(0, block, 2):
        done = []
        for d in (c, c + 1):
            re = high[d * rows : (d + 1) * rows, :LANES]
            im = high[d * rows : (d + 1) * rows, LANES:]
            hr = resp_ref[0, d].astype(jnp.float32)
            hi = resp_ref[1, d].astype(jnp.float32)
            done.append(jnp.concatenate([re * hr - im * hi, re * hi + im * hr], axis=1))
        low[c * rows : c * rows + pair, :] = jnp.concatenate(done, axis=0).astype(jnp.bfloat16)
    high[...] = jnp.dot(low[...], bwd_ref[...], preferred_element_type=jnp.float32)
    for c in range(0, block, 2):
        turned = []
        for d in (c, c + 1):
            re = high[d * rows : (d + 1) * rows, :LANES]
            im = high[d * rows : (d + 1) * rows, LANES:]
            turned.append(jnp.concatenate([re * cos - im * sin, im * cos + re * sin], axis=0))
        w = jnp.concatenate(turned, axis=1).astype(jnp.bfloat16)
        y = jnp.dot(last_ref[...], w, preferred_element_type=jnp.float32)
        held[c * span : (c + 1) * span, :] = y[:, :LANES]
        held[(c + 1) * span : (c + 2) * span, :] = y[:, LANES:]
    for s in range(seq_count):
        for r in range(runs):
            piece = held[pl.ds(s * runs + r, block, stride=span), :]
            out_ref[s, :, r * LANES : (r + 1) * LANES] = piece.astype(out_ref.dtype)


def long_conv(values, response, start=0):
    seq_count, chans, tok_rows = values.shape
    rows = response.shape[2]
    block = min(CHAN_BLOCK, chans)
    tables = transform_tables(seq_count, tok_rows)
    fixed = [pl.BlockSpec(t.shape, lambda i: (0, 0)) for t in tables]
    span = seq_count * tok_rows // LANES
    flops = chans * 2 * (2 * 2 * rows * span * LANES + 2 * rows * 4 * LANES * LANES)
    moved = 2 * (2 * values.size + 2 * chans * rows * LANES)
    return pl.pallas_call(
        conv_kernel,
        grid=(chans // block,),
        in_specs=[
            pl.BlockSpec((seq_count, block, tok_rows), lambda i: (0, i, 0)),
            pl.BlockSpec((2, block, rows, LANES), lambda i: (0, start // block + i, 0, 0)),
            *fixed,
        ],
        out_specs=pl.BlockSpec((seq_count, block, tok_rows), lambda i: (0, i, 0)),
        out_shape=jax.ShapeDtypeStruct((seq_count, chans, tok_rows), jnp.bfloat16),
        scratch_shapes=[
            pltpu.VMEM((block * span + span, LANES), jnp.float32),
            pltpu.VMEM((block * rows, 2 * LANES), jnp.bfloat16),
            pltpu.VMEM((block * rows, 2 * LANES), jnp.float32),
        ],
        compiler_params=pltpu.CompilerParams(vmem_limit_bytes=12 * MIB),
        cost_estimate=pl.CostEstimate(flops=flops, bytes_accessed=moved, transcendentals=0),
    )(values, response, *tables)


def gate_kernel(conv_ref, skip_ref, signal_ref, query_ref, out_ref):
    conv = conv_ref[...].astype(jnp.float32).T
    inner = conv + skip_ref[...] * signal_ref[...].astype(jnp.float32)
    out_ref[...] = (query_ref[...].astype(jnp.float32) * inner).astype(out_ref.dtype)


def gate(longconv, skip, lo, signal, query):
    chans, tok_rows = longconv.shape
    first = lo // LANES
    flat = pl.BlockSpec((tok_rows, LANES), lambda i: (0, i))
    return pl.pallas_call(
        gate_kernel,
        grid=(chans // LANES,),
        in_specs=[
            pl.BlockSpec((LANES, tok_rows), lambda i: (i, 0)),
            pl.BlockSpec((1, LANES), lambda i: (0, first + i)),
            flat,
            flat,
        ],
        out_specs=flat,
        out_shape=jax.ShapeDtypeStruct((tok_rows, chans), jnp.bfloat16),
        compiler_params=pltpu.CompilerParams(vmem_limit_bytes=8 * MIB),
        cost_estimate=pl.CostEstimate(flops=4 * chans * tok_rows, bytes_accessed=8 * chans * tok_rows, transcendentals=0),
    )(longconv, skip[None, :], signal, query)


def reorder_kernel(spec_ref, order_ref, out_ref):
    each = out_ref.shape[3]
    x = spec_ref[0].astype(jnp.bfloat16)
    y = jnp.dot(x, order_ref[...], preferred_element_type=jnp.float32).astype(jnp.bfloat16)
    for d in range(out_ref.shape[0]):
        out_ref[d, 0, 0] = y[d * each : (d + 1) * each]


def fold_kernel(got_ref, out_ref, came, held):
    seq_count, pairs, tok_rows = got_ref.shape[0], got_ref.shape[3], got_ref.shape[4]
    chans = pairs // 2
    runs = tok_rows // LANES
    rows = (seq_count + 1) * runs
    for part in range(2):
        sign = 1.0 if part == 0 else -1.0
        for s in range(seq_count):
            for r in range(runs):
                at = (s * runs + r) * pairs
                lanes = slice(r * LANES, (r + 1) * LANES)
                came[at : at + pairs, :] = got_ref[s, part, 0, :, lanes].astype(jnp.float32)
        for k1 in range(seq_count + 1):
            other = 2 * seq_count - k1
            for r in range(runs):
                value = came[pl.ds((k1 // 2 * runs + r) * pairs + k1 % 2, chans, stride=2), :]
                if k1 == seq_count:
                    value = sign * value
                elif k1 > 0:
                    value = value + sign * came[pl.ds((other // 2 * runs + r) * pairs + other % 2, chans, stride=2), :]
                held[pl.ds(k1 * runs + r, chans, stride=rows), :] = value
        out_ref[part] = held[: chans * rows, :].reshape(chans, rows, LANES).astype(out_ref.dtype)


def reordered_spectrum(spectrum, seq_count, chunks):
    parts, chans, own, tok_rows = spectrum.shape
    runs = tok_rows // LANES
    size = chans // chunks
    each = size // seq_count
    col = lax.broadcasted_iota(jnp.int32, (tok_rows, tok_rows), 1)
    row = lax.broadcasted_iota(jnp.int32, (tok_rows, tok_rows), 0)
    wanted = col // LANES + runs * (col % LANES)
    wanted = jnp.where(lax.axis_index("seq") >= seq_count // 2, tok_rows - 1 - wanted, wanted)
    order = (row == wanted).astype(jnp.bfloat16)
    shape = (seq_count, parts, chunks, own * each, tok_rows)
    return pl.pallas_call(
        reorder_kernel,
        grid=(parts, chunks),
        in_specs=[
            pl.BlockSpec((1, own * size, tok_rows), lambda p, j: (p, j, 0)),
            pl.BlockSpec((tok_rows, tok_rows), lambda p, j: (0, 0)),
        ],
        out_specs=pl.BlockSpec((seq_count, 1, 1, own * each, tok_rows), lambda p, j: (0, p, j, 0, 0)),
        out_shape=jax.ShapeDtypeStruct(shape, jnp.bfloat16),
        compiler_params=pltpu.CompilerParams(vmem_limit_bytes=48 * MIB),
        cost_estimate=pl.CostEstimate(
            flops=2 * spectrum.size * tok_rows, bytes_accessed=6 * spectrum.size, transcendentals=0
        ),
    )(spectrum.reshape(parts, chans * own, tok_rows), order)


def folded_response(sent, own):
    seq_count, parts, chunks, pairs, tok_rows = sent.shape
    runs = tok_rows // LANES
    each = pairs // own
    got = lax.all_to_all(sent, "seq", split_axis=0, concat_axis=0, tiled=True)
    block = min(CHAN_BLOCK, each)
    rows = (seq_count + 1) * runs
    return pl.pallas_call(
        fold_kernel,
        grid=(chunks, each // block),
        in_specs=[pl.BlockSpec((seq_count, parts, 1, own * block, tok_rows), lambda j, i: (0, 0, j, i, 0))],
        out_specs=pl.BlockSpec((parts, block, rows, LANES), lambda j, i: (0, j * (each // block) + i, 0, 0)),
        out_shape=jax.ShapeDtypeStruct((parts, chunks * each, rows, LANES), jnp.bfloat16),
        scratch_shapes=[
            pltpu.VMEM((seq_count * runs * own * block + 8, LANES), jnp.float32),
            pltpu.VMEM((block * rows + rows, LANES), jnp.float32),
        ],
        compiler_params=pltpu.CompilerParams(vmem_limit_bytes=12 * MIB),
        cost_estimate=pl.CostEstimate(flops=sent.size, bytes_accessed=3 * sent.size, transcendentals=0),
    )(got)


def feature_rows(out_weight, seq_count):
    each = out_weight.shape[0] // seq_count
    own = lax.dynamic_slice_in_dim(out_weight, lax.axis_index("seq") * each, each, axis=0)
    own = lax.all_to_all(own, "chan", split_axis=1, concat_axis=0, tiled=True)
    return own.reshape(lax.axis_size("chan"), each, own.shape[1])


def combine_kernel(gated_ref, w_ref, *refs):
    out_ref = refs[-1]
    gated = jnp.concatenate([gated_ref[z] for z in range(gated_ref.shape[0])], axis=1)
    total = jnp.dot(gated, w_ref[0], preferred_element_type=jnp.float32)
    if len(refs) == 2:
        total = total + refs[0][...].astype(jnp.float32)
    out_ref[...] = total.astype(out_ref.dtype)


def combine(gathered, weight, chunk, total):
    count, tok_rows, size = gathered.shape
    depth = count * size
    features = weight.shape[2]
    tile = min(8 * LANES, features)
    block = pl.BlockSpec((tok_rows, tile), lambda i: (0, i))
    given = [] if total is None else [total]
    return pl.pallas_call(
        combine_kernel,
        grid=(features // tile,),
        in_specs=[
            pl.BlockSpec((count, tok_rows, size), lambda i: (0, 0, 0)),
            pl.BlockSpec((1, depth, tile), lambda i: (chunk, 0, i)),
            *[block for _ in given],
        ],
        out_specs=block,
        out_shape=jax.ShapeDtypeStruct((tok_rows, features), jnp.bfloat16),
        compiler_params=pltpu.CompilerParams(vmem_limit_bytes=60 * MIB),
        cost_estimate=pl.CostEstimate(
            flops=2 * tok_rows * depth * features,
            bytes_accessed=2 * depth * (tok_rows + features) + 6 * tok_rows * features,
            transcendentals=0,
        ),
    )(gathered, weight, *given)


def shards(tokens, in_weight, conv_weight, spectrum, skip, out_weight):
    tok_rows, depth = tokens.shape
    seq_count = lax.axis_size("seq")
    chan_count = lax.axis_size("chan")
    chans = in_weight.shape[2]
    chunks = chunk_count(chans, seq_count)
    size = chans // chunks
    gathered = lax.all_gather(tokens, "chan")
    weight = feature_rows(out_weight, seq_count)
    last_rows = tokens[tok_rows - HALO :]
    weight, last_rows = lax.optimization_barrier((weight, last_rows))
    halo = gather_by_doubling(from_behind(last_rows, "seq", 1), "chan")
    sent = reordered_spectrum(spectrum, seq_count, chunks)
    halo, sent, weight = lax.optimization_barrier((halo, sent, weight))
    response = folded_response(sent, spectrum.shape[2])
    weight = gather_by_doubling(weight, "seq")
    weight = weight.reshape((chunks, seq_count // chunks) + weight.shape[1:]).transpose(0, 2, 1, 3, 4)
    weight = weight.reshape(chunks, chan_count * size, weight.shape[4])
    halo = jnp.einsum(
        "ztd,pzdc->ptc",
        halo,
        in_weight.reshape(3, chan_count, depth, chans),
        preferred_element_type=jnp.float32,
    ).astype(jnp.bfloat16)
    total = None
    for j, lo in enumerate(range(0, chans, size)):
        given = (gathered, in_weight, conv_weight, halo, lo, size, response, weight)
        query_t, signal, signal_t = project(*given)
        values = signal.reshape(seq_count, size // seq_count, tok_rows)
        values = lax.all_to_all(values, "seq", split_axis=0, concat_axis=0, tiled=True)
        longconv = lax.all_to_all(
            long_conv(values, response, lo // seq_count), "seq", split_axis=0, concat_axis=0, tiled=True
        ).reshape(size, tok_rows)
        gated = lax.all_gather(gate(longconv, skip, lo, signal_t, query_t), "chan")
        total = combine(gated, weight, j, total)
    return total


def solution(mesh):
    placed = (
        P("seq", "chan"),
        P(None, None, "chan"),
        P(None, None, "chan"),
        P(None, "chan", "seq", None),
        P("chan"),
        P("chan", None),
    )
    return jax.shard_map(
        shards, mesh=mesh, in_specs=placed, out_specs=P("seq", "chan"), check_vma=False
    )
```
